32 devices in a mesh: dp: 4 (over y, x), mp: 8 (over z, core).
Axes of the slice: x: 2, y: 2, z: 4, core: 2. Of those that a mesh axis runs over, the one named last changes fastest.
Arguments:
- features: bfloat16 [512, 16, 4096], P('mp', None, 'dp'), may hold values from -6 to 6
- styles: float32 [16, 512], P(None, 'mp'), may hold values from 0.3 to 8.5
- noise_field: bfloat16 [16, 4096], P(None, 'dp'), may hold values from -6 to 6
- noise_keep: int32 [16, 4096], P(None, 'dp'), may hold values 0 or 1
- path_noise: bfloat16 [3, 16, 4096], P(None, None, 'dp'), may hold values from -0.28125 to 0.28125
- length_mean: float32 [1], replicated, may hold values from 3 to 9
- conv_weight: float32 [512, 9, 512], P('mp'), may hold values from -4 to 4
- conv_moment: float32 [512, 9, 512], P('mp'), may hold values from -0.0007324219 to 0.0007324219
- conv_second: float32 [512, 9, 512], P('mp'), may hold values from 2.3841857e-09 to 9.536743e-09
- chan_params: float32 [2, 512], P(None, 'mp'), may hold values from -3 to 3
- chan_moment: float32 [2, 512], P(None, 'mp'), may hold values from -0.046875 to 0.046875
- chan_second: float32 [2, 512], P(None, 'mp'), may hold values from 8.583069e-06 to 3.4332275e-05
- rgb_weight: float32 [3, 512], P(None, 'mp'), may hold values from -18 to 18
- rgb_moment: float32 [3, 512], P(None, 'mp'), may hold values from -0.0234375 to 0.0234375
- rgb_second: float32 [3, 512], P(None, 'mp'), may hold values from 2.1457672e-06 to 8.583069e-06
Outputs:
- loss_sum: float32 [1], replicated
- clip_norm: float32 [1], replicated
- conv_moment_new: float32 [512, 9, 512], P('mp')
- conv_second_new: float32 [512, 9, 512], P('mp')
- conv_weight_new: float32 [512, 9, 512], P('mp')
- conv_weight_low: bfloat16 [512, 9, 512], P('mp')
- chan_moment_new: float32 [2, 512], P(None, 'mp')
- chan_second_new: float32 [2, 512], P(None, 'mp')
- chan_params_new: float32 [2, 512], P(None, 'mp')
- rgb_moment_new: float32 [3, 512], P(None, 'mp')
- rgb_second_new: float32 [3, 512], P(None, 'mp')
- rgb_weight_new: float32 [3, 512], P(None, 'mp')
- rgb_weight_low: bfloat16 [3, 512], P(None, 'mp')
The draws below stay inside these ranges and needn't reach their ends.
All inputs are finite; a program needn't handle non-finite values. No bound on the sum of `noise_keep` on one device may be relied on, other than what follows from the above.
Results may differ from the reference program's by a relative error of at most 0.012.
Values may be sent and summed in bfloat16 or wider, within the bound.
A program may use at most 320 MiB of HBM per device.

```python
import math
import jax
import jax.numpy as jnp
from jax import lax

C = 512
SIDE = 64
STEP = 5
IMAGES = 16
PIXELS = 4096


def draw_styles(key, part):
    key = jax.random.fold_in(key, 11)
    channel = jnp.arange(C, dtype=jnp.float32) / (C - 1)
    base = jax.random.uniform(key, (IMAGES, C), jnp.float32, 0.5, 1.5)
    rising = 1.0 + 2.0 * channel
    return base * rising[None, :]


def draw_path_noise(key, part):
    key = jax.random.fold_in(key, 23)
    row_index = (jnp.arange(SIDE * SIDE, dtype=jnp.int32) // SIDE).astype(jnp.float32) / (SIDE - 1)
    base = jnp.clip(jax.random.normal(key, (3, IMAGES, SIDE * SIDE), jnp.float32), -6.0, 6.0)
    rising = 1.0 + 2.0 * row_index
    return (base * rising[None, None, :] / SIDE).astype(jnp.bfloat16)


def draw_rgb_weight(key, part):
    key = jax.random.fold_in(key, 37)
    channel = jnp.arange(C, dtype=jnp.float32) / (C - 1)
    base = jnp.clip(jax.random.normal(key, (3, C), jnp.float32), -6.0, 6.0)
    rising = 1.0 + 2.0 * channel
    return base * rising[None, :]


def place_ends(result, key, low, high):
    shape = result.shape
    spot = [jax.random.randint(jax.random.fold_in(key, axis), (), 0, shape[axis]) for axis in range(len(shape))]
    result = result.at[tuple(spot)].set(low)
    longest = shape.index(max(shape))
    spot[longest] = (spot[longest] + 1) % shape[longest]
    return result.at[tuple(spot)].set(high)


def block_scale(key, dims, split, smallest, top_value):
    factor_of = 1.0
    for position, blocks in split:
        draws = jax.random.uniform(jax.random.fold_in(jax.random.fold_in(key, 6), position), (blocks,), jnp.float32, smallest / len(split), top_value / len(split))
        factor_of = factor_of * jnp.repeat(jnp.exp(draws), dims[position] // blocks).reshape((-1,) + (1,) * (len(dims) - 1 - position))
    return factor_of


def centred(key, dims, deviation, reach, cuts=(), kind=jnp.bfloat16):
    level = block_scale(key, dims, cuts, -0.22, 0.18) if cuts else 1.0
    array = jax.random.normal(key, dims, jnp.float32) * deviation * level
    return jnp.minimum(jnp.maximum(array, -reach), reach).astype(kind)


def setup_inputs(seed: int = 0) -> dict:
    keys = jax.random.split(jax.random.key(seed), 16)
    return {
        "features": centred(keys[0], (C, IMAGES, PIXELS), 1.0, 6.0, ((0, 8), (2, 4))),
        "styles": draw_styles(jax.random.fold_in(keys[15], 71), 0),
        "noise_field": centred(keys[2], (IMAGES, PIXELS), 1.0, 6.0, ((1, 4),)),
        "noise_keep": place_ends((jax.random.randint(keys[3], (IMAGES, PIXELS), 0, 4) < 3).astype(jnp.int32), jax.random.fold_in(keys[3], 1), 0, 1),
        "path_noise": draw_path_noise(jax.random.fold_in(keys[15], 71), 0),
        "length_mean": jnp.clip(jax.random.uniform(keys[5], (1,), jnp.float32, 3.0, 9.0), 3.0, 9.0),
        "conv_weight": centred(keys[6], (C, 9, C), 1.0, 4.0, ((0, 8),), jnp.float32),
        "conv_moment": centred(keys[7], (C, 9, C), (0.025 / C), 0.0007324219, ((0, 8),), jnp.float32),
        "conv_second": jnp.clip(jnp.exp(math.log(9.53674295089968e-09) - 1.3862944 * jax.random.uniform(keys[8], (C, 9, C), jnp.float32) ** block_scale(keys[8], (C, 9, C), ((0, 8),), -0.2, 0.2)), 2.38418573772492e-09, 9.53674295089968e-09),
        "chan_params": centred(keys[9], (2, C), 0.5, 3.0, ((1, 8),), jnp.float32),
        "chan_moment": centred(keys[10], (2, C), (1.5 / C), 0.046875, ((1, 8),), jnp.float32),
        "chan_second": jnp.clip(jnp.exp(math.log(3.4332275390625e-05) - 1.3862944 * jax.random.uniform(keys[11], (2, C), jnp.float32) ** block_scale(keys[11], (2, C), ((1, 8),), -0.2, 0.2)), 8.58306884765625e-06, 3.4332275390625e-05),
        "rgb_weight": draw_rgb_weight(jax.random.fold_in(keys[15], 71), 0),
        "rgb_moment": centred(keys[13], (3, C), (0.75 / C), 0.0234375, ((1, 8),), jnp.float32),
        "rgb_second": jnp.clip(jnp.exp(math.log(8.58306884765625e-06) - 1.3862944 * jax.random.uniform(keys[14], (3, C), jnp.float32) ** block_scale(keys[14], (3, C), ((1, 8),), -0.2, 0.2)), 2.1457672119140625e-06, 8.58306884765625e-06),
    }


@jax.custom_vjp
def low(v):
    return lax.optimization_barrier(v.astype(jnp.bfloat16)).astype(jnp.float32)

@jax.custom_vjp
def low_back(v):
    return v

def low_keep(v):
    return (low(v), None)

def low_pass(kept, grad):
    return (grad,)

def back_keep(v):
    return (v, None)

def back_low(kept, grad):
    return (low(grad),)
low.defvjp(low_keep, low_pass)
low_back.defvjp(back_keep, back_low)
CLIP_LIMIT = 0.1
LEARN_RATE = 0.3
DECAY_RATE = 0.01
BETA_FIRST = 0.5
BETA_SECOND = 0.5
ADAM_EPSILON = 1e-08
DEMOD_EPSILON = 1e-08
HIGHEST = lax.Precision.HIGHEST

def adam_update(weight, moment, second, gradient, factor):
    clipped = gradient * factor
    moment_new = BETA_FIRST * moment + (1.0 - BETA_FIRST) * clipped
    second_new = BETA_SECOND * second + (1.0 - BETA_SECOND) * clipped * clipped
    moment_hat = moment_new / (1.0 - BETA_FIRST ** STEP)
    second_hat = second_new / (1.0 - BETA_SECOND ** STEP)
    weight_new = weight - LEARN_RATE * (moment_hat / (jnp.sqrt(second_hat) + ADAM_EPSILON) + DECAY_RATE * weight)
    return (moment_new, second_new, weight_new)

@jax.checkpoint
def convolve(modulated, weight):
    image = modulated.reshape(C, IMAGES, SIDE, SIDE)
    padded = jnp.pad(image, ((0, 0), (0, 0), (1, 1), (1, 1)))
    running = jnp.zeros((C, IMAGES, SIDE * SIDE), jnp.float32)
    for vertical in range(3):
        for lateral in range(3):
            window = padded[:, :, vertical:vertical + SIDE, lateral:lateral + SIDE].reshape(C, IMAGES, SIDE * SIDE)
            running = running + jnp.einsum('io,inp->onp', weight[:, 3 * vertical + lateral, :], window, precision=HIGHEST)
    return running

def generate(conv_weight, chan_params, rgb_weight, features, styles, noise_field, noise_keep, path_noise, length_mean):
    conv_gain = 1.0 / math.sqrt(9 * C)
    rgb_gain = 1.0 / math.sqrt(C)
    weight = low(conv_weight)
    rgb_eff = low(rgb_weight) * rgb_gain
    modulated = low(features.astype(jnp.float32) * styles.T[:, :, None])
    scaled = low_back(convolve(modulated, weight)) * conv_gain
    demod_sq = jnp.dot(styles * styles, lax.optimization_barrier(jnp.sum(weight * weight, axis=1)), precision=HIGHEST)
    demod_scale = lax.rsqrt(conv_gain * conv_gain * demod_sq + DEMOD_EPSILON)
    noise_term = noise_field.astype(jnp.float32) * noise_keep.astype(jnp.float32)
    pre_act = scaled * demod_scale.T[:, :, None] + chan_params[1][:, None, None] * noise_term[None] + chan_params[0][:, None, None]
    activated = low(jax.nn.silu(pre_act))
    projected = jnp.einsum('onp,cnp->noc', activated, path_noise.astype(jnp.float32), precision=HIGHEST)
    path_slope = lax.optimization_barrier(jnp.sum(projected * rgb_eff.T[None], axis=2))
    length = jnp.sqrt(lax.optimization_barrier(jnp.sum(path_slope * path_slope, axis=1)) + 1e-08)
    excess = length - length_mean[0]
    return jnp.sum(excess * excess)

def reference(features, styles, noise_field, noise_keep, path_noise, length_mean, conv_weight, conv_moment, conv_second, chan_params, chan_moment, chan_second, rgb_weight, rgb_moment, rgb_second):

    def closed(conv_part, chan_part, rgb_part):
        return generate(conv_part, chan_part, rgb_part, features, styles, noise_field, noise_keep, path_noise, length_mean)
    loss_sum, pullback = jax.vjp(closed, conv_weight, chan_params, rgb_weight)
    conv_grad, chan_grad, rgb_grad = pullback(jnp.ones_like(loss_sum))
    squares = jnp.sum(conv_grad * conv_grad) + jnp.sum(chan_grad * chan_grad) + jnp.sum(rgb_grad * rgb_grad)
    grad_norm = jnp.sqrt(squares)
    factor = jnp.minimum(1.0, CLIP_LIMIT / (grad_norm + 1e-06))
    conv_m, conv_v, conv_new = adam_update(conv_weight, conv_moment, conv_second, conv_grad, factor)
    chan_m, chan_v, chan_new = adam_update(chan_params, chan_moment, chan_second, chan_grad, factor)
    rgb_m, rgb_v, rgb_new = adam_update(rgb_weight, rgb_moment, rgb_second, rgb_grad, factor)
    return (loss_sum.reshape(1), grad_norm.reshape(1), conv_m, conv_v, conv_new, conv_new.astype(jnp.bfloat16), chan_m, chan_v, chan_new, rgb_m, rgb_v, rgb_new, rgb_new.astype(jnp.bfloat16))
```

```python
import functools
import math

import jax
import jax.numpy as jnp
from jax import lax
from jax.experimental import pallas as pl
from jax.experimental.pallas import tpu as pltpu
from jax.sharding import PartitionSpec as P

SIDE = 64
STEP = 5
TAPS = 9
LANES = 128

CLIP_LIMIT = 0.1
LEARN_RATE = 0.3
DECAY_RATE = 0.01
BETA_FIRST = 0.5
BETA_SECOND = 0.5
ADAM_EPSILON = 1e-08
DEMOD_EPSILON = 1e-08
HIGHEST = lax.Precision.HIGHEST
MESH = pl.DeviceIdType.MESH
F32 = jnp.float32
BF16 = jnp.bfloat16
NT = (((1,), (1,)), ((), ()))


class Sizes:
    def __init__(self, mesh_shape, features, conv_weight):
        self.dp = mesh_shape["dp"]
        self.mp = mesh_shape["mp"]
        self.chips = self.mp // 2
        self.ch, self.images, self.px = features
        self.width = conv_weight[2]
        self.half = self.width // 2
        self.group = self.images // self.chips
        self.blocks = self.px // LANES
        self.ext = self.px + 2 * LANES
        self.split = (self.ch // self.dp) % 16 == 0
        self.shares = self.dp if self.split else 1
        self.rows = self.ch // self.shares
        self.taps_each = 3


def flip(value, bit):
    return value + bit - 2 * bit * lax.rem(lax.div(value, bit), 2)


def swap_halves(x):
    return pltpu.roll(x, SIDE, x.ndim - 1)


def kernel(
    s,
    feat_hbm,
    styles,
    weight_hbm,
    pack,
    aux_hbm,
    mean,
    grad_out,
    small_out,
    norm_out,
    feat,
    turned,
    outbox,
    grids,
    weight_own,
    weight_low,
    weights,
    weights_t,
    weight_sq,
    pack_all,
    columns,
    rgb_rows,
    demod_rows,
    demod_cols,
    chan_cols,
    aux,
    halo_out,
    halo_in,
    scaled,
    slope_of,
    proj_all,
    half_pick,
    stat_rows,
    rgb_acc,
    loss_acc,
    chan_acc,
    grad_conv,
    total,
    share_out,
    share_in,
    line_out,
    line_in,
    final,
    gathered,
    small_own,
    small_plane,
    small_mid,
    small_line,
    square_all,
    in_sem,
    w_send,
    w_recv,
    w_plane_send,
    w_plane_recv,
    p_send,
    p_recv,
    f_send,
    f_recv,
    f_local,
    f_swap,
    h_send,
    h_recv,
    j_send,
    j_recv,
    r_send,
    r_recv,
    l_send,
    l_recv,
    g_send,
    g_recv,
    sp_send,
    sp_recv,
    sl_send,
    sl_recv,
    n_send,
    n_recv,
):
    d = lax.axis_index("dp")
    m = lax.axis_index("mp")
    z = lax.div(m, 2)
    c = lax.rem(m, 2)
    other = 1 - c
    mate = 2 * z + other
    conv_gain = 1.0 / math.sqrt(TAPS * s.width)
    rgb_gain = 1.0 / math.sqrt(s.width)
    last = s.group - 1

    def copy_to(src, dst, send, recv, dd, mm):
        return pltpu.make_async_remote_copy(
            src_ref=src, dst_ref=dst, send_sem=send, recv_sem=recv, device_id=(dd, mm), device_id_type=MESH
        )

    def z_at(r):
        return lax.rem(z + r, s.chips)

    def d_at(r):
        return lax.rem(d + r, s.dp)

    line = [(d, lax.rem(m + r, s.mp)) for r in range(1, s.mp)]
    plane = [(d_at(r), mm) for r in range(1, s.dp) for mm in (m, mate)]
    near = plane + [(d, mate)]

    get_weight = pltpu.make_async_copy(weight_hbm, weight_own, in_sem.at[0])
    get_feat = pltpu.make_async_copy(feat_hbm, feat, in_sem.at[1])
    get_aux = pltpu.make_async_copy(aux_hbm.at[pl.ds(z * s.group, s.group)], aux, in_sem.at[2])
    get_weight.start()
    get_feat.start()
    get_aux.start()
    halo_in[...] = jnp.zeros_like(halo_in)
    barrier = pltpu.get_barrier_semaphore()
    for dd, mm in line + plane:
        pl.semaphore_signal(barrier, inc=1, device_id=(dd, mm), device_id_type=MESH)

    get_weight.wait()
    for k in range(TAPS):
        weight_low[k] = weight_own[k].astype(BF16)
    weights[:, pl.ds(pl.multiple_of(m * s.ch, 16), s.ch), :] = weight_low[
        :, :, pl.ds(pl.multiple_of(c * s.half, LANES), s.half)
    ]
    pl.semaphore_wait(barrier, len(line) + len(plane))

    share = d if s.split else 0
    piece_rows = s.rows

    def piece(m_of):
        return pl.ds(pl.multiple_of(m_of * s.ch + share * piece_rows, 16), piece_rows)

    def own_piece(half_of):
        return weight_low.at[
            :,
            pl.ds(pl.multiple_of(share * piece_rows, 16), piece_rows),
            pl.ds(pl.multiple_of(half_of * s.half, LANES), s.half),
        ]

    mate_rows = pl.ds(pl.multiple_of(m * s.ch, 16), s.ch)
    sends = []
    to_mate = copy_to(
        weight_low.at[:, :, pl.ds(pl.multiple_of(other * s.half, LANES), s.half)],
        weights.at[:, mate_rows, :],
        w_send.at[0],
        w_recv.at[m],
        d,
        mate,
    )
    to_mate.start()
    sends.append(to_mate)
    bits = []
    bit = s.chips // 2
    while bit >= 1:
        bits.append(bit)
        bit //= 2
    count = 1
    for bit in bits:
        for cc in range(2):
            cp = copy_to(
                own_piece(cc), weights.at[:, piece(m), :], w_send.at[count], w_recv.at[m], d, 2 * flip(z, bit) + cc
            )
            cp.start()
            sends.append(cp)
            count += 1
    for r, (dd, mm) in enumerate(line):
        cp = copy_to(pack.at[lax.div(mm, 2)], pack_all.at[m], p_send.at[r], p_recv.at[m], dd, mm)
        cp.start()
        sends.append(cp)
    pack_all[m] = pack[z]

    get_feat.wait()
    lane = lax.broadcasted_iota(jnp.int32, (1, 1, LANES), 2)
    low_lanes = lane < SIDE
    step = 8

    def modulate(index, carry):
        rows = pl.ds(pl.multiple_of(index * step, step), step)
        factor = styles[rows]
        for q in range(s.blocks // 2):
            first = feat[rows, :, q * LANES : (q + 1) * LANES].astype(F32) * factor
            q2 = q + s.blocks // 2
            second = feat[rows, :, q2 * LANES : (q2 + 1) * LANES].astype(F32) * factor
            even = jnp.where(low_lanes, first, swap_halves(second))
            odd = jnp.where(low_lanes, swap_halves(first), second)
            out_rows = pl.ds(pl.multiple_of(index * step * s.images, step * 8), step * s.images)
            turned[2 * q, out_rows, :] = even.reshape(step * s.images, LANES)
            turned[2 * q + 1, out_rows, :] = odd.reshape(step * s.images, LANES)
        return carry

    lax.fori_loop(0, s.ch // step, modulate, 0)

    def pick(n, carry):
        for j in range(s.blocks):
            part = turned[j, pl.ds(n, s.ch, stride=s.images), :]
            outbox[n, :, j * LANES : (j + 1) * LANES] = part.astype(BF16)
        return carry

    lax.fori_loop(0, s.images, pick, 0)

    middle = pl.ds(LANES, s.px)

    def grid_rows(m_of):
        return pl.ds(pl.multiple_of(m_of * s.ch, 16), s.ch)

    def feature_send(q, r):
        zz = z_at(r)
        return copy_to(
            outbox.at[zz * s.group + q],
            grids.at[q, 1, grid_rows(m), middle],
            f_send.at[q, r],
            f_recv.at[q, m],
            d,
            2 * zz + c,
        )

    def own_to_mate(q):
        return copy_to(
            outbox.at[z * s.group + q],
            grids.at[q, 1, grid_rows(m), middle],
            f_send.at[q, 0],
            f_recv.at[q, m],
            d,
            mate,
        )

    def own_local(q):
        return pltpu.make_async_copy(
            outbox.at[z * s.group + q], grids.at[q, 1, grid_rows(m), middle], f_local.at[q]
        )

    def swap_send(q, r):
        rows = grid_rows(2 * z_at(r) + c)
        return copy_to(
            grids.at[q, 1, rows, middle],
            grids.at[q, 1, rows, middle],
            f_swap.at[q, r],
            f_recv.at[q, 2 * z_at(r) + c],
            d,
            mate,
        )

    for q in range(s.group):
        own_local(q).start()
        own_to_mate(q).start()
    for q in range(2):
        for r in range(1, s.chips):
            feature_send(q, r).start()

    held = [z]
    for index, bit in enumerate(bits):
        peer = flip(z, bit)
        for h in held[1:]:
            for cc in range(2):
                cp = copy_to(
                    weights.at[:, piece(2 * h + cc), :],
                    weights.at[:, piece(2 * h + cc), :],
                    w_send.at[count],
                    w_recv.at[2 * h + cc],
                    d,
                    2 * peer + c,
                )
                cp.start()
                sends.append(cp)
                count += 1
        fresh = [flip(h, bit) for h in held]
        for h in fresh:
            for cc in range(2):
                mm = 2 * h + cc
                copy_to(
                    weights.at[:, piece(mm), :], weights.at[:, piece(mm), :], w_send.at[0], w_recv.at[mm], d, mate
                ).wait_recv()
                if s.split:
                    for r in range(1, s.dp):
                        cp = copy_to(
                            weights.at[:, piece(mm), :],
                            weights.at[:, piece(mm), :],
                            w_plane_send.at[r, mm],
                            w_plane_recv.at[r, mm],
                            d_at(r),
                            m,
                        )
                        cp.start()
                        sends.append(cp)
        held = held + fresh

    for dd, mm in line:
        copy_to(pack.at[0], pack_all.at[mm], p_send.at[0], p_recv.at[mm], d, mate).wait_recv()
    for mm in range(s.mp):
        columns[mm * s.ch : (mm + 1) * s.ch, :] = pack_all[mm].T[: s.ch, :]
    rows_all = columns[...].T
    for h in range(2):
        rgb_rows[h] = rows_all[8:16, h * s.half : (h + 1) * s.half]
    mine = columns[pl.ds(pl.multiple_of(c * s.half, 8), s.half), :]
    for k in range(2):
        chan_cols[k] = jnp.broadcast_to(mine[:, s.group + k : s.group + k + 1], (s.half, LANES))
    total[...] = jnp.zeros_like(total)
    stat_rows[...] = jnp.zeros_like(stat_rows)
    rgb_acc[...] = jnp.zeros_like(rgb_acc)
    loss_acc[...] = jnp.zeros_like(loss_acc)
    chan_acc[...] = jnp.zeros_like(chan_acc)

    copy_to(weights.at[:, mate_rows, :], weights.at[:, mate_rows, :], w_send.at[0], w_recv.at[mate], d, mate).wait_recv()
    if s.split:
        for h in held[1:]:
            for cc in range(2):
                mm = 2 * h + cc
                for r in range(1, s.dp):
                    copy_to(
                        weights.at[:, piece(mm), :],
                        weights.at[:, piece(mm), :],
                        w_plane_send.at[r, mm],
                        w_plane_recv.at[r, mm],
                        d,
                        mate,
                    ).wait_recv()
    square = jnp.zeros((s.width, s.half), F32)
    for k in range(TAPS):
        w = weights[k]
        weights_t[:, k * s.width : (k + 1) * s.width] = w.T
        wf = w.astype(F32)
        square = square + wf * wf
    weight_sq[...] = square
    demod_sq = jnp.dot(rows_all * rows_all, weight_sq[...], precision=HIGHEST, preferred_element_type=F32)
    demod = lax.rsqrt(conv_gain * conv_gain * demod_sq + DEMOD_EPSILON)
    demod_rows[...] = demod
    demod_t = demod.T
    for q in range(s.group):
        demod_cols[q] = jnp.broadcast_to(demod_t[:, q : q + 1], (s.half, LANES))
    get_aux.wait()

    lane2 = lax.broadcasted_iota(jnp.int32, (1, LANES), 1)
    low2 = lane2 < SIDE
    column = lax.rem(lane2, SIDE)
    not_first = column >= 1
    not_last = column <= SIDE - 2
    pair = s.width // 2
    up = lax.rem(d + s.dp - 1, s.dp)
    down = lax.rem(d + 1, s.dp)

    def halo_up(q):
        return copy_to(halo_out.at[q, 0], halo_in.at[q, 1], h_send.at[q, 0], h_recv.at[q, 1], up, m)

    def halo_down(q):
        return copy_to(halo_out.at[q, 1], halo_in.at[q, 0], h_send.at[q, 1], h_recv.at[q, 0], down, m)

    place = 2 * d + c

    def proj_send(q, index):
        dd, mm = near[index]
        return copy_to(
            proj_all.at[q, place],
            proj_all.at[q, place],
            j_send.at[q, index],
            j_recv.at[q, place],
            dd,
            mm,
        )

    def forward(q):
        for r in range(1, s.chips):
            mm = 2 * z_at(r) + c
            rows = grid_rows(mm)
            copy_to(
                grids.at[q, 1, rows, middle], grids.at[q, 1, rows, middle], f_swap.at[q, r], f_recv.at[q, mm], d, mate
            ).wait_recv()
            swap_send(q, r).start()

        @pl.when(q + 2 < s.group)
        def _():
            for r in range(1, s.chips):
                feature_send(q + 2, r).start()

        own_local(q).wait()
        for r in range(s.chips):
            mm = 2 * z_at(r) + other
            rows = grid_rows(mm)
            copy_to(
                grids.at[q, 1, rows, middle], grids.at[q, 1, rows, middle], f_swap.at[q, 0], f_recv.at[q, mm], d, mate
            ).wait_recv()
        top = grids[q, 1, :, LANES : 2 * LANES]
        end = grids[q, 1, :, s.px : s.px + LANES]
        halo_out[q, 0] = jnp.where(low2, top[:pair], swap_halves(top[pair:]))
        halo_out[q, 1] = jnp.where(low2, swap_halves(end[:pair]), end[pair:])

        @pl.when(d > 0)
        def _():
            halo_up(q).start()

        @pl.when(d < s.dp - 1)
        def _():
            halo_down(q).start()

        def lateral(j):
            x = grids[q, 1, :, j * LANES : (j + 1) * LANES]
            none = jnp.zeros_like(x)
            grids[q, 0, :, j * LANES : (j + 1) * LANES] = jnp.where(not_first, pltpu.roll(x, 1, 1), none)
            grids[q, 2, :, j * LANES : (j + 1) * LANES] = jnp.where(not_last, pltpu.roll(x, LANES - 1, 1), none)

        for j in range(1, s.blocks + 1):
            lateral(j)

        @pl.when(d > 0)
        def _():
            halo_down(q).wait_recv()

        @pl.when(d < s.dp - 1)
        def _():
            halo_up(q).wait_recv()

        above = halo_in[q, 0]
        below = halo_in[q, 1]
        swapped_end = swap_halves(end)
        swapped_top = swap_halves(top)
        grids[q, 1, :pair, :LANES] = jnp.where(low2, above, swapped_end[:pair])
        grids[q, 1, pair:, :LANES] = jnp.where(low2, swap_halves(above), swapped_end[pair:])
        tail = s.px + LANES
        grids[q, 1, :pair, tail : tail + LANES] = jnp.where(low2, swapped_top[:pair], swap_halves(below))
        grids[q, 1, pair:, tail : tail + LANES] = jnp.where(low2, swapped_top[pair:], below)
        lateral(0)
        lateral(s.blocks + 1)

        projected = jnp.zeros((16, s.half), F32)
        wide = 2 * LANES
        for p in range(0, s.px, wide):
            acc = jnp.zeros((s.half, wide), F32)
            for a in range(3):
                for b in range(3):
                    k = 3 * a + b
                    acc += jnp.dot(
                        weights_t[:, k * s.width : (k + 1) * s.width],
                        grids[q, b, :, a * LANES + p : a * LANES + p + wide],
                        preferred_element_type=F32,
                    )
            acts = []
            for t in range(2):
                cut = slice(p + t * LANES, p + (t + 1) * LANES)
                conv = acc[:, t * LANES : (t + 1) * LANES] * conv_gain
                noise = aux[q, :, cut].astype(F32)[3:4]
                pre = conv * demod_cols[q] + chan_cols[1] * noise + chan_cols[0]
                sig = jax.nn.sigmoid(pre)
                act = pre * sig
                scaled[q, :, cut] = conv
                slope_of[q, :, cut] = sig * (1.0 + pre * (1.0 - sig))
                acts.append(act.astype(BF16))
            act = jnp.concatenate(acts, axis=1)
            projected += lax.dot_general(aux[q, :, p : p + wide], act, NT, preferred_element_type=F32)
        proj_all[q, place] = projected[:8]
        for index in range(len(near)):
            proj_send(q, index).start()

    def signal_back(q):
        for r in range(1, 2 * s.dp):
            at = lax.rem(place + r, 2 * s.dp)
            copy_to(
                proj_all.at[q, at], proj_all.at[q, at], j_send.at[q, 0], j_recv.at[q, at], d, mate
            ).wait_recv()
        halves = []
        for h in range(2):
            acc = proj_all[q, h]
            for dd in range(1, s.dp):
                acc = acc + proj_all[q, 2 * dd + h]
            halves.append(acc)
        slopes = [jnp.sum(rgb_rows[h] * halves[h], axis=0, keepdims=True) for h in range(2)]
        row = lax.broadcasted_iota(jnp.int32, (8, s.half), 0)
        length_sq = jnp.sum(slopes[0] * slopes[0] + slopes[1] * slopes[1], axis=1, keepdims=True)
        length = jnp.sqrt(length_sq + 1e-08)
        excess = length - mean[0]
        loss_acc[...] += jnp.broadcast_to(excess * excess, (1, s.half))
        scale = 2.0 * excess / length
        for h in range(2):
            grad = scale * slopes[h]
            half_pick[h, 0] = grad * rgb_rows[h]
            half_pick[h, 1] = jnp.where(row < 3, grad * halves[h] * rgb_gain, 0.0)
        rgb_acc[...] += half_pick[c, 1]
        coef = half_pick[c, 0]
        high = coef.astype(BF16).astype(F32)
        coef_t = jnp.concatenate([high, coef - high], axis=0).T.astype(BF16)
        wide = 2 * LANES
        bias_part = chan_acc[0]
        strength_part = chan_acc[1]
        stat_part = jnp.zeros((s.half, LANES), F32)
        back = demod_cols[q] * conv_gain
        for p in range(0, s.px, wide):
            act_grad = jnp.dot(coef_t, aux[q, :, p : p + wide], preferred_element_type=F32)
            for t in range(2):
                cut = slice(p + t * LANES, p + (t + 1) * LANES)
                noise = aux[q, :, cut].astype(F32)[3:4]
                grad = act_grad[:, t * LANES : (t + 1) * LANES] * slope_of[q, :, cut]
                bias_part = bias_part + grad
                strength_part = strength_part + grad * noise
                stat_part = stat_part + grad * scaled[q, :, cut]
                grad_conv[:, cut] = (grad * back).astype(BF16)
        chan_acc[0] = bias_part
        chan_acc[1] = strength_part
        stat = jnp.sum(stat_part.T, axis=0, keepdims=True)
        dem = demod_rows[pl.ds(q, 1), :]
        stat_rows[pl.ds(q, 1), :] = stat * (dem * dem * dem) * (-0.5 * conv_gain * conv_gain)

    def tap_grad(q, k):
        a, b = k // 3, k % 3
        return lax.dot_general(
            grids[q, b, :, a * LANES : a * LANES + s.px], grad_conv[...], NT, preferred_element_type=F32
        )

    def stage(q, carry):
        forward(q)

        @pl.when(q > 0)
        def _():
            signal_back(q - 1)
            for k in range(TAPS):
                total[k] += tap_grad(q - 1, k)

        return carry

    lax.fori_loop(0, s.group, stage, 0)

    signal_back(last)
    small_own[0:1] = jnp.sum(chan_acc[0].T, axis=0, keepdims=True)
    small_own[1:2] = jnp.sum(chan_acc[1].T, axis=0, keepdims=True)
    small_own[2:3] = loss_acc[...]
    small_own[3:8] = jnp.zeros((5, s.half), F32)
    small_own[8:16] = rgb_acc[...]
    small_plane[place] = small_own[...]
    for index, (dd, mm) in enumerate(near):
        cp = copy_to(small_own, small_plane.at[place], sp_send.at[index], sp_recv.at[place], dd, mm)
        cp.start()
        sends.append(cp)
    cross = 2.0 * jnp.dot(
        columns[...] * columns[...], stat_rows[...], precision=HIGHEST, preferred_element_type=F32
    )
    weight_sq[...] = cross

    def share_part(k, share_of):
        return share_out.at[k, :, pl.ds(pl.multiple_of(share_of * s.rows, 16), s.rows), :]

    for k in range(TAPS):
        grad = total[k] + tap_grad(last, k) + weights[k].astype(F32) * weight_sq[...]
        share_out[k] = grad.astype(BF16).reshape(s.mp, s.ch, s.half)
        for r in range(1, s.dp):
            cp = copy_to(
                share_part(k, d_at(r) if s.split else 0),
                share_in.at[d, k],
                r_send.at[r, k],
                r_recv.at[d, k],
                d_at(r),
                m,
            )
            cp.start()
            sends.append(cp)

    for r in range(1, 2 * s.dp):
        at = lax.rem(place + r, 2 * s.dp)
        copy_to(small_own, small_plane.at[at], sp_send.at[0], sp_recv.at[at], d, mate).wait_recv()
    for h in range(2):
        acc = small_plane[h, 0:8]
        for dd in range(1, s.dp):
            acc = acc + small_plane[2 * dd + h, 0:8]
        row = lax.broadcasted_iota(jnp.int32, (8, s.half), 0)
        small_mid[h, 0:8] = jnp.where(row < 2, acc, small_plane[h, 0:8])
        small_mid[h, 8:16] = small_plane[h, 8:16]
    small_line[z] = small_mid[...]
    for r in range(1, s.chips):
        cp = copy_to(small_mid, small_line.at[z], sl_send.at[r], sl_recv.at[z], d, 2 * z_at(r) + c)
        cp.start()
        sends.append(cp)

    groups = TAPS // s.taps_each
    for g in range(groups):
        for k in range(g * s.taps_each, (g + 1) * s.taps_each):
            for r in range(1, s.dp):
                copy_to(
                    share_in.at[d_at(r), k], share_in.at[d_at(r), k], r_send.at[r, k], r_recv.at[d_at(r), k], d, mate
                ).wait_recv()
            own = share_out[k, :, pl.ds(pl.multiple_of(share * s.rows, 16), s.rows), :].astype(F32)
            acc = None
            for dd in range(s.dp):
                term = jnp.where(d == dd, own, share_in[dd, k].astype(F32))
                acc = term if acc is None else acc + term
            line_out[:, k] = acc.astype(BF16).reshape(s.chips, 2, s.rows, s.half)
        taps = pl.ds(g * s.taps_each, s.taps_each)
        for r in range(1, s.chips):
            cp = copy_to(
                line_out.at[z_at(r), taps], line_in.at[r, taps], l_send.at[r, g], l_recv.at[r, g], d, 2 * z_at(r) + c
            )
            cp.start()
            sends.append(cp)
    own_rows = pl.ds(pl.multiple_of(share * s.rows, 16), s.rows)
    own_cols = pl.ds(pl.multiple_of(c * s.half, LANES), s.half)
    targets = near if s.split else [(d, mate)]
    for g in range(groups):
        taps = pl.ds(g * s.taps_each, s.taps_each)
        for r in range(1, s.chips):
            copy_to(line_out.at[0, taps], line_in.at[r, taps], l_send.at[r, g], l_recv.at[r, g], d, mate).wait_recv()
        for k in range(g * s.taps_each, (g + 1) * s.taps_each):
            acc = line_out[z, k].astype(F32)
            for r in range(1, s.chips):
                acc = acc + line_in[r, k].astype(F32)
            final[:, k] = acc.astype(BF16)
            gathered[k, own_rows, own_cols] = final[c, k]
        for index, (dd, mm) in enumerate(targets):
            cp = copy_to(
                final.at[lax.rem(mm, 2), taps],
                gathered.at[taps, own_rows, own_cols],
                g_send.at[index, g],
                g_recv.at[place, g],
                dd,
                mm,
            )
            cp.start()
            sends.append(cp)
    for r in range(1, s.chips):
        copy_to(small_mid, small_line.at[z_at(r)], sl_send.at[r], sl_recv.at[z_at(r)], d, mate).wait_recv()
    sums = small_line[0]
    for zz in range(1, s.chips):
        sums = sums + small_line[zz]
    small_out[...] = sums
    chan_squares = jnp.sum(sums[:, 0:2] * sums[:, 0:2]) + jnp.sum(sums[:, 8:16] * sums[:, 8:16])

    for g in range(groups):
        taps = pl.ds(g * s.taps_each, s.taps_each)
        if s.split:
            for r in range(1, 2 * s.dp):
                at = lax.rem(place + r, 2 * s.dp)
                rows = pl.ds(pl.multiple_of(lax.div(at, 2) * s.rows, 16), s.rows)
                cols = pl.ds(pl.multiple_of(lax.rem(at, 2) * s.half, LANES), s.half)
                copy_to(
                    final.at[0, taps], gathered.at[taps, rows, cols], g_send.at[0, g], g_recv.at[at, g], d, mate
                ).wait_recv()
        else:
            cols = pl.ds(pl.multiple_of(other * s.half, LANES), s.half)
            copy_to(
                final.at[0, taps], gathered.at[taps, own_rows, cols], g_send.at[0, g], g_recv.at[2 * d + other, g], d, mate
            ).wait_recv()
    acc = jnp.zeros((s.ch, s.width), F32)
    for k in range(TAPS):
        grad = gathered[k].astype(F32)
        acc = acc + grad * grad
    square_all[m] = jnp.broadcast_to(jnp.sum(acc, keepdims=True), (8, LANES))
    for index, (dd, mm) in enumerate(line):
        cp = copy_to(square_all.at[m], square_all.at[m], n_send.at[index], n_recv.at[m], dd, mm)
        cp.start()
        sends.append(cp)
    grad_out[...] = gathered[...]
    for dd, mm in line:
        copy_to(square_all.at[mm], square_all.at[mm], n_send.at[0], n_recv.at[mm], d, mate).wait_recv()
    acc = square_all[0]
    for mm in range(1, s.mp):
        acc = acc + square_all[mm]
    norm_out[...] = jnp.sqrt(acc + chan_squares)

    for cp in sends:
        cp.wait_send()

    def settle(q, carry):
        for r in range(1, s.chips):
            feature_send(q, r).wait_send()
            swap_send(q, r).wait_send()
        own_to_mate(q).wait_send()
        for index in range(len(near)):
            proj_send(q, index).wait_send()

        @pl.when(d > 0)
        def _():
            halo_up(q).wait_send()

        @pl.when(d < s.dp - 1)
        def _():
            halo_down(q).wait_send()

        return carry

    lax.fori_loop(0, s.group, settle, 0)


def run_kernel(s, feat, styles, weight, pack, aux, mean):
    vm, dma = pltpu.VMEM, pltpu.SemaphoreType.DMA
    bits = int(math.log2(s.chips))
    near = 2 * s.dp - 1
    groups = TAPS // s.taps_each
    scratch = [
        vm((s.ch, s.images, s.px), BF16),
        vm((s.blocks, s.ch * s.images, LANES), F32),
        vm((s.images, s.ch, s.px), BF16),
        vm((s.group, 3, s.width, s.ext), BF16),
        vm((TAPS, s.ch, s.width), F32),
        vm((TAPS, s.ch, s.width), BF16),
        vm((TAPS, s.width, s.half), BF16),
        vm((s.half, TAPS * s.width), BF16),
        vm((s.width, s.half), F32),
        vm((s.mp, 16, LANES), F32),
        vm((s.width, 16), F32),
        vm((2, 8, s.half), F32),
        vm((16, s.half), F32),
        vm((s.group, s.half, LANES), F32),
        vm((2, s.half, LANES), F32),
        vm((s.group, 16, s.px), BF16),
        vm((s.group, 2, s.width // 2, LANES), BF16),
        vm((s.group, 2, s.width // 2, LANES), BF16),
        vm((s.group, s.half, s.px), F32),
        vm((s.group, s.half, s.px), F32),
        vm((s.group, 2 * s.dp, 8, s.half), F32),
        vm((2, 2, 8, s.half), F32),
        vm((16, s.half), F32),
        vm((8, s.half), F32),
        vm((1, s.half), F32),
        vm((2, s.half, LANES), F32),
        vm((s.half, s.px), BF16),
        vm((TAPS, s.width, s.half), F32),
        vm((TAPS, s.mp, s.ch, s.half), BF16),
        vm((s.dp, TAPS, s.mp, s.rows, s.half), BF16),
        vm((s.chips, TAPS, 2, s.rows, s.half), BF16),
        vm((s.chips, TAPS, 2, s.rows, s.half), BF16),
        vm((2, TAPS, s.rows, s.half), BF16),
        vm((TAPS, s.ch, s.width), BF16),
        vm((16, s.half), F32),
        vm((2 * s.dp, 16, s.half), F32),
        vm((2, 16, s.half), F32),
        vm((s.chips, 2, 16, s.half), F32),
        vm((s.mp, 8, LANES), F32),
        dma((3,)),
        dma((1 + 2 * bits + 2 * s.chips,)),
        dma((s.mp,)),
        dma((s.dp, s.mp)),
        dma((s.dp, s.mp)),
        dma((s.mp,)),
        dma((s.mp,)),
        dma((s.group, s.chips)),
        dma((s.group, s.mp)),
        dma((s.group,)),
        dma((s.group, s.chips)),
        dma((s.group, 2)),
        dma((s.group, 2)),
        dma((s.group, near)),
        dma((s.group, 2 * s.dp)),
        dma((s.dp, TAPS)),
        dma((s.dp, TAPS)),
        dma((s.chips, groups)),
        dma((s.chips, groups)),
        dma((near, groups)),
        dma((2 * s.dp, groups)),
        dma((near,)),
        dma((2 * s.dp,)),
        dma((s.chips,)),
        dma((s.chips,)),
        dma((s.mp,)),
        dma((s.mp,)),
    ]
    flops = 2 * 2 * s.group * s.px * s.half * s.width * TAPS
    return pl.pallas_call(
        functools.partial(kernel, s),
        out_shape=(
            jax.ShapeDtypeStruct((TAPS, s.ch, s.width), BF16),
            jax.ShapeDtypeStruct((2, 16, s.half), F32),
            jax.ShapeDtypeStruct((8, LANES), F32),
        ),
        in_specs=[
            pl.BlockSpec(memory_space=pl.ANY),
            pl.BlockSpec(memory_space=pltpu.VMEM),
            pl.BlockSpec(memory_space=pl.ANY),
            pl.BlockSpec(memory_space=pltpu.VMEM),
            pl.BlockSpec(memory_space=pl.ANY),
            pl.BlockSpec(memory_space=pltpu.SMEM),
        ],
        out_specs=[pl.BlockSpec(memory_space=pltpu.VMEM)] * 3,
        scratch_shapes=scratch,
        compiler_params=pltpu.CompilerParams(
            collective_id=0, has_side_effects=True, vmem_limit_bytes=62 * 2**20
        ),
        cost_estimate=pl.CostEstimate(flops=flops, bytes_accessed=2**23, transcendentals=2**20),
        name="synthesis_step",
    )(feat, styles, weight, pack, aux, mean)


def adam_update(weight, moment, second, gradient, factor):
    clipped = gradient * factor
    moment_new = BETA_FIRST * moment + (1.0 - BETA_FIRST) * clipped
    second_new = BETA_SECOND * second + (1.0 - BETA_SECOND) * clipped * clipped
    moment_hat = moment_new / (1.0 - BETA_FIRST**STEP)
    second_hat = second_new / (1.0 - BETA_SECOND**STEP)
    weight_new = weight - LEARN_RATE * (
        moment_hat / (jnp.sqrt(second_hat) + ADAM_EPSILON) + DECAY_RATE * weight
    )
    return (moment_new, second_new, weight_new)


def block_order(x, s):
    lead = x.shape[:-1]
    x = x.reshape(lead + (2, s.px // (2 * SIDE), SIDE))
    return jnp.swapaxes(x, -3, -2).reshape(lead + (s.px,))


def local(
    mesh_shape,
    features,
    styles,
    noise_field,
    noise_keep,
    path_noise,
    length_mean,
    conv_weight,
    conv_moment,
    conv_second,
    chan_params,
    chan_moment,
    chan_second,
    rgb_weight,
    rgb_moment,
    rgb_second,
):
    s = Sizes(mesh_shape, features.shape, conv_weight.shape)
    m = lax.axis_index("mp")
    rgb_eff = rgb_weight.astype(BF16).astype(F32) * (1.0 / math.sqrt(s.width))
    noise = (noise_field.astype(F32) * noise_keep.astype(F32)).astype(BF16)
    aux = jnp.zeros((s.images, 16, s.px), BF16)
    path = block_order(jnp.swapaxes(path_noise, 0, 1), s)
    blank = functools.partial(jnp.zeros, dtype=BF16)
    aux = jnp.concatenate(
        [
            path,
            block_order(noise, s)[:, None],
            blank((s.images, 4, s.px)),
            path,
            blank((s.images, 5, s.px)),
        ],
        axis=1,
    )
    pack = jnp.concatenate(
        [
            styles.reshape(s.chips, s.group, s.ch),
            jnp.broadcast_to(chan_params[None], (s.chips, 2, s.ch)),
            jnp.zeros((s.chips, 8 - s.group - 2, s.ch), F32),
            jnp.broadcast_to(rgb_eff[None], (s.chips, 3, s.ch)),
            jnp.zeros((s.chips, 5, s.ch), F32),
        ],
        axis=1,
    )
    pack = jnp.pad(pack, ((0, 0), (0, 0), (0, LANES - s.ch)))
    wide_styles = jnp.broadcast_to(styles.T[:, :, None], (s.ch, s.images, LANES))
    taps_first = functools.partial(jnp.transpose, axes=(1, 0, 2))
    grad, sums, norm = run_kernel(
        s, features, wide_styles, taps_first(conv_weight), pack, aux, length_mean
    )
    grad_norm = norm[0, 0]
    factor = jnp.minimum(1.0, CLIP_LIMIT / (grad_norm + 1e-06))
    sums = jnp.swapaxes(sums, 0, 1).reshape(16, s.width)
    own = lax.dynamic_slice_in_dim(sums, m * s.ch, s.ch, 1)
    conv_m, conv_v, conv_new = adam_update(
        taps_first(conv_weight), taps_first(conv_moment), taps_first(conv_second), grad.astype(F32), factor
    )
    chan_m, chan_v, chan_new = adam_update(chan_params, chan_moment, chan_second, own[0:2], factor)
    rgb_m, rgb_v, rgb_new = adam_update(rgb_weight, rgb_moment, rgb_second, own[8:11], factor)
    return (
        sums[2, 0].reshape(1),
        grad_norm.reshape(1),
        taps_first(conv_m),
        taps_first(conv_v),
        taps_first(conv_new),
        taps_first(conv_new.astype(BF16)),
        chan_m,
        chan_v,
        chan_new,
        rgb_m,
        rgb_v,
        rgb_new,
        rgb_new.astype(BF16),
    )


def solution(mesh):
    whole, line = P(), P("mp", None, None)
    row, pixels = P(None, "mp"), P(None, "dp")
    in_specs = (
        P("mp", None, "dp"),
        row,
        pixels,
        pixels,
        P(None, None, "dp"),
        whole,
        line,
        line,
        line,
    ) + (row,) * 6
    out_specs = (whole, whole) + (line,) * 4 + (row,) * 7
    return jax.shard_map(
        functools.partial(local, dict(mesh.shape)),
        mesh=mesh,
        in_specs=in_specs,
        out_specs=out_specs,
        check_vma=False,
    )
```

```python
import functools
import math

import jax
import jax.numpy as jnp
from jax import lax
from jax.experimental import pallas as pl
from jax.experimental.pallas import tpu as pltpu
from jax.sharding import PartitionSpec as P

SIDE = 64
STEP = 5
TAPS = 9
LANES = 128

CLIP_LIMIT = 0.1
LEARN_RATE = 0.3
DECAY_RATE = 0.01
BETA_FIRST = 0.5
BETA_SECOND = 0.5
ADAM_EPSILON = 1e-08
DEMOD_EPSILON = 1e-08
HIGHEST = lax.Precision.HIGHEST
MESH = pl.DeviceIdType.MESH
F32 = jnp.float32
BF16 = jnp.bfloat16
NT = (((1,), (1,)), ((), ()))


class Sizes:
    def __init__(self, mesh_shape, features, conv_weight):
        self.dp = mesh_shape["dp"]
        self.mp = mesh_shape["mp"]
        self.chips = self.mp // 2
        self.ch, self.images, self.px = features
        self.width = conv_weight[2]
        self.half = self.width // 2
        self.group = self.images // self.chips
        self.blocks = self.px // LANES
        self.ext = self.px + 2 * LANES
        self.split = (self.ch // self.dp) % 16 == 0
        self.shares = self.dp if self.split else 1
        self.rows = self.ch // self.shares
        self.taps_each = 3
        self.first = 6
        self.bits = []
        bit = self.chips // 2
        while bit >= 1:
            self.bits.append(bit)
            bit //= 2


def flip(value, bit):
    return value + bit - 2 * bit * lax.rem(lax.div(value, bit), 2)


def swap_halves(x):
    return pltpu.roll(x, SIDE, x.ndim - 1)


def kernel(
    s,
    feat_hbm,
    styles,
    weight_hbm,
    chan,
    rgb,
    path_hbm,
    field_hbm,
    keep_hbm,
    mean,
    grad_out,
    small_out,
    norm_out,
    feat,
    style_cols,
    turned,
    outbox,
    grids,
    weight_own,
    weight_low,
    weights,
    weights_t,
    weight_sq,
    pack,
    pack_all,
    columns,
    rgb_low,
    rgb_rows,
    demod_rows,
    demod_cols,
    chan_cols,
    path,
    field,
    keep,
    pixel_rows,
    aux_rows,
    aux,
    halo_out,
    halo_in,
    scaled,
    slope_of,
    proj_all,
    half_pick,
    stat_rows,
    rgb_acc,
    loss_acc,
    chan_acc,
    grad_conv,
    total,
    share_out,
    share_in,
    line_out,
    line_in,
    wide_out,
    wide_in,
    wide_sum,
    narrow_in,
    final,
    gathered,
    small_own,
    small_plane,
    small_mid,
    small_line,
    small_sum,
    square_all,
    in_sem,
    w_send,
    w_recv,
    p_sem,
    f_send,
    f_recv,
    f_local,
    h_send,
    h_recv,
    j_send,
    j_recv,
    r_send,
    r_recv,
    l_send,
    l_recv,
    b_recv,
    n_recv,
    g_sem,
    sp_sem,
    sl_sem,
    n_sem,
):
    d = lax.axis_index("dp")
    m = lax.axis_index("mp")
    z = lax.div(m, 2)
    c = lax.rem(m, 2)
    other = 1 - c
    mate = 2 * z + other
    conv_gain = 1.0 / math.sqrt(TAPS * s.width)
    rgb_gain = 1.0 / math.sqrt(s.width)
    last = s.group - 1

    def copy_to(src, dst, send, recv, dd, mm):
        return pltpu.make_async_remote_copy(
            src_ref=src, dst_ref=dst, send_sem=send, recv_sem=recv, device_id=(dd, mm), device_id_type=MESH
        )

    def taken(ref, sem):
        copy_to(ref, ref, sem, sem, d, mate).wait_recv()

    def gone(ref, sem):
        copy_to(ref, ref, sem, sem, d, mate).wait_send()

    def z_at(r):
        return lax.rem(z + r, s.chips)

    def d_at(r):
        return lax.rem(d + r, s.dp)

    line = [(d, lax.rem(m + r, s.mp)) for r in range(1, s.mp)]
    plane = [(d_at(r), mm) for r in range(1, s.dp) for mm in (m, mate)]
    near = plane + [(d, mate)]
    place = 2 * d + c

    get_weight = pltpu.make_async_copy(weight_hbm, weight_own, in_sem.at[0])
    get_feat = pltpu.make_async_copy(feat_hbm, feat, in_sem.at[1])
    get_path = pltpu.make_async_copy(path_hbm, path, in_sem.at[2])
    get_field = pltpu.make_async_copy(field_hbm, field, in_sem.at[3])
    get_keep = pltpu.make_async_copy(keep_hbm, keep, in_sem.at[4])
    get_weight.start()
    get_feat.start()
    get_path.start()
    get_field.start()
    get_keep.start()
    halo_in[...] = jnp.zeros_like(halo_in)
    barrier = pltpu.get_barrier_semaphore()
    for dd, mm in line + plane:
        pl.semaphore_signal(barrier, inc=1, device_id=(dd, mm), device_id_type=MESH)
    pack[...] = jnp.zeros_like(pack)
    rgb_low[...] = rgb[...].astype(BF16)
    rgb_eff = rgb_low[...].astype(F32) * rgb_gain
    for zz in range(s.chips):
        pack[zz, : s.group, : s.ch] = styles[zz * s.group : (zz + 1) * s.group, :]
        pack[zz, s.group : s.group + 2, : s.ch] = chan[...]
        pack[zz, 8:11, : s.ch] = rgb_eff
    pack_all[m] = pack[z]
    for i in range(s.ch):
        style_cols[i] = jnp.broadcast_to(styles[:, i : i + 1], (s.images, LANES))

    get_weight.wait()
    for k in range(TAPS):
        weight_low[k] = weight_own[k].astype(BF16)
    pl.semaphore_wait(barrier, len(line) + len(plane))

    share = d if s.split else 0

    def piece(m_of):
        return weights.at[:, pl.ds(pl.multiple_of(m_of * s.ch + share * s.rows, 16), s.rows), :]

    def own_piece(half_of):
        return weight_low.at[
            :,
            pl.ds(pl.multiple_of(share * s.rows, 16), s.rows),
            pl.ds(pl.multiple_of(half_of * s.half, LANES), s.half),
        ]

    sent_rows = 0
    for index, bit in enumerate(s.bits):
        for cc in range(2):
            copy_to(
                own_piece(cc), piece(m), w_send.at[0], w_recv.at[index], d, 2 * flip(z, bit) + cc
            ).start()
            sent_rows += s.rows
    copy_to(
        weight_low.at[:, :, pl.ds(pl.multiple_of(other * s.half, LANES), s.half)],
        weights.at[:, pl.ds(pl.multiple_of(m * s.ch, 16), s.ch), :],
        w_send.at[0],
        w_recv.at[len(s.bits)],
        d,
        mate,
    ).start()
    sent_rows += s.ch
    for dd, mm in line:
        copy_to(pack.at[lax.div(mm, 2)], pack_all.at[m], p_sem.at[0], p_sem.at[1], dd, mm).start()

    get_feat.wait()
    lane = lax.broadcasted_iota(jnp.int32, (1, 1, LANES), 2)
    low_lanes = lane < SIDE
    step = 8

    def modulate(index, carry):
        rows = pl.ds(pl.multiple_of(index * step, step), step)
        factor = style_cols[rows]
        for q in range(s.blocks // 2):
            first = feat[rows, :, q * LANES : (q + 1) * LANES].astype(F32) * factor
            q2 = q + s.blocks // 2
            second = feat[rows, :, q2 * LANES : (q2 + 1) * LANES].astype(F32) * factor
            even = jnp.where(low_lanes, first, swap_halves(second))
            odd = jnp.where(low_lanes, swap_halves(first), second)
            out_rows = pl.ds(pl.multiple_of(index * step * s.images, step * 8), step * s.images)
            turned[2 * q, out_rows, :] = even.reshape(step * s.images, LANES)
            turned[2 * q + 1, out_rows, :] = odd.reshape(step * s.images, LANES)
        return carry

    lax.fori_loop(0, s.ch // step, modulate, 0)

    def pick(n, carry):
        for j in range(s.blocks):
            part = turned[j, pl.ds(n, s.ch, stride=s.images), :]
            outbox[n, :, j * LANES : (j + 1) * LANES] = part.astype(BF16)
        return carry

    lax.fori_loop(0, s.images, pick, 0)

    middle = pl.ds(LANES, s.px)

    def grid_rows(m_of):
        return pl.ds(pl.multiple_of(m_of * s.ch, 16), s.ch)

    def feature_send(q, r):
        zz = z_at(r)
        return copy_to(
            outbox.at[zz * s.group + q],
            grids.at[q, 1, grid_rows(m), middle],
            f_send.at[q],
            f_recv.at[q, 0],
            d,
            2 * zz + c,
        )

    def start_features():
        for q in range(s.group):
            own = outbox.at[z * s.group + q]
            there = grids.at[q, 1, grid_rows(m), middle]
            pltpu.make_async_copy(own, there, f_local.at[0]).start()
            copy_to(own, there, f_send.at[q], f_recv.at[q, 1], d, mate).start()
            if q < 2:
                for r in range(1, s.chips):
                    feature_send(q, r).start()

    held = [z]
    plane_rows = 0
    for index, bit in enumerate(s.bits):
        peer = flip(z, bit)
        for h in held[1:]:
            for cc in range(2):
                at = piece(2 * h + cc)
                copy_to(at, at, w_send.at[0], w_recv.at[index], d, 2 * peer + c).start()
                sent_rows += s.rows
        if index == len(s.bits) - 1:
            start_features()
        fresh = [flip(h, bit) for h in held]
        taken(weights.at[:, pl.ds(0, 2 * len(fresh) * s.rows), :], w_recv.at[index])
        if s.split:
            for h in fresh:
                for cc in range(2):
                    at = piece(2 * h + cc)
                    for r in range(1, s.dp):
                        copy_to(at, at, w_send.at[1], w_recv.at[len(s.bits) + 1], d_at(r), m).start()
                        plane_rows += s.rows
        held = held + fresh

    weights[:, grid_rows(m), :] = weight_low[:, :, pl.ds(pl.multiple_of(c * s.half, LANES), s.half)]
    get_path.wait()
    get_field.wait()
    get_keep.wait()
    lane2 = lax.broadcasted_iota(jnp.int32, (1, LANES), 1)
    low2 = lane2 < SIDE
    for k in range(4):
        for q in range(s.blocks // 2):
            q2 = q + s.blocks // 2
            cuts = [slice(q * LANES, (q + 1) * LANES), slice(q2 * LANES, (q2 + 1) * LANES)]
            if k < 3:
                first, second = [path[k, :, cut].astype(F32) for cut in cuts]
            else:
                first, second = [field[:, cut].astype(F32) * keep[:, cut].astype(F32) for cut in cuts]
            pixel_rows[k, :, 2 * q * LANES : (2 * q + 1) * LANES] = jnp.where(low2, first, swap_halves(second))
            pixel_rows[k, :, (2 * q + 1) * LANES : (2 * q + 2) * LANES] = jnp.where(low2, swap_halves(first), second)
    aux_rows[...] = jnp.zeros_like(aux_rows)
    for q in range(s.group):
        for k in range(4):
            row = pixel_rows[k, pl.ds(z * s.group + q, 1), :]
            aux_rows[q, k : k + 1, :] = row
            if k < 3:
                aux_rows[q, 8 + k : 9 + k, :] = row
        aux[q] = aux_rows[q].astype(BF16)

    taken(pack_all.at[pl.ds(0, s.mp - 1)], p_sem.at[1])
    for mm in range(s.mp):
        columns[mm * s.ch : (mm + 1) * s.ch, :] = pack_all[mm].T[: s.ch, :]
    rows_all = columns[...].T
    for h in range(2):
        rgb_rows[h] = rows_all[8:16, h * s.half : (h + 1) * s.half]
    mine = columns[pl.ds(pl.multiple_of(c * s.half, 8), s.half), :]
    for k in range(2):
        chan_cols[k] = jnp.broadcast_to(mine[:, s.group + k : s.group + k + 1], (s.half, LANES))
    total[...] = jnp.zeros_like(total)
    stat_rows[...] = jnp.zeros_like(stat_rows)
    rgb_acc[...] = jnp.zeros_like(rgb_acc)
    loss_acc[...] = jnp.zeros_like(loss_acc)
    chan_acc[...] = jnp.zeros_like(chan_acc)

    column = lax.rem(lane2, SIDE)
    not_first = column >= 1
    not_last = column <= SIDE - 2
    pair = s.width // 2
    up = lax.rem(d + s.dp - 1, s.dp)
    down = lax.rem(d + 1, s.dp)

    def halo_up(q):
        return copy_to(halo_out.at[q, 0], halo_in.at[q, 1], h_send.at[q, 0], h_recv.at[q, 1], up, m)

    def halo_down(q):
        return copy_to(halo_out.at[q, 1], halo_in.at[q, 0], h_send.at[q, 1], h_recv.at[q, 0], down, m)

    def ends(q):
        return grids[q, 1, :, LANES : 2 * LANES], grids[q, 1, :, s.px : s.px + LANES]

    def take_line(q):
        taken(grids.at[q, 1, pl.ds(0, (s.chips - 1) * s.ch), middle], f_recv.at[q, 0])
        for r in range(1, s.chips):
            at = grids.at[q, 1, grid_rows(2 * z_at(r) + c), middle]
            copy_to(at, at, f_send.at[q], f_recv.at[q, 1], d, mate).start()

        @pl.when(q + 2 < s.group)
        def _():
            for r in range(1, s.chips):
                feature_send(q + 2, r).start()

    def take_mate(q):
        taken(grids.at[q, 1, pl.ds(0, s.chips * s.ch), middle], f_recv.at[q, 1])
        top, end = ends(q)
        halo_out[q, 0] = jnp.where(low2, top[:pair], swap_halves(top[pair:]))
        halo_out[q, 1] = jnp.where(low2, swap_halves(end[:pair]), end[pair:])

        @pl.when(d > 0)
        def _():
            halo_up(q).start()

        @pl.when(d < s.dp - 1)
        def _():
            halo_down(q).start()

    def lateral(q, j):
        x = grids[q, 1, :, j * LANES : (j + 1) * LANES]
        none = jnp.zeros_like(x)
        grids[q, 0, :, j * LANES : (j + 1) * LANES] = jnp.where(not_first, pltpu.roll(x, 1, 1), none)
        grids[q, 2, :, j * LANES : (j + 1) * LANES] = jnp.where(not_last, pltpu.roll(x, LANES - 1, 1), none)

    def inner(q):
        for j in range(1, s.blocks + 1):
            lateral(q, j)

    def border(q):
        @pl.when(d > 0)
        def _():
            halo_down(q).wait_recv()

        @pl.when(d < s.dp - 1)
        def _():
            halo_up(q).wait_recv()

        top, end = ends(q)
        above = halo_in[q, 0]
        below = halo_in[q, 1]
        swapped_end = swap_halves(end)
        swapped_top = swap_halves(top)
        grids[q, 1, :pair, :LANES] = jnp.where(low2, above, swapped_end[:pair])
        grids[q, 1, pair:, :LANES] = jnp.where(low2, swap_halves(above), swapped_end[pair:])
        tail = s.px + LANES
        grids[q, 1, :pair, tail : tail + LANES] = jnp.where(low2, swapped_top[:pair], swap_halves(below))
        grids[q, 1, pair:, tail : tail + LANES] = jnp.where(low2, swapped_top[pair:], below)
        lateral(q, 0)
        lateral(q, s.blocks + 1)

    def convolve_math(q):
        projected = jnp.zeros((16, s.half), F32)
        wide = 2 * LANES
        for p in range(0, s.px, wide):
            acc = jnp.zeros((s.half, wide), F32)
            for a in range(3):
                for b in range(3):
                    k = 3 * a + b
                    acc += jnp.dot(
                        weights_t[:, k * s.width : (k + 1) * s.width],
                        grids[q, b, :, a * LANES + p : a * LANES + p + wide],
                        preferred_element_type=F32,
                    )
            acts = []
            for t in range(2):
                cut = slice(p + t * LANES, p + (t + 1) * LANES)
                conv = acc[:, t * LANES : (t + 1) * LANES] * conv_gain
                noise = aux[q, :, cut].astype(F32)[3:4]
                pre = conv * demod_cols[q] + chan_cols[1] * noise + chan_cols[0]
                sig = jax.nn.sigmoid(pre)
                act = pre * sig
                scaled[q, :, cut] = conv
                slope_of[q, :, cut] = sig * (1.0 + pre * (1.0 - sig))
                acts.append(act.astype(BF16))
            act = jnp.concatenate(acts, axis=1)
            projected += lax.dot_general(aux[q, :, p : p + wide], act, NT, preferred_element_type=F32)
        proj_all[q, place] = projected[:8]

    def convolve(q):
        convolve_math(q)
        for dd, mm in near:
            at = proj_all.at[q, place]
            copy_to(at, at, j_send.at[q], j_recv.at[q], dd, mm).start()

    def signal_back(q):
        taken(proj_all.at[q, pl.ds(0, 2 * s.dp - 1)], j_recv.at[q])
        signal_math(q)

    def signal_math(q):
        halves = []
        for h in range(2):
            acc = proj_all[q, h]
            for dd in range(1, s.dp):
                acc = acc + proj_all[q, 2 * dd + h]
            halves.append(acc)
        slopes = [jnp.sum(rgb_rows[h] * halves[h], axis=0, keepdims=True) for h in range(2)]
        row = lax.broadcasted_iota(jnp.int32, (8, s.half), 0)
        length_sq = jnp.sum(slopes[0] * slopes[0] + slopes[1] * slopes[1], axis=1, keepdims=True)
        length = jnp.sqrt(length_sq + 1e-08)
        excess = length - mean[0]
        loss_acc[...] += jnp.broadcast_to(excess * excess, (1, s.half))
        scale = 2.0 * excess / length
        for h in range(2):
            grad = scale * slopes[h]
            half_pick[h, 0] = grad * rgb_rows[h]
            half_pick[h, 1] = jnp.where(row < 3, grad * halves[h] * rgb_gain, 0.0)
        rgb_acc[...] += half_pick[c, 1]
        coef = half_pick[c, 0]
        high = coef.astype(BF16).astype(F32)
        coef_t = jnp.concatenate([high, coef - high], axis=0).T.astype(BF16)
        wide = 2 * LANES
        bias_part = chan_acc[0]
        strength_part = chan_acc[1]
        stat_part = jnp.zeros((s.half, LANES), F32)
        back = demod_cols[q] * conv_gain
        for p in range(0, s.px, wide):
            act_grad = jnp.dot(coef_t, aux[q, :, p : p + wide], preferred_element_type=F32)
            for t in range(2):
                cut = slice(p + t * LANES, p + (t + 1) * LANES)
                noise = aux[q, :, cut].astype(F32)[3:4]
                grad = act_grad[:, t * LANES : (t + 1) * LANES] * slope_of[q, :, cut]
                bias_part = bias_part + grad
                strength_part = strength_part + grad * noise
                stat_part = stat_part + grad * scaled[q, :, cut]
                grad_conv[lax.rem(q, 2), :, cut] = (grad * back).astype(BF16)
        chan_acc[0] = bias_part
        chan_acc[1] = strength_part
        stat = jnp.sum(stat_part.T, axis=0, keepdims=True)
        dem = demod_rows[pl.ds(q, 1), :]
        stat_rows[pl.ds(q, 1), :] = stat * (dem * dem * dem) * (-0.5 * conv_gain * conv_gain)

    def tap_grad(q, k):
        a, b = k // 3, k % 3
        return lax.dot_general(
            grids[q, b, :, a * LANES : a * LANES + s.px], grad_conv[lax.rem(q, 2)], NT, preferred_element_type=F32
        )

    pltpu.make_async_copy(
        grids.at[0, 1, pl.ds(0, s.group * s.ch), middle],
        grids.at[0, 1, pl.ds(0, s.group * s.ch), middle],
        f_local.at[0],
    ).wait()
    take_line(0)
    take_mate(0)
    inner(0)
    border(0)

    taken(weights.at[:, pl.ds(0, s.ch), :], w_recv.at[len(s.bits)])
    if s.split:
        taken(weights.at[:, pl.ds(0, plane_rows), :], w_recv.at[len(s.bits) + 1])
    square = jnp.zeros((s.width, s.half), F32)
    for k in range(TAPS):
        w = weights[k]
        weights_t[:, k * s.width : (k + 1) * s.width] = w.T
        wf = w.astype(F32)
        square = square + wf * wf
    weight_sq[...] = square
    demod_sq = jnp.dot(rows_all * rows_all, weight_sq[...], precision=HIGHEST, preferred_element_type=F32)
    demod = lax.rsqrt(conv_gain * conv_gain * demod_sq + DEMOD_EPSILON)
    demod_rows[...] = demod
    demod_t = demod.T
    for q in range(s.group):
        demod_cols[q] = jnp.broadcast_to(demod_t[:, q : q + 1], (s.half, LANES))

    def add_taps(q, taps):
        for k in taps:
            total[k] += tap_grad(q, k)

    def stage(q, carry):
        convolve(q)
        take_line(q + 1)

        @pl.when(q > 0)
        def _():
            add_taps(q - 1, range(TAPS // 2))

        take_mate(q + 1)

        @pl.when(q > 0)
        def _():
            add_taps(q - 1, range(TAPS // 2, TAPS))

        signal_back(q)
        inner(q + 1)
        border(q + 1)
        return carry

    lax.fori_loop(0, last, stage, 0)

    convolve(last)
    add_taps(last - 1, range(TAPS))
    signal_back(last)
    small_own[0:1] = jnp.sum(chan_acc[0].T, axis=0, keepdims=True)
    small_own[1:2] = jnp.sum(chan_acc[1].T, axis=0, keepdims=True)
    small_own[2:3] = loss_acc[...]
    small_own[3:8] = jnp.zeros((5, s.half), F32)
    small_own[8:16] = rgb_acc[...]
    small_plane[place] = small_own[...]
    for dd, mm in near:
        copy_to(small_own, small_plane.at[place], sp_sem.at[0], sp_sem.at[1], dd, mm).start()
    cross = 2.0 * jnp.dot(
        columns[...] * columns[...], stat_rows[...], precision=HIGHEST, preferred_element_type=F32
    )
    weight_sq[...] = cross

    def share_rows(share_of):
        return pl.ds(pl.multiple_of(share_of * s.rows, 16), s.rows)

    own_rows = share_rows(share)
    own_cols = pl.ds(pl.multiple_of(c * s.half, LANES), s.half)
    targets = near if s.split else [(d, mate)]

    def last_tap(k):
        grad = total[k] + tap_grad(last, k) + weights[k].astype(F32) * weight_sq[...]
        grad = grad.astype(BF16).reshape(s.mp, s.ch, s.half)
        if k < s.first:
            share_out[k] = grad
            for r in range(1, s.dp):
                part = share_out.at[k, :, share_rows(d_at(r) if s.split else 0), :]
                copy_to(part, share_in.at[d, k], r_send.at[0], r_recv.at[k], d_at(r), m).start()
        else:
            b = k - s.first
            wide_out[b] = grad
            for r in range(1, s.chips):
                part = wide_out.at[b, pl.ds(2 * z_at(r), 2)]
                copy_to(part, wide_in.at[r, b], l_send.at[1], b_recv.at[b], d, 2 * z_at(r) + c).start()

    def by_shares(own, parts):
        acc = None
        for dd in range(s.dp):
            term = jnp.where(d == dd, own, parts[dd].astype(F32))
            acc = term if acc is None else acc + term
        return acc

    def plane_done(k):
        taken(share_in.at[pl.ds(0, s.dp - 1), k], r_recv.at[k])
        acc = by_shares(share_out[k, :, own_rows, :].astype(F32), [share_in[dd, k] for dd in range(s.dp)])
        line_out[:, k] = acc.astype(BF16).reshape(s.chips, 2, s.rows, s.half)
        for r in range(1, s.chips):
            copy_to(
                line_out.at[z_at(r), k], line_in.at[r, k], l_send.at[0], l_recv.at[k], d, 2 * z_at(r) + c
            ).start()

    def line_done(b):
        taken(wide_in.at[pl.ds(1, s.chips - 1), b], b_recv.at[b])
        acc = wide_out[b, pl.ds(2 * z, 2)].astype(F32)
        for r in range(1, s.chips):
            acc = acc + wide_in[r, b].astype(F32)
        wide_sum[b] = acc.astype(BF16)
        for r in range(1, s.dp):
            part = wide_sum.at[b, :, share_rows(d_at(r) if s.split else 0), :]
            copy_to(part, narrow_in.at[d, b], r_send.at[1], n_recv.at[b], d_at(r), m).start()

    def byte_count():
        return weights.at[:, pl.ds(0, len(targets) * s.rows), :]

    def finish(first_tap):
        for k in range(first_tap, first_tap + s.taps_each):
            if k < s.first:
                taken(line_in.at[pl.ds(1, s.chips - 1), k], l_recv.at[k])
                acc = line_out[z, k].astype(F32)
                for r in range(1, s.chips):
                    acc = acc + line_in[r, k].astype(F32)
            else:
                b = k - s.first
                taken(narrow_in.at[pl.ds(0, s.dp - 1), b], n_recv.at[b])
                acc = by_shares(wide_sum[b, :, own_rows, :].astype(F32), [narrow_in[dd, b] for dd in range(s.dp)])
            final[:, k] = acc.astype(BF16)
            gathered[k, own_rows, own_cols] = final[c, k]
        taps = pl.ds(first_tap, s.taps_each)
        for dd, mm in targets:
            copy_to(
                final.at[lax.rem(mm, 2), taps],
                gathered.at[taps, own_rows, own_cols],
                g_sem.at[0],
                g_sem.at[1],
                dd,
                mm,
            ).start()

    for k in (0, 6, 1, 2, 7, 3, 4, 8, 5):
        last_tap(k)

    taken(small_plane.at[pl.ds(0, 2 * s.dp - 1)], sp_sem.at[1])
    for h in range(2):
        acc = small_plane[h, 0:8]
        for dd in range(1, s.dp):
            acc = acc + small_plane[2 * dd + h, 0:8]
        row = lax.broadcasted_iota(jnp.int32, (8, s.half), 0)
        small_mid[h, 0:8] = jnp.where(row < 2, acc, small_plane[h, 0:8])
        small_mid[h, 8:16] = small_plane[h, 8:16]
    small_line[z] = small_mid[...]
    for r in range(1, s.chips):
        copy_to(small_mid, small_line.at[z], sl_sem.at[0], sl_sem.at[1], d, 2 * z_at(r) + c).start()

    plane_done(0)
    line_done(0)
    plane_done(1)
    plane_done(2)
    line_done(1)
    plane_done(3)
    finish(0)
    plane_done(4)
    line_done(2)
    plane_done(5)
    finish(6)
    finish(3)
    taken(small_line.at[pl.ds(0, s.chips - 1)], sl_sem.at[1])
    sums = small_line[0]
    for zz in range(1, s.chips):
        sums = sums + small_line[zz]
    small_sum[...] = sums
    chan_squares = jnp.sum(sums[:, 0:2] * sums[:, 0:2]) + jnp.sum(sums[:, 8:16] * sums[:, 8:16])
    start = m * s.ch
    first = lax.rem(start, s.half)
    block = pl.multiple_of(lax.div(first, LANES) * LANES, LANES)
    mine = small_sum[lax.div(start, s.half), :, pl.ds(block, LANES)]
    small_out[...] = pltpu.roll(mine, lax.rem(2 * LANES - lax.rem(first, LANES), LANES), 1)

    taken(byte_count(), g_sem.at[1])
    acc = jnp.zeros((s.ch, s.width), F32)
    for k in range(TAPS):
        grad = gathered[k].astype(F32)
        acc = acc + grad * grad
    square_all[m] = jnp.broadcast_to(jnp.sum(acc, keepdims=True), (8, LANES))
    for dd, mm in line:
        copy_to(square_all.at[m], square_all.at[m], n_sem.at[0], n_sem.at[1], dd, mm).start()
    grad_out[...] = gathered[...]
    taken(square_all.at[pl.ds(0, s.mp - 1)], n_sem.at[1])
    acc = square_all[0]
    for mm in range(1, s.mp):
        acc = acc + square_all[mm]
    norm_out[...] = jnp.sqrt(acc + chan_squares)

    gone(weights.at[:, pl.ds(0, sent_rows), :], w_send.at[0])
    if s.split:
        gone(weights.at[:, pl.ds(0, plane_rows), :], w_send.at[1])
    gone(pack_all.at[pl.ds(0, s.mp - 1)], p_sem.at[0])
    for q in range(s.group):
        gone(grids.at[q, 1, pl.ds(0, (2 * s.chips - 1) * s.ch), middle], f_send.at[q])
        gone(proj_all.at[q, pl.ds(0, 2 * s.dp - 1)], j_send.at[q])
    gone(small_plane.at[pl.ds(0, 2 * s.dp - 1)], sp_sem.at[0])
    gone(share_in.at[pl.ds(0, s.dp - 1)], r_send.at[0])
    gone(small_line.at[pl.ds(0, s.chips - 1)], sl_sem.at[0])
    gone(line_in.at[pl.ds(1, s.chips - 1)], l_send.at[0])
    gone(wide_in.at[pl.ds(1, s.chips - 1)], l_send.at[1])
    gone(narrow_in.at[pl.ds(0, s.dp - 1)], r_send.at[1])
    gone(byte_count(), g_sem.at[0])
    gone(square_all.at[pl.ds(0, s.mp - 1)], n_sem.at[0])

    @pl.when(d > 0)
    def _():
        for q in range(s.group):
            halo_up(q).wait_send()

    @pl.when(d < s.dp - 1)
    def _():
        for q in range(s.group):
            halo_down(q).wait_send()


def run_kernel(s, *operands):
    vm, dma = pltpu.VMEM, pltpu.SemaphoreType.DMA
    rest = TAPS - s.first
    scratch = [
        vm((s.ch, s.images, s.px), BF16),
        vm((s.ch, s.images, LANES), F32),
        vm((s.blocks, s.ch * s.images, LANES), F32),
        vm((s.images, s.ch, s.px), BF16),
        vm((s.group, 3, s.width, s.ext), BF16),
        vm((TAPS, s.ch, s.width), F32),
        vm((TAPS, s.ch, s.width), BF16),
        vm((TAPS, s.width, s.half), BF16),
        vm((s.half, TAPS * s.width), BF16),
        vm((s.width, s.half), F32),
        vm((s.chips, 16, LANES), F32),
        vm((s.mp, 16, LANES), F32),
        vm((s.width, 16), F32),
        vm((3, s.ch), BF16),
        vm((2, 8, s.half), F32),
        vm((16, s.half), F32),
        vm((s.group, s.half, LANES), F32),
        vm((2, s.half, LANES), F32),
        vm((3, s.images, s.px), BF16),
        vm((s.images, s.px), BF16),
        vm((s.images, s.px), jnp.int32),
        vm((4, s.images, s.px), F32),
        vm((s.group, 16, s.px), F32),
        vm((s.group, 16, s.px), BF16),
        vm((s.group, 2, s.width // 2, LANES), BF16),
        vm((s.group, 2, s.width // 2, LANES), BF16),
        vm((s.group, s.half, s.px), F32),
        vm((s.group, s.half, s.px), F32),
        vm((s.group, 2 * s.dp, 8, s.half), F32),
        vm((2, 2, 8, s.half), F32),
        vm((16, s.half), F32),
        vm((8, s.half), F32),
        vm((1, s.half), F32),
        vm((2, s.half, LANES), F32),
        vm((2, s.half, s.px), BF16),
        vm((TAPS, s.width, s.half), F32),
        vm((s.first, s.mp, s.ch, s.half), BF16),
        vm((s.dp, s.first, s.mp, s.rows, s.half), BF16),
        vm((s.chips, s.first, 2, s.rows, s.half), BF16),
        vm((s.chips, s.first, 2, s.rows, s.half), BF16),
        vm((rest, s.mp, s.ch, s.half), BF16),
        vm((s.chips, rest, 2, s.ch, s.half), BF16),
        vm((rest, 2, s.ch, s.half), BF16),
        vm((s.dp, rest, 2, s.rows, s.half), BF16),
        vm((2, TAPS, s.rows, s.half), BF16),
        vm((TAPS, s.ch, s.width), BF16),
        vm((16, s.half), F32),
        vm((2 * s.dp, 16, s.half), F32),
        vm((2, 16, s.half), F32),
        vm((s.chips, 2, 16, s.half), F32),
        vm((2, 16, s.half), F32),
        vm((s.mp, 8, LANES), F32),
        dma((5,)),
        dma((2,)),
        dma((len(s.bits) + 2,)),
        dma((2,)),
        dma((s.group,)),
        dma((s.group, 2)),
        dma((1,)),
        dma((s.group, 2)),
        dma((s.group, 2)),
        dma((s.group,)),
        dma((s.group,)),
        dma((2,)),
        dma((s.first,)),
        dma((2,)),
        dma((s.first,)),
        dma((rest,)),
        dma((rest,)),
        dma((2,)),
        dma((2,)),
        dma((2,)),
        dma((2,)),
    ]
    flops = 2 * 2 * s.group * s.px * s.half * s.width * TAPS
    here, there = pl.BlockSpec(memory_space=pltpu.VMEM), pl.BlockSpec(memory_space=pl.ANY)
    return pl.pallas_call(
        functools.partial(kernel, s),
        out_shape=(
            jax.ShapeDtypeStruct((TAPS, s.ch, s.width), BF16),
            jax.ShapeDtypeStruct((16, LANES), F32),
            jax.ShapeDtypeStruct((8, LANES), F32),
        ),
        in_specs=[there, here, there, here, here, there, there, there, pl.BlockSpec(memory_space=pltpu.SMEM)],
        out_specs=[here] * 3,
        scratch_shapes=scratch,
        compiler_params=pltpu.CompilerParams(
            collective_id=0, has_side_effects=True, vmem_limit_bytes=62 * 2**20
        ),
        cost_estimate=pl.CostEstimate(flops=flops, bytes_accessed=2**23, transcendentals=2**20),
        name="synthesis_step",
    )(*operands)


def adam_update(weight, moment, second, gradient, factor):
    clipped = gradient * factor
    moment_new = BETA_FIRST * moment + (1.0 - BETA_FIRST) * clipped
    second_new = BETA_SECOND * second + (1.0 - BETA_SECOND) * clipped * clipped
    moment_hat = moment_new / (1.0 - BETA_FIRST**STEP)
    second_hat = second_new / (1.0 - BETA_SECOND**STEP)
    weight_new = weight - LEARN_RATE * (
        moment_hat / (jnp.sqrt(second_hat) + ADAM_EPSILON) + DECAY_RATE * weight
    )
    return (moment_new, second_new, weight_new)


def adam_kernel(
    s,
    grad,
    sums,
    norm,
    conv_w,
    conv_m,
    conv_v,
    chan_w,
    chan_m,
    chan_v,
    rgb_w,
    rgb_m,
    rgb_v,
    loss_out,
    norm_out,
    conv_m_out,
    conv_v_out,
    conv_w_out,
    conv_low_out,
    chan_m_out,
    chan_v_out,
    chan_w_out,
    rgb_m_out,
    rgb_v_out,
    rgb_w_out,
    rgb_low_out,
):
    factor = jnp.minimum(1.0, CLIP_LIMIT / (norm[0:1, 0:1] + 1e-06))
    moment, second, weight = adam_update(
        conv_w[...], conv_m[...], conv_v[...], grad[...].astype(F32), factor[None]
    )
    conv_m_out[...] = moment
    conv_v_out[...] = second
    conv_w_out[...] = weight
    conv_low_out[...] = weight.astype(BF16)

    @pl.when(pl.program_id(0) == 0)
    def _():
        loss_out[0] = sums[2, 0]
        norm_out[0] = norm[0, 0]
        moment, second, weight = adam_update(
            chan_w[...], chan_m[...], chan_v[...], sums[0:2, : s.ch], factor
        )
        chan_m_out[...] = moment
        chan_v_out[...] = second
        chan_w_out[...] = weight
        moment, second, weight = adam_update(
            rgb_w[...], rgb_m[...], rgb_v[...], sums[8:11, : s.ch], factor
        )
        rgb_m_out[...] = moment
        rgb_v_out[...] = second
        rgb_w_out[...] = weight
        rgb_low_out[...] = weight.astype(BF16)


def run_adam(s, *operands):
    steps = 3
    taps = pl.BlockSpec((TAPS // steps, s.ch, s.width), lambda i: (i, 0, 0))

    def small(shape):
        return pl.BlockSpec(shape, lambda i: (0, 0))

    scalar = pl.BlockSpec(memory_space=pltpu.SMEM)
    conv = jax.ShapeDtypeStruct((TAPS, s.ch, s.width), F32)
    chan = jax.ShapeDtypeStruct((2, s.ch), F32)
    rgb = jax.ShapeDtypeStruct((3, s.ch), F32)
    one = jax.ShapeDtypeStruct((1,), F32)
    return pl.pallas_call(
        functools.partial(adam_kernel, s),
        grid=(steps,),
        out_shape=(one, one)
        + (conv,) * 3
        + (jax.ShapeDtypeStruct(conv.shape, BF16),)
        + (chan,) * 3
        + (rgb,) * 3
        + (jax.ShapeDtypeStruct(rgb.shape, BF16),),
        in_specs=[taps, small((16, LANES)), small((8, LANES))]
        + [taps] * 3
        + [small((2, s.ch))] * 3
        + [small((3, s.ch))] * 3,
        out_specs=[scalar, scalar] + [taps] * 4 + [small((2, s.ch))] * 3 + [small((3, s.ch))] * 4,
        compiler_params=pltpu.CompilerParams(vmem_limit_bytes=62 * 2**20),
        name="optimizer_step",
    )(*operands)


def local(
    mesh_shape,
    features,
    styles,
    noise_field,
    noise_keep,
    path_noise,
    length_mean,
    conv_weight,
    conv_moment,
    conv_second,
    chan_params,
    chan_moment,
    chan_second,
    rgb_weight,
    rgb_moment,
    rgb_second,
):
    s = Sizes(mesh_shape, features.shape, conv_weight.shape)
    taps_first = functools.partial(jnp.transpose, axes=(1, 0, 2))
    weight = taps_first(conv_weight)
    grad, sums, norm = run_kernel(
        s,
        features,
        styles,
        weight,
        chan_params,
        rgb_weight,
        path_noise,
        noise_field,
        noise_keep,
        length_mean,
    )
    outs = run_adam(
        s,
        grad,
        sums,
        norm,
        weight,
        taps_first(conv_moment),
        taps_first(conv_second),
        chan_params,
        chan_moment,
        chan_second,
        rgb_weight,
        rgb_moment,
        rgb_second,
    )
    return outs[:2] + tuple(taps_first(x) for x in outs[2:6]) + outs[6:]


def solution(mesh):
    whole, line = P(), P("mp", None, None)
    row, pixels = P(None, "mp"), P(None, "dp")
    in_specs = (
        P("mp", None, "dp"),
        row,
        pixels,
        pixels,
        P(None, None, "dp"),
        whole,
        line,
        line,
        line,
    ) + (row,) * 6
    out_specs = (whole, whole) + (line,) * 4 + (row,) * 7
    return jax.shard_map(
        functools.partial(local, dict(mesh.shape)),
        mesh=mesh,
        in_specs=in_specs,
        out_specs=out_specs,
        check_vma=False,
    )
```

```python
import functools
import math

import jax
import jax.numpy as jnp
from jax import lax
from jax.experimental import pallas as pl
from jax.experimental.pallas import tpu as pltpu
from jax.sharding import PartitionSpec as P

SIDE = 64
STEP = 5
TAPS = 9
LANES = 128

CLIP_LIMIT = 0.1
LEARN_RATE = 0.3
DECAY_RATE = 0.01
BETA_FIRST = 0.5
BETA_SECOND = 0.5
ADAM_EPSILON = 1e-08
DEMOD_EPSILON = 1e-08
HIGHEST = lax.Precision.HIGHEST
MESH = pl.DeviceIdType.MESH
F32 = jnp.float32
BF16 = jnp.bfloat16
NT = (((1,), (1,)), ((), ()))


class Sizes:
    def __init__(self, mesh_shape, features, conv_weight):
        self.dp = mesh_shape["dp"]
        self.mp = mesh_shape["mp"]
        self.chips = self.mp // 2
        self.ch, self.images, self.px = features
        self.width = conv_weight[2]
        self.half = self.width // 2
        self.group = self.images // self.chips
        self.blocks = self.px // LANES
        self.ext = self.px + 2 * LANES
        self.split = (self.ch // self.dp) % 16 == 0
        self.shares = self.dp if self.split else 1
        self.rows = self.ch // self.shares
        self.first = 7
        self.part = 3
        self.bits = []
        bit = self.chips // 2
        while bit >= 1:
            self.bits.append(bit)
            bit //= 2


def flip(value, bit):
    return value + bit - 2 * bit * lax.rem(lax.div(value, bit), 2)


def swap_halves(x):
    return pltpu.roll(x, SIDE, x.ndim - 1)


def kernel(
    s,
    feat_hbm,
    styles,
    weight_hbm,
    chan,
    rgb,
    path_hbm,
    field_hbm,
    keep_hbm,
    mean,
    grad_out,
    small_out,
    norm_out,
    feat,
    style_cols,
    turned,
    outbox,
    grids,
    weight_own,
    weight_low,
    weights,
    weights_t,
    weight_sq,
    pack,
    pack_all,
    columns,
    rgb_low,
    rgb_rows,
    demod_rows,
    demod_cols,
    chan_cols,
    path,
    field,
    keep,
    pixel_rows,
    aux_rows,
    aux,
    halo_out,
    halo_in,
    scaled,
    slope_of,
    proj_all,
    half_pick,
    stat_rows,
    rgb_acc,
    loss_acc,
    chan_acc,
    grad_conv,
    total,
    share_out,
    share_in,
    line_out,
    line_in,
    wide_out,
    wide_in,
    wide_sum,
    narrow_in,
    final,
    small_own,
    small_plane,
    small_mid,
    small_line,
    small_sum,
    square_near,
    square_line,
    in_sem,
    w_send,
    w_recv,
    p_sem,
    f_send,
    f_recv,
    f_local,
    h_send,
    h_recv,
    j_send,
    j_recv,
    r_send,
    r_recv,
    l_send,
    l_recv,
    b_recv,
    n_recv,
    g_sem,
    sp_sem,
    sl_sem,
    q_sem,
):
    d = lax.axis_index("dp")
    m = lax.axis_index("mp")
    z = lax.div(m, 2)
    c = lax.rem(m, 2)
    other = 1 - c
    mate = 2 * z + other
    conv_gain = 1.0 / math.sqrt(TAPS * s.width)
    rgb_gain = 1.0 / math.sqrt(s.width)
    last = s.group - 1

    def copy_to(src, dst, send, recv, dd, mm):
        return pltpu.make_async_remote_copy(
            src_ref=src, dst_ref=dst, send_sem=send, recv_sem=recv, device_id=(dd, mm), device_id_type=MESH
        )

    def taken(ref, sem):
        copy_to(ref, ref, sem, sem, d, mate).wait_recv()

    def gone(ref, sem):
        copy_to(ref, ref, sem, sem, d, mate).wait_send()

    def z_at(r):
        return lax.rem(z + r, s.chips)

    def d_at(r):
        return lax.rem(d + r, s.dp)

    line = [(d, lax.rem(m + r, s.mp)) for r in range(1, s.mp)]
    plane = [(d_at(r), mm) for r in range(1, s.dp) for mm in (m, mate)]
    near = plane + [(d, mate)]
    place = 2 * d + c

    get_weight = pltpu.make_async_copy(weight_hbm, weight_own, in_sem.at[0])
    get_feat = pltpu.make_async_copy(feat_hbm, feat, in_sem.at[1])
    get_path = pltpu.make_async_copy(path_hbm, path, in_sem.at[2])
    get_field = pltpu.make_async_copy(field_hbm, field, in_sem.at[3])
    get_keep = pltpu.make_async_copy(keep_hbm, keep, in_sem.at[4])
    get_weight.start()
    get_feat.start()
    get_path.start()
    get_field.start()
    get_keep.start()
    halo_in[...] = jnp.zeros_like(halo_in)
    barrier = pltpu.get_barrier_semaphore()
    for dd, mm in line + plane:
        pl.semaphore_signal(barrier, inc=1, device_id=(dd, mm), device_id_type=MESH)
    pack[...] = jnp.zeros_like(pack)
    rgb_low[...] = rgb[...].astype(BF16)
    rgb_eff = rgb_low[...].astype(F32) * rgb_gain
    for zz in range(s.chips):
        pack[zz, : s.group, : s.ch] = styles[zz * s.group : (zz + 1) * s.group, :]
        pack[zz, s.group : s.group + 2, : s.ch] = chan[...]
        pack[zz, 8:11, : s.ch] = rgb_eff
    pack_all[m] = pack[z]
    for i in range(s.ch):
        style_cols[i] = jnp.broadcast_to(styles[:, i : i + 1], (s.images, LANES))

    get_weight.wait()
    for k in range(TAPS):
        weight_low[k] = weight_own[k].astype(BF16)
    pl.semaphore_wait(barrier, len(line) + len(plane))

    share = d if s.split else 0

    def piece(m_of):
        return weights.at[:, pl.ds(pl.multiple_of(m_of * s.ch + share * s.rows, 16), s.rows), :]

    def own_piece(half_of):
        return weight_low.at[
            :,
            pl.ds(pl.multiple_of(share * s.rows, 16), s.rows),
            pl.ds(pl.multiple_of(half_of * s.half, LANES), s.half),
        ]

    sent_rows = 0
    for index, bit in enumerate(s.bits):
        for cc in range(2):
            copy_to(
                own_piece(cc), piece(m), w_send.at[0], w_recv.at[index], d, 2 * flip(z, bit) + cc
            ).start()
            sent_rows += s.rows
    copy_to(
        weight_low.at[:, :, pl.ds(pl.multiple_of(other * s.half, LANES), s.half)],
        weights.at[:, pl.ds(pl.multiple_of(m * s.ch, 16), s.ch), :],
        w_send.at[0],
        w_recv.at[len(s.bits)],
        d,
        mate,
    ).start()
    sent_rows += s.ch
    for dd, mm in line:
        copy_to(pack.at[lax.div(mm, 2)], pack_all.at[m], p_sem.at[0], p_sem.at[1], dd, mm).start()

    get_feat.wait()
    lane = lax.broadcasted_iota(jnp.int32, (1, 1, LANES), 2)
    low_lanes = lane < SIDE
    step = 8

    def modulate(index, carry):
        rows = pl.ds(pl.multiple_of(index * step, step), step)
        factor = style_cols[rows]
        for q in range(s.blocks // 2):
            first = feat[rows, :, q * LANES : (q + 1) * LANES].astype(F32) * factor
            q2 = q + s.blocks // 2
            second = feat[rows, :, q2 * LANES : (q2 + 1) * LANES].astype(F32) * factor
            even = jnp.where(low_lanes, first, swap_halves(second))
            odd = jnp.where(low_lanes, swap_halves(first), second)
            out_rows = pl.ds(pl.multiple_of(index * step * s.images, step * 8), step * s.images)
            turned[2 * q, out_rows, :] = even.reshape(step * s.images, LANES)
            turned[2 * q + 1, out_rows, :] = odd.reshape(step * s.images, LANES)
        return carry

    lax.fori_loop(0, s.ch // step, modulate, 0)

    def pick(n, carry):
        for j in range(s.blocks):
            part = turned[j, pl.ds(n, s.ch, stride=s.images), :]
            outbox[n, :, j * LANES : (j + 1) * LANES] = part.astype(BF16)
        return carry

    lax.fori_loop(0, s.images, pick, 0)

    middle = pl.ds(LANES, s.px)

    def grid_rows(m_of):
        return pl.ds(pl.multiple_of(m_of * s.ch, 16), s.ch)

    def feature_send(q, r):
        zz = z_at(r)
        return copy_to(
            outbox.at[zz * s.group + q],
            grids.at[q, 1, grid_rows(m), middle],
            f_send.at[q],
            f_recv.at[q, 0],
            d,
            2 * zz + c,
        )

    def start_features():
        for q in range(s.group):
            own = outbox.at[z * s.group + q]
            there = grids.at[q, 1, grid_rows(m), middle]
            pltpu.make_async_copy(own, there, f_local.at[0]).start()
            copy_to(own, there, f_send.at[q], f_recv.at[q, 1], d, mate).start()
            if q < 2:
                for r in range(1, s.chips):
                    feature_send(q, r).start()

    held = [z]
    plane_rows = 0
    for index, bit in enumerate(s.bits):
        peer = flip(z, bit)
        for h in held[1:]:
            for cc in range(2):
                at = piece(2 * h + cc)
                copy_to(at, at, w_send.at[0], w_recv.at[index], d, 2 * peer + c).start()
                sent_rows += s.rows
        if index == len(s.bits) - 1:
            start_features()
        fresh = [flip(h, bit) for h in held]
        taken(weights.at[:, pl.ds(0, 2 * len(fresh) * s.rows), :], w_recv.at[index])
        if s.split:
            for h in fresh:
                for cc in range(2):
                    at = piece(2 * h + cc)
                    for r in range(1, s.dp):
                        copy_to(at, at, w_send.at[1], w_recv.at[len(s.bits) + 1], d_at(r), m).start()
                        plane_rows += s.rows
        held = held + fresh

    weights[:, grid_rows(m), :] = weight_low[:, :, pl.ds(pl.multiple_of(c * s.half, LANES), s.half)]
    get_path.wait()
    get_field.wait()
    get_keep.wait()
    lane2 = lax.broadcasted_iota(jnp.int32, (1, LANES), 1)
    low2 = lane2 < SIDE
    for k in range(4):
        for q in range(s.blocks // 2):
            q2 = q + s.blocks // 2
            cuts = [slice(q * LANES, (q + 1) * LANES), slice(q2 * LANES, (q2 + 1) * LANES)]
            if k < 3:
                first, second = [path[k, :, cut].astype(F32) for cut in cuts]
            else:
                first, second = [field[:, cut].astype(F32) * keep[:, cut].astype(F32) for cut in cuts]
            pixel_rows[k, :, 2 * q * LANES : (2 * q + 1) * LANES] = jnp.where(low2, first, swap_halves(second))
            pixel_rows[k, :, (2 * q + 1) * LANES : (2 * q + 2) * LANES] = jnp.where(low2, swap_halves(first), second)
    aux_rows[...] = jnp.zeros_like(aux_rows)
    for q in range(s.group):
        for k in range(4):
            row = pixel_rows[k, pl.ds(z * s.group + q, 1), :]
            aux_rows[q, k : k + 1, :] = row
            if k < 3:
                aux_rows[q, 8 + k : 9 + k, :] = row
        aux[q] = aux_rows[q].astype(BF16)

    taken(pack_all.at[pl.ds(0, s.mp - 1)], p_sem.at[1])
    for mm in range(s.mp):
        columns[mm * s.ch : (mm + 1) * s.ch, :] = pack_all[mm].T[: s.ch, :]
    rows_all = columns[...].T
    for h in range(2):
        rgb_rows[h] = rows_all[8:16, h * s.half : (h + 1) * s.half]
    mine = columns[pl.ds(pl.multiple_of(c * s.half, 8), s.half), :]
    for k in range(2):
        chan_cols[k] = jnp.broadcast_to(mine[:, s.group + k : s.group + k + 1], (s.half, LANES))
    total[...] = jnp.zeros_like(total)
    stat_rows[...] = jnp.zeros_like(stat_rows)
    rgb_acc[...] = jnp.zeros_like(rgb_acc)
    loss_acc[...] = jnp.zeros_like(loss_acc)
    chan_acc[...] = jnp.zeros_like(chan_acc)

    column = lax.rem(lane2, SIDE)
    not_first = column >= 1
    not_last = column <= SIDE - 2
    pair = s.width // 2
    up = lax.rem(d + s.dp - 1, s.dp)
    down = lax.rem(d + 1, s.dp)

    def halo_up(q):
        return copy_to(halo_out.at[q, 0], halo_in.at[q, 1], h_send.at[q, 0], h_recv.at[q, 1], up, m)

    def halo_down(q):
        return copy_to(halo_out.at[q, 1], halo_in.at[q, 0], h_send.at[q, 1], h_recv.at[q, 0], down, m)

    def ends(q):
        return grids[q, 1, :, LANES : 2 * LANES], grids[q, 1, :, s.px : s.px + LANES]

    def take_line(q):
        taken(grids.at[q, 1, pl.ds(0, (s.chips - 1) * s.ch), middle], f_recv.at[q, 0])
        for r in range(1, s.chips):
            at = grids.at[q, 1, grid_rows(2 * z_at(r) + c), middle]
            copy_to(at, at, f_send.at[q], f_recv.at[q, 1], d, mate).start()

        @pl.when(q + 2 < s.group)
        def _():
            for r in range(1, s.chips):
                feature_send(q + 2, r).start()

    def take_mate(q):
        taken(grids.at[q, 1, pl.ds(0, s.chips * s.ch), middle], f_recv.at[q, 1])
        top, end = ends(q)
        halo_out[q, 0] = jnp.where(low2, top[:pair], swap_halves(top[pair:]))
        halo_out[q, 1] = jnp.where(low2, swap_halves(end[:pair]), end[pair:])

        @pl.when(d > 0)
        def _():
            halo_up(q).start()

        @pl.when(d < s.dp - 1)
        def _():
            halo_down(q).start()

    def lateral(q, j):
        x = grids[q, 1, :, j * LANES : (j + 1) * LANES]
        none = jnp.zeros_like(x)
        grids[q, 0, :, j * LANES : (j + 1) * LANES] = jnp.where(not_first, pltpu.roll(x, 1, 1), none)
        grids[q, 2, :, j * LANES : (j + 1) * LANES] = jnp.where(not_last, pltpu.roll(x, LANES - 1, 1), none)

    def inner(q):
        for j in range(1, s.blocks + 1):
            lateral(q, j)

    def border(q):
        @pl.when(d > 0)
        def _():
            halo_down(q).wait_recv()

        @pl.when(d < s.dp - 1)
        def _():
            halo_up(q).wait_recv()

        top, end = ends(q)
        above = halo_in[q, 0]
        below = halo_in[q, 1]
        swapped_end = swap_halves(end)
        swapped_top = swap_halves(top)
        grids[q, 1, :pair, :LANES] = jnp.where(low2, above, swapped_end[:pair])
        grids[q, 1, pair:, :LANES] = jnp.where(low2, swap_halves(above), swapped_end[pair:])
        tail = s.px + LANES
        grids[q, 1, :pair, tail : tail + LANES] = jnp.where(low2, swapped_top[:pair], swap_halves(below))
        grids[q, 1, pair:, tail : tail + LANES] = jnp.where(low2, swapped_top[pair:], below)
        lateral(q, 0)
        lateral(q, s.blocks + 1)

    def blocks_of(ref, first, second):
        if second == first + 1:
            return ref[:, first * LANES : (second + 1) * LANES]
        return jnp.concatenate([ref[:, j * LANES : (j + 1) * LANES] for j in (first, second)], axis=1)

    def convolve(q, first, second):
        acc = jnp.zeros((s.half, 2 * LANES), F32)
        for a in range(3):
            for b in range(3):
                k = 3 * a + b
                acc += jnp.dot(
                    weights_t[:, k * s.width : (k + 1) * s.width],
                    blocks_of(grids.at[q, b], first + a, second + a),
                    preferred_element_type=F32,
                )
        acts = []
        for t, j in enumerate((first, second)):
            cut = slice(j * LANES, (j + 1) * LANES)
            conv = acc[:, t * LANES : (t + 1) * LANES] * conv_gain
            noise = aux[q, :, cut].astype(F32)[3:4]
            pre = conv * demod_cols[q] + chan_cols[1] * noise + chan_cols[0]
            sig = jax.nn.sigmoid(pre)
            act = pre * sig
            scaled[q, :, cut] = conv
            slope_of[q, :, cut] = sig * (1.0 + pre * (1.0 - sig))
            acts.append(act.astype(BF16))
        act = jnp.concatenate(acts, axis=1)
        return lax.dot_general(blocks_of(aux.at[q], first, second), act, NT, preferred_element_type=F32)[:8]

    def convolve_inner(q):
        projected = jnp.zeros((8, s.half), F32)
        for j in range(1, s.blocks - 1, 2):
            projected += convolve(q, j, j + 1)
        proj_all[q, place] = projected

    def convolve_border(q):
        proj_all[q, place] += convolve(q, 0, s.blocks - 1)
        for dd, mm in near:
            at = proj_all.at[q, place]
            copy_to(at, at, j_send.at[q], j_recv.at[q], dd, mm).start()

    def signal_back(q):
        taken(proj_all.at[q, pl.ds(0, 2 * s.dp - 1)], j_recv.at[q])
        signal_math(q)

    def signal_math(q):
        halves = []
        for h in range(2):
            acc = proj_all[q, h]
            for dd in range(1, s.dp):
                acc = acc + proj_all[q, 2 * dd + h]
            halves.append(acc)
        slopes = [jnp.sum(rgb_rows[h] * halves[h], axis=0, keepdims=True) for h in range(2)]
        row = lax.broadcasted_iota(jnp.int32, (8, s.half), 0)
        length_sq = jnp.sum(slopes[0] * slopes[0] + slopes[1] * slopes[1], axis=1, keepdims=True)
        length = jnp.sqrt(length_sq + 1e-08)
        excess = length - mean[0]
        loss_acc[...] += jnp.broadcast_to(excess * excess, (1, s.half))
        scale = 2.0 * excess / length
        for h in range(2):
            grad = scale * slopes[h]
            half_pick[h, 0] = grad * rgb_rows[h]
            half_pick[h, 1] = jnp.where(row < 3, grad * halves[h] * rgb_gain, 0.0)
        rgb_acc[...] += half_pick[c, 1]
        coef = half_pick[c, 0]
        high = coef.astype(BF16).astype(F32)
        coef_t = jnp.concatenate([high, coef - high], axis=0).T.astype(BF16)
        wide = 2 * LANES
        bias_part = chan_acc[0]
        strength_part = chan_acc[1]
        stat_part = jnp.zeros((s.half, LANES), F32)
        back = demod_cols[q] * conv_gain
        for p in range(0, s.px, wide):
            act_grad = jnp.dot(coef_t, aux[q, :, p : p + wide], preferred_element_type=F32)
            for t in range(2):
                cut = slice(p + t * LANES, p + (t + 1) * LANES)
                noise = aux[q, :, cut].astype(F32)[3:4]
                grad = act_grad[:, t * LANES : (t + 1) * LANES] * slope_of[q, :, cut]
                bias_part = bias_part + grad
                strength_part = strength_part + grad * noise
                stat_part = stat_part + grad * scaled[q, :, cut]
                grad_conv[lax.rem(q, 2), :, cut] = (grad * back).astype(BF16)
        chan_acc[0] = bias_part
        chan_acc[1] = strength_part
        stat = jnp.sum(stat_part.T, axis=0, keepdims=True)
        dem = demod_rows[pl.ds(q, 1), :]
        stat_rows[pl.ds(q, 1), :] = stat * (dem * dem * dem) * (-0.5 * conv_gain * conv_gain)

    def tap_grad(q, k):
        a, b = k // 3, k % 3
        return lax.dot_general(
            grids[q, b, :, a * LANES : a * LANES + s.px], grad_conv[lax.rem(q, 2)], NT, preferred_element_type=F32
        )

    pltpu.make_async_copy(
        grids.at[0, 1, pl.ds(0, s.group * s.ch), middle],
        grids.at[0, 1, pl.ds(0, s.group * s.ch), middle],
        f_local.at[0],
    ).wait()
    take_line(0)
    take_mate(0)
    inner(0)

    taken(weights.at[:, pl.ds(0, s.ch), :], w_recv.at[len(s.bits)])
    if s.split:
        taken(weights.at[:, pl.ds(0, plane_rows), :], w_recv.at[len(s.bits) + 1])
    square = jnp.zeros((s.width, s.half), F32)
    for k in range(TAPS):
        w = weights[k]
        weights_t[:, k * s.width : (k + 1) * s.width] = w.T
        wf = w.astype(F32)
        square = square + wf * wf
    weight_sq[...] = square
    demod_sq = jnp.dot(rows_all * rows_all, weight_sq[...], precision=HIGHEST, preferred_element_type=F32)
    demod = lax.rsqrt(conv_gain * conv_gain * demod_sq + DEMOD_EPSILON)
    demod_rows[...] = demod
    demod_t = demod.T
    for q in range(s.group):
        demod_cols[q] = jnp.broadcast_to(demod_t[:, q : q + 1], (s.half, LANES))

    def add_taps(q):
        for k in range(TAPS):
            total[k] += tap_grad(q, k)

    def stage(q, carry):
        border(q)
        convolve_border(q)

        @pl.when(q == last - 1)
        def _():
            if last > 1:
                add_taps(q - 1)
            signal_back(q)

        take_line(q + 1)

        @pl.when(lax.rem(q, last - 1) > 0)
        def _():
            add_taps(q - 1)

        take_mate(q + 1)
        inner(q + 1)
        convolve_inner(q + 1)

        @pl.when(q < last - 1)
        def _():
            signal_back(q)

        return carry

    convolve_inner(0)
    lax.fori_loop(0, last, stage, 0)

    border(last)
    convolve_border(last)
    add_taps(last - 1)
    signal_back(last)
    cross = 2.0 * jnp.dot(
        columns[...] * columns[...], stat_rows[...], precision=HIGHEST, preferred_element_type=F32
    )
    weight_sq[...] = cross

    def share_rows(share_of):
        return pl.ds(pl.multiple_of(share_of * s.rows, 16), s.rows)

    own_rows = share_rows(share)
    own_cols = pl.ds(pl.multiple_of(c * s.half, LANES), s.half)
    targets = near if s.split else [(d, mate)]

    def last_tap(k):
        grad = total[k] + tap_grad(last, k) + weights[k].astype(F32) * weight_sq[...]
        grad = grad.astype(BF16).reshape(s.mp, s.ch, s.half)
        if k < s.first:
            share_out[k] = grad
            for r in range(1, s.dp):
                part = share_out.at[k, :, share_rows(d_at(r) if s.split else 0), :]
                copy_to(part, share_in.at[d, k], r_send.at[0], r_recv.at[k], d_at(r), m).start()
        else:
            b = k - s.first
            wide_out[b] = grad
            for r in range(1, s.chips):
                part = wide_out.at[b, pl.ds(2 * z_at(r), 2)]
                copy_to(part, wide_in.at[r, b], l_send.at[1], b_recv.at[b], d, 2 * z_at(r) + c).start()

    def by_shares(own, parts):
        acc = None
        for dd in range(s.dp):
            term = jnp.where(d == dd, own, parts[dd].astype(F32))
            acc = term if acc is None else acc + term
        return acc

    def plane_done(k):
        taken(share_in.at[pl.ds(0, s.dp - 1), k], r_recv.at[k])
        acc = by_shares(share_out[k, :, own_rows, :].astype(F32), [share_in[dd, k] for dd in range(s.dp)])
        line_out[:, k] = acc.astype(BF16).reshape(s.chips, 2, s.rows, s.half)
        for r in range(1, s.chips):
            copy_to(
                line_out.at[z_at(r), k], line_in.at[r, k], l_send.at[0], l_recv.at[k], d, 2 * z_at(r) + c
            ).start()

    def line_done(b):
        taken(wide_in.at[pl.ds(1, s.chips - 1), b], b_recv.at[b])
        acc = wide_out[b, pl.ds(2 * z, 2)].astype(F32)
        for r in range(1, s.chips):
            acc = acc + wide_in[r, b].astype(F32)
        wide_sum[b] = acc.astype(BF16)
        for r in range(1, s.dp):
            part = wide_sum.at[b, :, share_rows(d_at(r) if s.split else 0), :]
            copy_to(part, narrow_in.at[d, b], r_send.at[1], n_recv.at[b], d_at(r), m).start()

    def byte_count():
        return weights.at[:, pl.ds(0, len(targets) * s.rows), :]

    def finish(k, squares):
        if k < s.first:
            taken(line_in.at[pl.ds(1, s.chips - 1), k], l_recv.at[k])
            acc = line_out[z, k].astype(F32)
            for r in range(1, s.chips):
                acc = acc + line_in[r, k].astype(F32)
        else:
            b = k - s.first
            taken(narrow_in.at[pl.ds(0, s.dp - 1), b], n_recv.at[b])
            acc = by_shares(wide_sum[b, :, own_rows, :].astype(F32), [narrow_in[dd, b] for dd in range(s.dp)])
        final[:, k] = acc.astype(BF16)
        kept = final[:, k].astype(F32)
        return squares + jnp.sum(kept * kept, axis=0)

    def hand_out(first_tap, count):
        taps = pl.ds(first_tap, count)
        there = grad_out.at[taps, own_rows, own_cols]
        for dd, mm in targets:
            copy_to(final.at[lax.rem(mm, 2), taps], there, g_sem.at[0], g_sem.at[1], dd, mm).start()
        pltpu.make_async_copy(final.at[c, taps], there, g_sem.at[2]).start()

    def send_small():
        small_own[0:1] = jnp.sum(chan_acc[0].T, axis=0, keepdims=True)
        small_own[1:2] = jnp.sum(chan_acc[1].T, axis=0, keepdims=True)
        small_own[2:3] = loss_acc[...]
        small_own[3:8] = jnp.zeros((5, s.half), F32)
        small_own[8:16] = rgb_acc[...]
        small_plane[place] = small_own[...]
        for dd, mm in near:
            copy_to(small_own, small_plane.at[place], sp_sem.at[0], sp_sem.at[1], dd, mm).start()

    for index, k in enumerate((0, 7, 1, 2, 3, 8, 4, 5, 6)):
        last_tap(k)
        if index == 1:
            send_small()

    taken(small_plane.at[pl.ds(0, 2 * s.dp - 1)], sp_sem.at[1])
    for h in range(2):
        acc = small_plane[h, 0:8]
        for dd in range(1, s.dp):
            acc = acc + small_plane[2 * dd + h, 0:8]
        row = lax.broadcasted_iota(jnp.int32, (8, s.half), 0)
        small_mid[h, 0:8] = jnp.where(row < 2, acc, small_plane[h, 0:8])
        small_mid[h, 8:16] = small_plane[h, 8:16]
    small_line[z] = small_mid[...]
    for r in range(1, s.chips):
        copy_to(small_mid, small_line.at[z], sl_sem.at[0], sl_sem.at[1], d, 2 * z_at(r) + c).start()

    squares = jnp.zeros((s.rows, s.half), F32)
    plane_done(0)
    plane_done(1)
    line_done(0)
    plane_done(2)
    plane_done(3)
    line_done(1)
    plane_done(4)
    for k in (0, 1, 2):
        squares = finish(k, squares)
    hand_out(0, 3)
    plane_done(5)
    plane_done(6)
    for k in (7, 8, 3, 4, 5, 6):
        squares = finish(k, squares)
    square_near[place] = jnp.broadcast_to(jnp.sum(squares, keepdims=True), (8, LANES))
    for dd, mm in near:
        at = square_near.at[place]
        copy_to(at, at, q_sem.at[0], q_sem.at[1], dd, mm).start()
    hand_out(3, TAPS - 3)
    taken(small_line.at[pl.ds(0, s.chips - 1)], sl_sem.at[1])
    sums = small_line[0]
    for zz in range(1, s.chips):
        sums = sums + small_line[zz]
    small_sum[...] = sums
    chan_squares = jnp.sum(sums[:, 0:2] * sums[:, 0:2]) + jnp.sum(sums[:, 8:16] * sums[:, 8:16])
    start = m * s.ch
    first = lax.rem(start, s.half)
    block = pl.multiple_of(lax.div(first, LANES) * LANES, LANES)
    mine = small_sum[lax.div(start, s.half), :, pl.ds(block, LANES)]
    small_out[...] = pltpu.roll(mine, lax.rem(2 * LANES - lax.rem(first, LANES), LANES), 1)

    taken(square_near.at[pl.ds(0, 2 * s.dp - 1)], q_sem.at[1])
    acc = square_near[0]
    for at in range(1, 2 * s.shares):
        acc = acc + square_near[at]
    square_line[z] = acc
    for r in range(1, s.chips):
        at = square_line.at[z]
        copy_to(at, at, q_sem.at[2], q_sem.at[3], d, 2 * z_at(r) + c).start()
    taken(square_line.at[pl.ds(0, s.chips - 1)], q_sem.at[3])
    acc = square_line[0]
    for zz in range(1, s.chips):
        acc = acc + square_line[zz]
    norm_out[...] = jnp.sqrt(acc + chan_squares)
    taken(byte_count(), g_sem.at[1])
    pltpu.make_async_copy(final.at[c], grad_out.at[:, own_rows, own_cols], g_sem.at[2]).wait()

    gone(weights.at[:, pl.ds(0, sent_rows), :], w_send.at[0])
    if s.split:
        gone(weights.at[:, pl.ds(0, plane_rows), :], w_send.at[1])
    gone(pack_all.at[pl.ds(0, s.mp - 1)], p_sem.at[0])
    for q in range(s.group):
        gone(grids.at[q, 1, pl.ds(0, (2 * s.chips - 1) * s.ch), middle], f_send.at[q])
        gone(proj_all.at[q, pl.ds(0, 2 * s.dp - 1)], j_send.at[q])
    gone(small_plane.at[pl.ds(0, 2 * s.dp - 1)], sp_sem.at[0])
    gone(share_in.at[pl.ds(0, s.dp - 1)], r_send.at[0])
    gone(small_line.at[pl.ds(0, s.chips - 1)], sl_sem.at[0])
    gone(line_in.at[pl.ds(1, s.chips - 1)], l_send.at[0])
    gone(wide_in.at[pl.ds(1, s.chips - 1)], l_send.at[1])
    gone(narrow_in.at[pl.ds(0, s.dp - 1)], r_send.at[1])
    gone(byte_count(), g_sem.at[0])
    gone(square_near.at[pl.ds(0, 2 * s.dp - 1)], q_sem.at[0])
    gone(square_line.at[pl.ds(0, s.chips - 1)], q_sem.at[2])

    @pl.when(d > 0)
    def _():
        for q in range(s.group):
            halo_up(q).wait_send()

    @pl.when(d < s.dp - 1)
    def _():
        for q in range(s.group):
            halo_down(q).wait_send()


def run_kernel(s, *operands):
    vm, dma = pltpu.VMEM, pltpu.SemaphoreType.DMA
    rest = TAPS - s.first
    scratch = [
        vm((s.ch, s.images, s.px), BF16),
        vm((s.ch, s.images, LANES), F32),
        vm((s.blocks, s.ch * s.images, LANES), F32),
        vm((s.images, s.ch, s.px), BF16),
        vm((s.group, 3, s.width, s.ext), BF16),
        vm((TAPS, s.ch, s.width), F32),
        vm((TAPS, s.ch, s.width), BF16),
        vm((TAPS, s.width, s.half), BF16),
        vm((s.half, TAPS * s.width), BF16),
        vm((s.width, s.half), F32),
        vm((s.chips, 16, LANES), F32),
        vm((s.mp, 16, LANES), F32),
        vm((s.width, 16), F32),
        vm((3, s.ch), BF16),
        vm((2, 8, s.half), F32),
        vm((16, s.half), F32),
        vm((s.group, s.half, LANES), F32),
        vm((2, s.half, LANES), F32),
        vm((3, s.images, s.px), BF16),
        vm((s.images, s.px), BF16),
        vm((s.images, s.px), jnp.int32),
        vm((4, s.images, s.px), F32),
        vm((s.group, 16, s.px), F32),
        vm((s.group, 16, s.px), BF16),
        vm((s.group, 2, s.width // 2, LANES), BF16),
        vm((s.group, 2, s.width // 2, LANES), BF16),
        vm((s.group, s.half, s.px), F32),
        vm((s.group, s.half, s.px), F32),
        vm((s.group, 2 * s.dp, 8, s.half), F32),
        vm((2, 2, 8, s.half), F32),
        vm((16, s.half), F32),
        vm((8, s.half), F32),
        vm((1, s.half), F32),
        vm((2, s.half, LANES), F32),
        vm((2, s.half, s.px), BF16),
        vm((TAPS, s.width, s.half), F32),
        vm((s.first, s.mp, s.ch, s.half), BF16),
        vm((s.dp, s.first, s.mp, s.rows, s.half), BF16),
        vm((s.chips, s.first, 2, s.rows, s.half), BF16),
        vm((s.chips, s.first, 2, s.rows, s.half), BF16),
        vm((rest, s.mp, s.ch, s.half), BF16),
        vm((s.chips, rest, 2, s.ch, s.half), BF16),
        vm((rest, 2, s.ch, s.half), BF16),
        vm((s.dp, rest, 2, s.rows, s.half), BF16),
        vm((2, TAPS, s.rows, s.half), BF16),
        vm((16, s.half), F32),
        vm((2 * s.dp, 16, s.half), F32),
        vm((2, 16, s.half), F32),
        vm((s.chips, 2, 16, s.half), F32),
        vm((2, 16, s.half), F32),
        vm((2 * s.dp, 8, LANES), F32),
        vm((s.chips, 8, LANES), F32),
        dma((5,)),
        dma((2,)),
        dma((len(s.bits) + 2,)),
        dma((2,)),
        dma((s.group,)),
        dma((s.group, 2)),
        dma((1,)),
        dma((s.group, 2)),
        dma((s.group, 2)),
        dma((s.group,)),
        dma((s.group,)),
        dma((2,)),
        dma((s.first,)),
        dma((2,)),
        dma((s.first,)),
        dma((rest,)),
        dma((rest,)),
        dma((3,)),
        dma((2,)),
        dma((2,)),
        dma((4,)),
    ]
    flops = 2 * 2 * s.group * s.px * s.half * s.width * TAPS
    here, there = pl.BlockSpec(memory_space=pltpu.VMEM), pl.BlockSpec(memory_space=pl.ANY)
    return pl.pallas_call(
        functools.partial(kernel, s),
        out_shape=(
            jax.ShapeDtypeStruct((TAPS, s.ch, s.width), BF16),
            jax.ShapeDtypeStruct((16, LANES), F32),
            jax.ShapeDtypeStruct((8, LANES), F32),
        ),
        in_specs=[there, here, there, here, here, there, there, there, pl.BlockSpec(memory_space=pltpu.SMEM)],
        out_specs=[here] * 3,
        scratch_shapes=scratch,
        compiler_params=pltpu.CompilerParams(
            collective_id=0, has_side_effects=True, vmem_limit_bytes=62 * 2**20
        ),
        cost_estimate=pl.CostEstimate(flops=flops, bytes_accessed=2**23, transcendentals=2**20),
        name="synthesis_step",
    )(*operands)


def adam_update(weight, moment, second, gradient, factor):
    clipped = gradient * factor
    moment_new = BETA_FIRST * moment + (1.0 - BETA_FIRST) * clipped
    second_new = BETA_SECOND * second + (1.0 - BETA_SECOND) * clipped * clipped
    moment_hat = moment_new / (1.0 - BETA_FIRST**STEP)
    second_hat = second_new / (1.0 - BETA_SECOND**STEP)
    weight_new = weight - LEARN_RATE * (
        moment_hat / (jnp.sqrt(second_hat) + ADAM_EPSILON) + DECAY_RATE * weight
    )
    return (moment_new, second_new, weight_new)


def adam_kernel(
    s,
    grad_hbm,
    sums,
    norm,
    conv_w_hbm,
    conv_m_hbm,
    conv_v_hbm,
    chan_w,
    chan_m,
    chan_v,
    rgb_w,
    rgb_m,
    rgb_v,
    loss_out,
    norm_out,
    conv_m_out,
    conv_v_out,
    conv_w_out,
    conv_low_out,
    chan_m_out,
    chan_v_out,
    chan_w_out,
    rgb_m_out,
    rgb_v_out,
    rgb_w_out,
    rgb_low_out,
    grad,
    conv_w,
    conv_m,
    conv_v,
    conv_low,
    get_sem,
    put_sem,
):
    def cut(part):
        return pl.ds(part * s.part, s.part)

    def get(part):
        pairs = ((grad_hbm, grad), (conv_w_hbm, conv_w), (conv_m_hbm, conv_m), (conv_v_hbm, conv_v))
        return [
            pltpu.make_async_copy(src.at[cut(part)], dst.at[cut(part)], get_sem.at[part, j])
            for j, (src, dst) in enumerate(pairs)
        ]

    def put(part):
        pairs = ((conv_m, conv_m_out), (conv_v, conv_v_out), (conv_w, conv_w_out), (conv_low, conv_low_out))
        return [
            pltpu.make_async_copy(src.at[cut(part)], dst.at[cut(part)], put_sem.at[part, j])
            for j, (src, dst) in enumerate(pairs)
        ]

    parts = TAPS // s.part
    for part in range(parts):
        for cp in get(part):
            cp.start()
    factor = jnp.minimum(1.0, CLIP_LIMIT / (norm[0:1, 0:1] + 1e-06))
    loss_out[0] = sums[2, 0]
    norm_out[0] = norm[0, 0]
    moment, second, weight = adam_update(chan_w[...], chan_m[...], chan_v[...], sums[0:2, : s.ch], factor)
    chan_m_out[...] = moment
    chan_v_out[...] = second
    chan_w_out[...] = weight
    moment, second, weight = adam_update(rgb_w[...], rgb_m[...], rgb_v[...], sums[8:11, : s.ch], factor)
    rgb_m_out[...] = moment
    rgb_v_out[...] = second
    rgb_w_out[...] = weight
    rgb_low_out[...] = weight.astype(BF16)
    for part in range(parts):
        for cp in get(part):
            cp.wait()
        for k in range(part * s.part, (part + 1) * s.part):
            moment, second, weight = adam_update(conv_w[k], conv_m[k], conv_v[k], grad[k].astype(F32), factor)
            conv_m[k] = moment
            conv_v[k] = second
            conv_w[k] = weight
            conv_low[k] = weight.astype(BF16)
        for cp in put(part):
            cp.start()
    for part in range(parts):
        for cp in put(part):
            cp.wait()


def run_adam(s, *operands):
    here, there = pl.BlockSpec(memory_space=pltpu.VMEM), pl.BlockSpec(memory_space=pl.ANY)
    scalar = pl.BlockSpec(memory_space=pltpu.SMEM)
    conv = jax.ShapeDtypeStruct((TAPS, s.ch, s.width), F32)
    chan = jax.ShapeDtypeStruct((2, s.ch), F32)
    rgb = jax.ShapeDtypeStruct((3, s.ch), F32)
    one = jax.ShapeDtypeStruct((1,), F32)
    parts = TAPS // s.part
    return pl.pallas_call(
        functools.partial(adam_kernel, s),
        out_shape=(one, one)
        + (conv,) * 3
        + (jax.ShapeDtypeStruct(conv.shape, BF16),)
        + (chan,) * 3
        + (rgb,) * 3
        + (jax.ShapeDtypeStruct(rgb.shape, BF16),),
        in_specs=[there, here, here] + [there] * 3 + [here] * 6,
        out_specs=[scalar, scalar] + [there] * 4 + [here] * 7,
        scratch_shapes=[
            pltpu.VMEM(conv.shape, BF16),
            pltpu.VMEM(conv.shape, F32),
            pltpu.VMEM(conv.shape, F32),
            pltpu.VMEM(conv.shape, F32),
            pltpu.VMEM(conv.shape, BF16),
            pltpu.SemaphoreType.DMA((parts, 4)),
            pltpu.SemaphoreType.DMA((parts, 4)),
        ],
        compiler_params=pltpu.CompilerParams(vmem_limit_bytes=62 * 2**20),
        name="optimizer_step",
    )(*operands)


def local(
    mesh_shape,
    features,
    styles,
    noise_field,
    noise_keep,
    path_noise,
    length_mean,
    conv_weight,
    conv_moment,
    conv_second,
    chan_params,
    chan_moment,
    chan_second,
    rgb_weight,
    rgb_moment,
    rgb_second,
):
    s = Sizes(mesh_shape, features.shape, conv_weight.shape)
    taps_first = functools.partial(jnp.transpose, axes=(1, 0, 2))
    weight = taps_first(conv_weight)
    grad, sums, norm = run_kernel(
        s,
        features,
        styles,
        weight,
        chan_params,
        rgb_weight,
        path_noise,
        noise_field,
        noise_keep,
        length_mean,
    )
    outs = run_adam(
        s,
        grad,
        sums,
        norm,
        weight,
        taps_first(conv_moment),
        taps_first(conv_second),
        chan_params,
        chan_moment,
        chan_second,
        rgb_weight,
        rgb_moment,
        rgb_second,
    )
    return outs[:2] + tuple(taps_first(x) for x in outs[2:6]) + outs[6:]


def solution(mesh):
    whole, line = P(), P("mp", None, None)
    row, pixels = P(None, "mp"), P(None, "dp")
    in_specs = (
        P("mp", None, "dp"),
        row,
        pixels,
        pixels,
        P(None, None, "dp"),
        whole,
        line,
        line,
        line,
    ) + (row,) * 6
    out_specs = (whole, whole) + (line,) * 4 + (row,) * 7
    return jax.shard_map(
        functools.partial(local, dict(mesh.shape)),
        mesh=mesh,
        in_specs=in_specs,
        out_specs=out_specs,
        check_vma=False,
    )
```

```python
import functools
import math

import jax
import jax.numpy as jnp
from jax import lax
from jax.experimental import pallas as pl
from jax.experimental.pallas import tpu as pltpu
from jax.sharding import PartitionSpec as P

SIDE = 64
STEP = 5
TAPS = 9
LANES = 128

CLIP_LIMIT = 0.1
LEARN_RATE = 0.3
DECAY_RATE = 0.01
BETA_FIRST = 0.5
BETA_SECOND = 0.5
ADAM_EPSILON = 1e-08
DEMOD_EPSILON = 1e-08
HIGHEST = lax.Precision.HIGHEST
MESH = pl.DeviceIdType.MESH
F32 = jnp.float32
BF16 = jnp.bfloat16
NT = (((1,), (1,)), ((), ()))


class Sizes:
    def __init__(self, mesh_shape, features, conv_weight):
        self.dp = mesh_shape["dp"]
        self.mp = mesh_shape["mp"]
        self.chips = self.mp // 2
        self.ch, self.images, self.px = features
        self.width = conv_weight[2]
        self.half = self.width // 2
        self.group = self.images // self.chips
        self.blocks = self.px // LANES
        self.ext = self.px + 2 * LANES
        self.split = (self.ch // self.dp) % 16 == 0
        self.shares = self.dp if self.split else 1
        self.rows = self.ch // self.shares
        self.first = 7
        self.part = 3
        self.bits = []
        bit = self.chips // 2
        while bit >= 1:
            self.bits.append(bit)
            bit //= 2


def flip(value, bit):
    return value + bit - 2 * bit * lax.rem(lax.div(value, bit), 2)


def swap_halves(x):
    return pltpu.roll(x, SIDE, x.ndim - 1)


def kernel(
    s,
    feat_hbm,
    small,
    weight_hbm,
    pixels_hbm,
    mean,
    grad_out,
    small_out,
    norm_out,
    feat,
    style_cols,
    turned,
    outbox,
    grids,
    weight_own,
    weight_low,
    weights,
    weights_t,
    weight_sq,
    pack,
    pack_all,
    columns,
    rgb_low,
    rgb_rows,
    demod_rows,
    demod_cols,
    chan_cols,
    pixels,
    pixel_rows,
    aux_rows,
    aux,
    halo_out,
    halo_in,
    scaled,
    slope_of,
    proj_all,
    half_pick,
    stat_rows,
    rgb_acc,
    loss_acc,
    chan_acc,
    grad_conv,
    total,
    share_out,
    share_in,
    line_out,
    line_in,
    wide_out,
    wide_in,
    wide_sum,
    narrow_in,
    final,
    small_own,
    small_plane,
    small_mid,
    small_line,
    small_sum,
    square_near,
    square_line,
    in_sem,
    w_send,
    w_recv,
    p_sem,
    f_send,
    f_recv,
    f_local,
    h_send,
    h_recv,
    j_send,
    j_recv,
    r_send,
    r_recv,
    l_send,
    l_recv,
    b_recv,
    n_recv,
    g_sem,
    sp_sem,
    sl_sem,
    q_sem,
):
    d = lax.axis_index("dp")
    m = lax.axis_index("mp")
    z = lax.div(m, 2)
    c = lax.rem(m, 2)
    other = 1 - c
    mate = 2 * z + other
    conv_gain = 1.0 / math.sqrt(TAPS * s.width)
    rgb_gain = 1.0 / math.sqrt(s.width)
    last = s.group - 1

    def copy_to(src, dst, send, recv, dd, mm):
        return pltpu.make_async_remote_copy(
            src_ref=src, dst_ref=dst, send_sem=send, recv_sem=recv, device_id=(dd, mm), device_id_type=MESH
        )

    def taken(ref, sem):
        copy_to(ref, ref, sem, sem, d, mate).wait_recv()

    def gone(ref, sem):
        copy_to(ref, ref, sem, sem, d, mate).wait_send()

    def z_at(r):
        return lax.rem(z + r, s.chips)

    def d_at(r):
        return lax.rem(d + r, s.dp)

    line = [(d, lax.rem(m + r, s.mp)) for r in range(1, s.mp)]
    plane = [(d_at(r), mm) for r in range(1, s.dp) for mm in (m, mate)]
    near = plane + [(d, mate)]
    place = 2 * d + c

    get_weight = pltpu.make_async_copy(weight_hbm, weight_own, in_sem.at[0])
    get_feat = pltpu.make_async_copy(feat_hbm, feat, in_sem.at[1])
    get_pixels = pltpu.make_async_copy(pixels_hbm, pixels, in_sem.at[2])
    styles = small.at[: s.images]
    chan = small.at[s.images : s.images + 2]
    rgb = small.at[s.images + 2 : s.images + 5]
    get_weight.start()
    get_feat.start()
    get_pixels.start()
    halo_in[...] = jnp.zeros_like(halo_in)
    barrier = pltpu.get_barrier_semaphore()
    for dd, mm in line + plane:
        pl.semaphore_signal(barrier, inc=1, device_id=(dd, mm), device_id_type=MESH)
    pack[...] = jnp.zeros_like(pack)
    rgb_low[...] = rgb[...].astype(BF16)
    rgb_eff = rgb_low[...].astype(F32) * rgb_gain
    for zz in range(s.chips):
        pack[zz, : s.group, : s.ch] = styles[zz * s.group : (zz + 1) * s.group, :]
        pack[zz, s.group : s.group + 2, : s.ch] = chan[...]
        pack[zz, 8:11, : s.ch] = rgb_eff
    pack_all[m] = pack[z]
    for i in range(s.ch):
        style_cols[i] = jnp.broadcast_to(styles[:, i : i + 1], (s.images, LANES))

    get_weight.wait()
    for k in range(TAPS):
        weight_low[k] = weight_own[k].astype(BF16)
    pl.semaphore_wait(barrier, len(line) + len(plane))

    share = d if s.split else 0

    def piece(m_of):
        return weights.at[:, pl.ds(pl.multiple_of(m_of * s.ch + share * s.rows, 16), s.rows), :]

    def own_piece(half_of):
        return weight_low.at[
            :,
            pl.ds(pl.multiple_of(share * s.rows, 16), s.rows),
            pl.ds(pl.multiple_of(half_of * s.half, LANES), s.half),
        ]

    sent_rows = 0
    for index, bit in enumerate(s.bits):
        for cc in range(2):
            copy_to(
                own_piece(cc), piece(m), w_send.at[0], w_recv.at[index], d, 2 * flip(z, bit) + cc
            ).start()
            sent_rows += s.rows
    copy_to(
        weight_low.at[:, :, pl.ds(pl.multiple_of(other * s.half, LANES), s.half)],
        weights.at[:, pl.ds(pl.multiple_of(m * s.ch, 16), s.ch), :],
        w_send.at[0],
        w_recv.at[len(s.bits)],
        d,
        mate,
    ).start()
    sent_rows += s.ch
    for dd, mm in line:
        copy_to(pack.at[lax.div(mm, 2)], pack_all.at[m], p_sem.at[0], p_sem.at[1], dd, mm).start()

    get_feat.wait()
    lane = lax.broadcasted_iota(jnp.int32, (1, 1, LANES), 2)
    low_lanes = lane < SIDE
    step = 8

    def modulate(index, carry):
        rows = pl.ds(pl.multiple_of(index * step, step), step)
        factor = style_cols[rows]
        for q in range(s.blocks // 2):
            first = feat[rows, :, q * LANES : (q + 1) * LANES].astype(F32) * factor
            q2 = q + s.blocks // 2
            second = feat[rows, :, q2 * LANES : (q2 + 1) * LANES].astype(F32) * factor
            even = jnp.where(low_lanes, first, swap_halves(second))
            odd = jnp.where(low_lanes, swap_halves(first), second)
            out_rows = pl.ds(pl.multiple_of(index * step * s.images, step * 8), step * s.images)
            turned[2 * q, out_rows, :] = even.reshape(step * s.images, LANES)
            turned[2 * q + 1, out_rows, :] = odd.reshape(step * s.images, LANES)
        return carry

    lax.fori_loop(0, s.ch // step, modulate, 0)

    def pick(n, carry):
        for j in range(s.blocks):
            part = turned[j, pl.ds(n, s.ch, stride=s.images), :]
            outbox[n, :, j * LANES : (j + 1) * LANES] = part.astype(BF16)
        return carry

    lax.fori_loop(0, s.images, pick, 0)

    middle = pl.ds(LANES, s.px)

    def grid_rows(m_of):
        return pl.ds(pl.multiple_of(m_of * s.ch, 16), s.ch)

    def feature_send(q, r):
        zz = z_at(r)
        return copy_to(
            outbox.at[zz * s.group + q],
            grids.at[q, 1, grid_rows(m), middle],
            f_send.at[q],
            f_recv.at[q, 0],
            d,
            2 * zz + c,
        )

    def start_features():
        for q in range(s.group):
            own = outbox.at[z * s.group + q]
            there = grids.at[q, 1, grid_rows(m), middle]
            pltpu.make_async_copy(own, there, f_local.at[0]).start()
            copy_to(own, there, f_send.at[q], f_recv.at[q, 1], d, mate).start()
            if q < 2:
                for r in range(1, s.chips):
                    feature_send(q, r).start()

    held = [z]
    plane_rows = 0
    for index, bit in enumerate(s.bits):
        peer = flip(z, bit)
        for h in held[1:]:
            for cc in range(2):
                at = piece(2 * h + cc)
                copy_to(at, at, w_send.at[0], w_recv.at[index], d, 2 * peer + c).start()
                sent_rows += s.rows
        if index == len(s.bits) - 1:
            start_features()
        fresh = [flip(h, bit) for h in held]
        taken(weights.at[:, pl.ds(0, 2 * len(fresh) * s.rows), :], w_recv.at[index])
        if s.split:
            for h in fresh:
                for cc in range(2):
                    at = piece(2 * h + cc)
                    for r in range(1, s.dp):
                        copy_to(at, at, w_send.at[1], w_recv.at[len(s.bits) + 1], d_at(r), m).start()
                        plane_rows += s.rows
        held = held + fresh

    weights[:, grid_rows(m), :] = weight_low[:, :, pl.ds(pl.multiple_of(c * s.half, LANES), s.half)]
    get_pixels.wait()
    lane2 = lax.broadcasted_iota(jnp.int32, (1, LANES), 1)
    low2 = lane2 < SIDE
    for k in range(4):
        for q in range(s.blocks // 2):
            q2 = q + s.blocks // 2
            cuts = [slice(q * LANES, (q + 1) * LANES), slice(q2 * LANES, (q2 + 1) * LANES)]
            first, second = [pixels[k, :, cut] for cut in cuts]
            pixel_rows[k, :, 2 * q * LANES : (2 * q + 1) * LANES] = jnp.where(low2, first, swap_halves(second))
            pixel_rows[k, :, (2 * q + 1) * LANES : (2 * q + 2) * LANES] = jnp.where(low2, swap_halves(first), second)
    aux_rows[...] = jnp.zeros_like(aux_rows)
    for q in range(s.group):
        for k in range(4):
            row = pixel_rows[k, pl.ds(z * s.group + q, 1), :]
            aux_rows[q, k : k + 1, :] = row
            if k < 3:
                aux_rows[q, 8 + k : 9 + k, :] = row
        aux[q] = aux_rows[q].astype(BF16)

    taken(pack_all.at[pl.ds(0, s.mp - 1)], p_sem.at[1])
    for mm in range(s.mp):
        columns[mm * s.ch : (mm + 1) * s.ch, :] = pack_all[mm].T[: s.ch, :]
    rows_all = columns[...].T
    for h in range(2):
        rgb_rows[h] = rows_all[8:16, h * s.half : (h + 1) * s.half]
    mine = columns[pl.ds(pl.multiple_of(c * s.half, 8), s.half), :]
    for k in range(2):
        chan_cols[k] = jnp.broadcast_to(mine[:, s.group + k : s.group + k + 1], (s.half, LANES))
    total[...] = jnp.zeros_like(total)
    stat_rows[...] = jnp.zeros_like(stat_rows)
    rgb_acc[...] = jnp.zeros_like(rgb_acc)
    loss_acc[...] = jnp.zeros_like(loss_acc)
    chan_acc[...] = jnp.zeros_like(chan_acc)

    column = lax.rem(lane2, SIDE)
    not_first = column >= 1
    not_last = column <= SIDE - 2
    pair = s.width // 2
    up = lax.rem(d + s.dp - 1, s.dp)
    down = lax.rem(d + 1, s.dp)

    def halo_up(q):
        return copy_to(halo_out.at[q, 0], halo_in.at[q, 1], h_send.at[q, 0], h_recv.at[q, 1], up, m)

    def halo_down(q):
        return copy_to(halo_out.at[q, 1], halo_in.at[q, 0], h_send.at[q, 1], h_recv.at[q, 0], down, m)

    def ends(q):
        return grids[q, 1, :, LANES : 2 * LANES], grids[q, 1, :, s.px : s.px + LANES]

    def take_line(q):
        taken(grids.at[q, 1, pl.ds(0, (s.chips - 1) * s.ch), middle], f_recv.at[q, 0])
        for r in range(1, s.chips):
            at = grids.at[q, 1, grid_rows(2 * z_at(r) + c), middle]
            copy_to(at, at, f_send.at[q], f_recv.at[q, 1], d, mate).start()

        @pl.when(q + 2 < s.group)
        def _():
            for r in range(1, s.chips):
                feature_send(q + 2, r).start()

    def take_mate(q):
        taken(grids.at[q, 1, pl.ds(0, s.chips * s.ch), middle], f_recv.at[q, 1])
        top, end = ends(q)
        halo_out[q, 0] = jnp.where(low2, top[:pair], swap_halves(top[pair:]))
        halo_out[q, 1] = jnp.where(low2, swap_halves(end[:pair]), end[pair:])

        @pl.when(d > 0)
        def _():
            halo_up(q).start()

        @pl.when(d < s.dp - 1)
        def _():
            halo_down(q).start()

    def lateral(q, j):
        x = grids[q, 1, :, j * LANES : (j + 1) * LANES]
        none = jnp.zeros_like(x)
        grids[q, 0, :, j * LANES : (j + 1) * LANES] = jnp.where(not_first, pltpu.roll(x, 1, 1), none)
        grids[q, 2, :, j * LANES : (j + 1) * LANES] = jnp.where(not_last, pltpu.roll(x, LANES - 1, 1), none)

    def inner(q):
        for j in range(1, s.blocks + 1):
            lateral(q, j)

    def border(q):
        @pl.when(d > 0)
        def _():
            halo_down(q).wait_recv()

        @pl.when(d < s.dp - 1)
        def _():
            halo_up(q).wait_recv()

        top, end = ends(q)
        above = halo_in[q, 0]
        below = halo_in[q, 1]
        swapped_end = swap_halves(end)
        swapped_top = swap_halves(top)
        grids[q, 1, :pair, :LANES] = jnp.where(low2, above, swapped_end[:pair])
        grids[q, 1, pair:, :LANES] = jnp.where(low2, swap_halves(above), swapped_end[pair:])
        tail = s.px + LANES
        grids[q, 1, :pair, tail : tail + LANES] = jnp.where(low2, swapped_top[:pair], swap_halves(below))
        grids[q, 1, pair:, tail : tail + LANES] = jnp.where(low2, swapped_top[pair:], below)
        lateral(q, 0)
        lateral(q, s.blocks + 1)

    def blocks_of(ref, first, second):
        if second == first + 1:
            return ref[:, first * LANES : (second + 1) * LANES]
        return jnp.concatenate([ref[:, j * LANES : (j + 1) * LANES] for j in (first, second)], axis=1)

    def convolve(q, first, second):
        acc = jnp.zeros((s.half, 2 * LANES), F32)
        for a in range(3):
            for b in range(3):
                k = 3 * a + b
                acc += jnp.dot(
                    weights_t[:, k * s.width : (k + 1) * s.width],
                    blocks_of(grids.at[q, b], first + a, second + a),
                    preferred_element_type=F32,
                )
        acts = []
        for t, j in enumerate((first, second)):
            cut = slice(j * LANES, (j + 1) * LANES)
            conv = acc[:, t * LANES : (t + 1) * LANES] * conv_gain
            noise = aux[q, :, cut].astype(F32)[3:4]
            pre = conv * demod_cols[q] + chan_cols[1] * noise + chan_cols[0]
            sig = jax.nn.sigmoid(pre)
            act = pre * sig
            scaled[lax.rem(q, 2), :, cut] = conv
            slope_of[lax.rem(q, 2), :, cut] = sig * (1.0 + pre * (1.0 - sig))
            acts.append(act.astype(BF16))
        act = jnp.concatenate(acts, axis=1)
        return lax.dot_general(blocks_of(aux.at[q], first, second), act, NT, preferred_element_type=F32)[:8]

    def convolve_inner(q):
        projected = jnp.zeros((8, s.half), F32)
        for j in range(1, s.blocks - 1, 2):
            projected += convolve(q, j, j + 1)
        proj_all[q, place] = projected

    def convolve_border(q):
        proj_all[q, place] += convolve(q, 0, s.blocks - 1)
        for dd, mm in near:
            at = proj_all.at[q, place]
            copy_to(at, at, j_send.at[q], j_recv.at[q], dd, mm).start()

    def signal_back(q):
        taken(proj_all.at[q, pl.ds(0, 2 * s.dp - 1)], j_recv.at[q])
        signal_math(q)

    def signal_math(q):
        halves = []
        for h in range(2):
            acc = proj_all[q, h]
            for dd in range(1, s.dp):
                acc = acc + proj_all[q, 2 * dd + h]
            halves.append(acc)
        slopes = [jnp.sum(rgb_rows[h] * halves[h], axis=0, keepdims=True) for h in range(2)]
        row = lax.broadcasted_iota(jnp.int32, (8, s.half), 0)
        length_sq = jnp.sum(slopes[0] * slopes[0] + slopes[1] * slopes[1], axis=1, keepdims=True)
        length = jnp.sqrt(length_sq + 1e-08)
        excess = length - mean[0]
        loss_acc[...] += jnp.broadcast_to(excess * excess, (1, s.half))
        scale = 2.0 * excess / length
        for h in range(2):
            grad = scale * slopes[h]
            half_pick[h, 0] = grad * rgb_rows[h]
            half_pick[h, 1] = jnp.where(row < 3, grad * halves[h] * rgb_gain, 0.0)
        rgb_acc[...] += half_pick[c, 1]
        coef = half_pick[c, 0]
        high = coef.astype(BF16).astype(F32)
        coef_t = jnp.concatenate([high, coef - high], axis=0).T.astype(BF16)
        wide = 2 * LANES
        bias_part = chan_acc[0]
        strength_part = chan_acc[1]
        stat_part = jnp.zeros((s.half, LANES), F32)
        back = demod_cols[q] * conv_gain
        for p in range(0, s.px, wide):
            act_grad = jnp.dot(coef_t, aux[q, :, p : p + wide], preferred_element_type=F32)
            for t in range(2):
                cut = slice(p + t * LANES, p + (t + 1) * LANES)
                noise = aux[q, :, cut].astype(F32)[3:4]
                grad = act_grad[:, t * LANES : (t + 1) * LANES] * slope_of[lax.rem(q, 2), :, cut]
                bias_part = bias_part + grad
                strength_part = strength_part + grad * noise
                stat_part = stat_part + grad * scaled[lax.rem(q, 2), :, cut]
                grad_conv[lax.rem(q, 2), :, cut] = (grad * back).astype(BF16)
        chan_acc[0] = bias_part
        chan_acc[1] = strength_part
        stat = jnp.sum(stat_part.T, axis=0, keepdims=True)
        dem = demod_rows[pl.ds(q, 1), :]
        stat_rows[pl.ds(q, 1), :] = stat * (dem * dem * dem) * (-0.5 * conv_gain * conv_gain)

    def tap_grad(q, k):
        a, b = k // 3, k % 3
        return lax.dot_general(
            grids[q, b, :, a * LANES : a * LANES + s.px], grad_conv[lax.rem(q, 2)], NT, preferred_element_type=F32
        )

    pltpu.make_async_copy(
        grids.at[0, 1, pl.ds(0, s.group * s.ch), middle],
        grids.at[0, 1, pl.ds(0, s.group * s.ch), middle],
        f_local.at[0],
    ).wait()
    take_line(0)
    take_mate(0)
    inner(0)

    taken(weights.at[:, pl.ds(0, s.ch), :], w_recv.at[len(s.bits)])
    if s.split:
        taken(weights.at[:, pl.ds(0, plane_rows), :], w_recv.at[len(s.bits) + 1])
    square = jnp.zeros((s.width, s.half), F32)
    for k in range(TAPS):
        w = weights[k]
        weights_t[:, k * s.width : (k + 1) * s.width] = w.T
        wf = w.astype(F32)
        square = square + wf * wf
    weight_sq[...] = square
    demod_sq = jnp.dot(rows_all * rows_all, weight_sq[...], precision=HIGHEST, preferred_element_type=F32)
    demod = lax.rsqrt(conv_gain * conv_gain * demod_sq + DEMOD_EPSILON)
    demod_rows[...] = demod
    demod_t = demod.T
    for q in range(s.group):
        demod_cols[q] = jnp.broadcast_to(demod_t[:, q : q + 1], (s.half, LANES))

    def add_taps(q):
        def three(a, carry):
            rows = pl.ds(pl.multiple_of(a * LANES, LANES), s.px)
            for b in range(3):
                total[3 * a + b] += lax.dot_general(
                    grids[q, b, :, rows], grad_conv[lax.rem(q, 2)], NT, preferred_element_type=F32
                )
            return carry

        lax.fori_loop(0, 3, three, 0)

    def stage(q, carry):
        border(q)
        convolve_border(q)

        @pl.when(q == last - 1)
        def _():
            if last > 1:
                add_taps(q - 1)
            signal_back(q)

        take_line(q + 1)

        @pl.when(lax.rem(q, last - 1) > 0)
        def _():
            add_taps(q - 1)

        take_mate(q + 1)
        inner(q + 1)
        convolve_inner(q + 1)

        @pl.when(q < last - 1)
        def _():
            signal_back(q)

        return carry

    convolve_inner(0)
    lax.fori_loop(0, last, stage, 0)

    border(last)
    convolve_border(last)
    add_taps(last - 1)
    signal_back(last)
    cross = 2.0 * jnp.dot(
        columns[...] * columns[...], stat_rows[...], precision=HIGHEST, preferred_element_type=F32
    )
    weight_sq[...] = cross

    def share_rows(share_of):
        return pl.ds(pl.multiple_of(share_of * s.rows, 16), s.rows)

    own_rows = share_rows(share)
    own_cols = pl.ds(pl.multiple_of(c * s.half, LANES), s.half)
    targets = near if s.split else [(d, mate)]

    def last_tap(k):
        grad = total[k] + tap_grad(last, k) + weights[k].astype(F32) * weight_sq[...]
        grad = grad.astype(BF16).reshape(s.mp, s.ch, s.half)
        if k < s.first:
            share_out[k] = grad
            for r in range(1, s.dp):
                part = share_out.at[k, :, share_rows(d_at(r) if s.split else 0), :]
                copy_to(part, share_in.at[d, k], r_send.at[0], r_recv.at[k], d_at(r), m).start()
        else:
            b = k - s.first
            wide_out[b] = grad
            for r in range(1, s.chips):
                part = wide_out.at[b, pl.ds(2 * z_at(r), 2)]
                copy_to(part, wide_in.at[r, b], l_send.at[1], b_recv.at[b], d, 2 * z_at(r) + c).start()

    def by_shares(own, parts):
        acc = None
        for dd in range(s.dp):
            term = jnp.where(d == dd, own, parts[dd].astype(F32))
            acc = term if acc is None else acc + term
        return acc

    def plane_done(k):
        taken(share_in.at[pl.ds(0, s.dp - 1), k], r_recv.at[k])
        acc = by_shares(share_out[k, :, own_rows, :].astype(F32), [share_in[dd, k] for dd in range(s.dp)])
        line_out[:, k] = acc.astype(BF16).reshape(s.chips, 2, s.rows, s.half)
        for r in range(1, s.chips):
            copy_to(
                line_out.at[z_at(r), k], line_in.at[r, k], l_send.at[0], l_recv.at[k], d, 2 * z_at(r) + c
            ).start()

    def line_done(b):
        taken(wide_in.at[pl.ds(1, s.chips - 1), b], b_recv.at[b])
        acc = wide_out[b, pl.ds(2 * z, 2)].astype(F32)
        for r in range(1, s.chips):
            acc = acc + wide_in[r, b].astype(F32)
        wide_sum[b] = acc.astype(BF16)
        for r in range(1, s.dp):
            part = wide_sum.at[b, :, share_rows(d_at(r) if s.split else 0), :]
            copy_to(part, narrow_in.at[d, b], r_send.at[1], n_recv.at[b], d_at(r), m).start()

    def byte_count():
        return weights.at[:, pl.ds(0, len(targets) * s.rows), :]

    def finish(k, squares):
        if k < s.first:
            taken(line_in.at[pl.ds(1, s.chips - 1), k], l_recv.at[k])
            acc = line_out[z, k].astype(F32)
            for r in range(1, s.chips):
                acc = acc + line_in[r, k].astype(F32)
        else:
            b = k - s.first
            taken(narrow_in.at[pl.ds(0, s.dp - 1), b], n_recv.at[b])
            acc = by_shares(wide_sum[b, :, own_rows, :].astype(F32), [narrow_in[dd, b] for dd in range(s.dp)])
        final[:, k] = acc.astype(BF16)
        kept = final[:, k].astype(F32)
        return squares + jnp.sum(kept * kept, axis=0)

    def hand_out(first_tap, count):
        taps = pl.ds(first_tap, count)
        there = grad_out.at[taps, own_rows, own_cols]
        for dd, mm in targets:
            copy_to(final.at[lax.rem(mm, 2), taps], there, g_sem.at[0], g_sem.at[1], dd, mm).start()
        pltpu.make_async_copy(final.at[c, taps], there, g_sem.at[2]).start()

    def send_small():
        small_own[0:1] = jnp.sum(chan_acc[0].T, axis=0, keepdims=True)
        small_own[1:2] = jnp.sum(chan_acc[1].T, axis=0, keepdims=True)
        small_own[2:3] = loss_acc[...]
        small_own[3:8] = jnp.zeros((5, s.half), F32)
        small_own[8:16] = rgb_acc[...]
        small_plane[place] = small_own[...]
        for dd, mm in near:
            copy_to(small_own, small_plane.at[place], sp_sem.at[0], sp_sem.at[1], dd, mm).start()

    for index, k in enumerate((0, 7, 1, 2, 3, 8, 4, 5, 6)):
        last_tap(k)
        if index == 1:
            send_small()

    taken(small_plane.at[pl.ds(0, 2 * s.dp - 1)], sp_sem.at[1])
    for h in range(2):
        acc = small_plane[h, 0:8]
        for dd in range(1, s.dp):
            acc = acc + small_plane[2 * dd + h, 0:8]
        row = lax.broadcasted_iota(jnp.int32, (8, s.half), 0)
        small_mid[h, 0:8] = jnp.where(row < 2, acc, small_plane[h, 0:8])
        small_mid[h, 8:16] = small_plane[h, 8:16]
    small_line[z] = small_mid[...]
    for r in range(1, s.chips):
        copy_to(small_mid, small_line.at[z], sl_sem.at[0], sl_sem.at[1], d, 2 * z_at(r) + c).start()

    squares = jnp.zeros((s.rows, s.half), F32)
    plane_done(0)
    plane_done(1)
    line_done(0)
    plane_done(2)
    plane_done(3)
    line_done(1)
    plane_done(4)
    for k in (0, 1, 2):
        squares = finish(k, squares)
    hand_out(0, 3)
    plane_done(5)
    plane_done(6)
    for k in (7, 8, 3, 4, 5, 6):
        squares = finish(k, squares)
    square_near[place] = jnp.broadcast_to(jnp.sum(squares, keepdims=True), (8, LANES))
    for dd, mm in near:
        at = square_near.at[place]
        copy_to(at, at, q_sem.at[0], q_sem.at[1], dd, mm).start()
    hand_out(3, TAPS - 3)
    taken(small_line.at[pl.ds(0, s.chips - 1)], sl_sem.at[1])
    sums = small_line[0]
    for zz in range(1, s.chips):
        sums = sums + small_line[zz]
    small_sum[...] = sums
    chan_squares = jnp.sum(sums[:, 0:2] * sums[:, 0:2]) + jnp.sum(sums[:, 8:16] * sums[:, 8:16])
    start = m * s.ch
    first = lax.rem(start, s.half)
    block = pl.multiple_of(lax.div(first, LANES) * LANES, LANES)
    mine = small_sum[lax.div(start, s.half), :, pl.ds(block, LANES)]
    small_out[...] = pltpu.roll(mine, lax.rem(2 * LANES - lax.rem(first, LANES), LANES), 1)

    taken(square_near.at[pl.ds(0, 2 * s.dp - 1)], q_sem.at[1])
    acc = square_near[0]
    for at in range(1, 2 * s.shares):
        acc = acc + square_near[at]
    square_line[z] = acc
    for r in range(1, s.chips):
        at = square_line.at[z]
        copy_to(at, at, q_sem.at[2], q_sem.at[3], d, 2 * z_at(r) + c).start()
    taken(square_line.at[pl.ds(0, s.chips - 1)], q_sem.at[3])
    acc = square_line[0]
    for zz in range(1, s.chips):
        acc = acc + square_line[zz]
    norm_out[...] = jnp.sqrt(acc + chan_squares)
    taken(byte_count(), g_sem.at[1])
    pltpu.make_async_copy(final.at[c], grad_out.at[:, own_rows, own_cols], g_sem.at[2]).wait()

    gone(weights.at[:, pl.ds(0, sent_rows), :], w_send.at[0])
    if s.split:
        gone(weights.at[:, pl.ds(0, plane_rows), :], w_send.at[1])
    gone(pack_all.at[pl.ds(0, s.mp - 1)], p_sem.at[0])
    for q in range(s.group):
        gone(grids.at[q, 1, pl.ds(0, (2 * s.chips - 1) * s.ch), middle], f_send.at[q])
        gone(proj_all.at[q, pl.ds(0, 2 * s.dp - 1)], j_send.at[q])
    gone(small_plane.at[pl.ds(0, 2 * s.dp - 1)], sp_sem.at[0])
    gone(share_in.at[pl.ds(0, s.dp - 1)], r_send.at[0])
    gone(small_line.at[pl.ds(0, s.chips - 1)], sl_sem.at[0])
    gone(line_in.at[pl.ds(1, s.chips - 1)], l_send.at[0])
    gone(wide_in.at[pl.ds(1, s.chips - 1)], l_send.at[1])
    gone(narrow_in.at[pl.ds(0, s.dp - 1)], r_send.at[1])
    gone(byte_count(), g_sem.at[0])
    gone(square_near.at[pl.ds(0, 2 * s.dp - 1)], q_sem.at[0])
    gone(square_line.at[pl.ds(0, s.chips - 1)], q_sem.at[2])

    @pl.when(d > 0)
    def _():
        for q in range(s.group):
            halo_up(q).wait_send()

    @pl.when(d < s.dp - 1)
    def _():
        for q in range(s.group):
            halo_down(q).wait_send()


def run_kernel(s, *operands):
    vm, dma = pltpu.VMEM, pltpu.SemaphoreType.DMA
    rest = TAPS - s.first
    scratch = [
        vm((s.ch, s.images, s.px), BF16),
        vm((s.ch, s.images, LANES), F32),
        vm((s.blocks, s.ch * s.images, LANES), F32),
        vm((s.images, s.ch, s.px), BF16),
        vm((s.group, 3, s.width, s.ext), BF16),
        vm((TAPS, s.ch, s.width), F32),
        vm((TAPS, s.ch, s.width), BF16),
        vm((TAPS, s.width, s.half), BF16),
        vm((s.half, TAPS * s.width), BF16),
        vm((s.width, s.half), F32),
        vm((s.chips, 16, LANES), F32),
        vm((s.mp, 16, LANES), F32),
        vm((s.width, 16), F32),
        vm((3, s.ch), BF16),
        vm((2, 8, s.half), F32),
        vm((16, s.half), F32),
        vm((s.group, s.half, LANES), F32),
        vm((2, s.half, LANES), F32),
        vm((4, s.images, s.px), F32),
        vm((4, s.images, s.px), F32),
        vm((s.group, 16, s.px), F32),
        vm((s.group, 16, s.px), BF16),
        vm((s.group, 2, s.width // 2, LANES), BF16),
        vm((s.group, 2, s.width // 2, LANES), BF16),
        vm((2, s.half, s.px), F32),
        vm((2, s.half, s.px), F32),
        vm((s.group, 2 * s.dp, 8, s.half), F32),
        vm((2, 2, 8, s.half), F32),
        vm((16, s.half), F32),
        vm((8, s.half), F32),
        vm((1, s.half), F32),
        vm((2, s.half, LANES), F32),
        vm((2, s.half, s.px), BF16),
        vm((TAPS, s.width, s.half), F32),
        vm((s.first, s.mp, s.ch, s.half), BF16),
        vm((s.dp, s.first, s.mp, s.rows, s.half), BF16),
        vm((s.chips, s.first, 2, s.rows, s.half), BF16),
        vm((s.chips, s.first, 2, s.rows, s.half), BF16),
        vm((rest, s.mp, s.ch, s.half), BF16),
        vm((s.chips, rest, 2, s.ch, s.half), BF16),
        vm((rest, 2, s.ch, s.half), BF16),
        vm((s.dp, rest, 2, s.rows, s.half), BF16),
        vm((2, TAPS, s.rows, s.half), BF16),
        vm((16, s.half), F32),
        vm((2 * s.dp, 16, s.half), F32),
        vm((2, 16, s.half), F32),
        vm((s.chips, 2, 16, s.half), F32),
        vm((2, 16, s.half), F32),
        vm((2 * s.dp, 8, LANES), F32),
        vm((s.chips, 8, LANES), F32),
        dma((3,)),
        dma((2,)),
        dma((len(s.bits) + 2,)),
        dma((2,)),
        dma((s.group,)),
        dma((s.group, 2)),
        dma((1,)),
        dma((s.group, 2)),
        dma((s.group, 2)),
        dma((s.group,)),
        dma((s.group,)),
        dma((2,)),
        dma((s.first,)),
        dma((2,)),
        dma((s.first,)),
        dma((rest,)),
        dma((rest,)),
        dma((3,)),
        dma((2,)),
        dma((2,)),
        dma((4,)),
    ]
    flops = 2 * 2 * s.group * s.px * s.half * s.width * TAPS
    here, there = pl.BlockSpec(memory_space=pltpu.VMEM), pl.BlockSpec(memory_space=pl.ANY)
    return pl.pallas_call(
        functools.partial(kernel, s),
        out_shape=(
            jax.ShapeDtypeStruct((TAPS, s.ch, s.width), BF16),
            jax.ShapeDtypeStruct((16, LANES), F32),
            jax.ShapeDtypeStruct((8, LANES), F32),
        ),
        in_specs=[there, here, there, there, pl.BlockSpec(memory_space=pltpu.SMEM)],
        out_specs=[here] * 3,
        scratch_shapes=scratch,
        compiler_params=pltpu.CompilerParams(
            collective_id=0, has_side_effects=True, vmem_limit_bytes=53 * 2**20
        ),
        cost_estimate=pl.CostEstimate(flops=flops, bytes_accessed=2**23, transcendentals=2**20),
        name="synthesis_step",
    )(*operands)


def adam_update(weight, moment, second, gradient, factor):
    clipped = gradient * factor
    moment_new = BETA_FIRST * moment + (1.0 - BETA_FIRST) * clipped
    second_new = BETA_SECOND * second + (1.0 - BETA_SECOND) * clipped * clipped
    moment_hat = moment_new / (1.0 - BETA_FIRST**STEP)
    second_hat = second_new / (1.0 - BETA_SECOND**STEP)
    weight_new = weight - LEARN_RATE * (
        moment_hat / (jnp.sqrt(second_hat) + ADAM_EPSILON) + DECAY_RATE * weight
    )
    return (moment_new, second_new, weight_new)


def adam_kernel(
    s,
    grad,
    sums,
    norm,
    conv_w,
    conv_m,
    conv_v,
    chan_w,
    chan_m,
    chan_v,
    rgb_w,
    rgb_m,
    rgb_v,
    loss_out,
    norm_out,
    conv_m_out,
    conv_v_out,
    conv_w_out,
    conv_low_out,
    chan_m_out,
    chan_v_out,
    chan_w_out,
    rgb_m_out,
    rgb_v_out,
    rgb_w_out,
    rgb_low_out,
    new_w,
    new_m,
    new_v,
    new_low,
    put_sem,
):
    def cut(part):
        return pl.ds(part * s.part, s.part)

    def put(part):
        pairs = ((new_m, conv_m_out), (new_v, conv_v_out), (new_w, conv_w_out), (new_low, conv_low_out))
        return [
            pltpu.make_async_copy(src.at[cut(part)], dst.at[cut(part)], put_sem.at[part, j])
            for j, (src, dst) in enumerate(pairs)
        ]

    parts = TAPS // s.part
    factor = jnp.minimum(1.0, CLIP_LIMIT / (norm[0:1, 0:1] + 1e-06))
    loss_out[0] = sums[2, 0]
    norm_out[0] = norm[0, 0]
    moment, second, weight = adam_update(chan_w[...], chan_m[...], chan_v[...], sums[0:2, : s.ch], factor)
    chan_m_out[...] = moment
    chan_v_out[...] = second
    chan_w_out[...] = weight
    moment, second, weight = adam_update(rgb_w[...], rgb_m[...], rgb_v[...], sums[8:11, : s.ch], factor)
    rgb_m_out[...] = moment
    rgb_v_out[...] = second
    rgb_w_out[...] = weight
    rgb_low_out[...] = weight.astype(BF16)
    for part in range(parts):
        for k in range(part * s.part, (part + 1) * s.part):
            moment, second, weight = adam_update(conv_w[k], conv_m[k], conv_v[k], grad[k].astype(F32), factor)
            new_m[k] = moment
            new_v[k] = second
            new_w[k] = weight
            new_low[k] = weight.astype(BF16)
        for cp in put(part):
            cp.start()
    for part in range(parts):
        for cp in put(part):
            cp.wait()


def run_adam(s, *operands):
    here, there = pl.BlockSpec(memory_space=pltpu.VMEM), pl.BlockSpec(memory_space=pl.ANY)
    scalar = pl.BlockSpec(memory_space=pltpu.SMEM)
    conv = jax.ShapeDtypeStruct((TAPS, s.ch, s.width), F32)
    chan = jax.ShapeDtypeStruct((2, s.ch), F32)
    rgb = jax.ShapeDtypeStruct((3, s.ch), F32)
    one = jax.ShapeDtypeStruct((1,), F32)
    parts = TAPS // s.part
    return pl.pallas_call(
        functools.partial(adam_kernel, s),
        out_shape=(one, one)
        + (conv,) * 3
        + (jax.ShapeDtypeStruct(conv.shape, BF16),)
        + (chan,) * 3
        + (rgb,) * 3
        + (jax.ShapeDtypeStruct(rgb.shape, BF16),),
        in_specs=[here] * 12,
        out_specs=[scalar, scalar] + [there] * 4 + [here] * 7,
        scratch_shapes=[
            pltpu.VMEM(conv.shape, F32),
            pltpu.VMEM(conv.shape, F32),
            pltpu.VMEM(conv.shape, F32),
            pltpu.VMEM(conv.shape, BF16),
            pltpu.SemaphoreType.DMA((parts, 4)),
        ],
        compiler_params=pltpu.CompilerParams(vmem_limit_bytes=24 * 2**20),
        name="optimizer_step",
    )(*operands)


def local(
    mesh_shape,
    features,
    styles,
    noise_field,
    noise_keep,
    path_noise,
    length_mean,
    conv_weight,
    conv_moment,
    conv_second,
    chan_params,
    chan_moment,
    chan_second,
    rgb_weight,
    rgb_moment,
    rgb_second,
):
    s = Sizes(mesh_shape, features.shape, conv_weight.shape)
    taps_first = functools.partial(jnp.transpose, axes=(1, 0, 2))
    weight = taps_first(conv_weight)
    grad, sums, norm = run_kernel(
        s,
        features,
        jnp.concatenate([styles, chan_params, rgb_weight], axis=0),
        weight,
        jnp.concatenate(
            [path_noise.astype(F32), (noise_field.astype(F32) * noise_keep.astype(F32))[None]], axis=0
        ),
        length_mean,
    )
    outs = run_adam(
        s,
        grad,
        sums,
        norm,
        weight,
        taps_first(conv_moment),
        taps_first(conv_second),
        chan_params,
        chan_moment,
        chan_second,
        rgb_weight,
        rgb_moment,
        rgb_second,
    )
    return outs[:2] + tuple(taps_first(x) for x in outs[2:6]) + outs[6:]


def solution(mesh):
    whole, line = P(), P("mp", None, None)
    row, pixels = P(None, "mp"), P(None, "dp")
    in_specs = (
        P("mp", None, "dp"),
        row,
        pixels,
        pixels,
        P(None, None, "dp"),
        whole,
        line,
        line,
        line,
    ) + (row,) * 6
    out_specs = (whole, whole) + (line,) * 4 + (row,) * 7
    return jax.shard_map(
        functools.partial(local, dict(mesh.shape)),
        mesh=mesh,
        in_specs=in_specs,
        out_specs=out_specs,
        check_vma=False,
    )
```

```python
import functools
import math

import jax
import jax.numpy as jnp
from jax import lax
from jax.experimental import pallas as pl
from jax.experimental.pallas import tpu as pltpu
from jax.sharding import PartitionSpec as P

SIDE = 64
STEP = 5
TAPS = 9
LANES = 128

CLIP_LIMIT = 0.1
LEARN_RATE = 0.3
DECAY_RATE = 0.01
BETA_FIRST = 0.5
BETA_SECOND = 0.5
ADAM_EPSILON = 1e-08
DEMOD_EPSILON = 1e-08
HIGHEST = lax.Precision.HIGHEST
MESH = pl.DeviceIdType.MESH
F32 = jnp.float32
BF16 = jnp.bfloat16
NT = (((1,), (1,)), ((), ()))


class Sizes:
    def __init__(self, mesh_shape, features, conv_weight):
        self.dp = mesh_shape["dp"]
        self.mp = mesh_shape["mp"]
        self.chips = self.mp // 2
        self.ch, self.images, self.px = features
        self.width = conv_weight[2]
        self.half = self.width // 2
        self.group = self.images // self.chips
        self.blocks = self.px // LANES
        self.ext = self.px + 2 * LANES
        self.split = (self.ch // self.dp) % 16 == 0
        self.shares = self.dp if self.split else 1
        self.rows = self.ch // self.shares
        self.first = 7
        self.part = 3
        self.bits = []
        bit = self.chips // 2
        while bit >= 1:
            self.bits.append(bit)
            bit //= 2


def flip(value, bit):
    return value + bit - 2 * bit * lax.rem(lax.div(value, bit), 2)


def swap_halves(x):
    return pltpu.roll(x, SIDE, x.ndim - 1)


def kernel(
    s,
    feat_hbm,
    small,
    weight_hbm,
    pixels_hbm,
    mean,
    grad_out,
    small_out,
    norm_out,
    feat,
    style_cols,
    turned,
    outbox,
    grids,
    weight_own,
    weight_low,
    weights,
    weights_t,
    weight_sq,
    pack,
    pack_all,
    columns,
    rgb_low,
    rgb_rows,
    demod_rows,
    demod_cols,
    chan_cols,
    pixels,
    pixel_rows,
    aux_rows,
    aux,
    halo_out,
    halo_in,
    scaled,
    slope_of,
    proj_all,
    half_pick,
    stat_rows,
    rgb_acc,
    loss_acc,
    chan_acc,
    grad_conv,
    total,
    share_out,
    share_in,
    line_out,
    line_in,
    wide_out,
    wide_in,
    wide_sum,
    narrow_in,
    final,
    small_own,
    small_plane,
    small_mid,
    small_line,
    small_sum,
    square_near,
    square_line,
    in_sem,
    w_send,
    w_recv,
    p_sem,
    f_send,
    f_recv,
    f_local,
    h_send,
    h_recv,
    j_send,
    j_recv,
    r_send,
    r_recv,
    l_send,
    l_recv,
    b_recv,
    n_recv,
    g_sem,
    sp_sem,
    sl_sem,
    q_sem,
):
    d = lax.axis_index("dp")
    m = lax.axis_index("mp")
    z = lax.div(m, 2)
    c = lax.rem(m, 2)
    other = 1 - c
    mate = 2 * z + other
    conv_gain = 1.0 / math.sqrt(TAPS * s.width)
    rgb_gain = 1.0 / math.sqrt(s.width)
    last = s.group - 1

    def copy_to(src, dst, send, recv, dd, mm):
        return pltpu.make_async_remote_copy(
            src_ref=src, dst_ref=dst, send_sem=send, recv_sem=recv, device_id=(dd, mm), device_id_type=MESH
        )

    def taken(ref, sem):
        copy_to(ref, ref, sem, sem, d, mate).wait_recv()

    def gone(ref, sem):
        copy_to(ref, ref, sem, sem, d, mate).wait_send()

    def z_at(r):
        return lax.rem(z + r, s.chips)

    def d_at(r):
        return lax.rem(d + r, s.dp)

    line = [(d, lax.rem(m + r, s.mp)) for r in range(1, s.mp)]
    plane = [(d_at(r), mm) for r in range(1, s.dp) for mm in (m, mate)]
    near = plane + [(d, mate)]
    place = 2 * d + c

    get_weight = pltpu.make_async_copy(weight_hbm, weight_own, in_sem.at[0])
    get_feat = pltpu.make_async_copy(feat_hbm, feat, in_sem.at[1])
    get_pixels = pltpu.make_async_copy(pixels_hbm, pixels, in_sem.at[2])
    styles = small.at[: s.images]
    chan = small.at[s.images : s.images + 2]
    rgb = small.at[s.images + 2 : s.images + 5]
    get_weight.start()
    get_feat.start()
    get_pixels.start()
    halo_in[...] = jnp.zeros_like(halo_in)
    barrier = pltpu.get_barrier_semaphore()
    for dd, mm in line + plane:
        pl.semaphore_signal(barrier, inc=1, device_id=(dd, mm), device_id_type=MESH)
    get_weight.wait()
    for k in range(TAPS):
        weight_low[k] = weight_own[k].astype(BF16)
    pl.semaphore_wait(barrier, len(line) + len(plane))

    share = d if s.split else 0

    def piece(m_of):
        return weights.at[:, pl.ds(pl.multiple_of(m_of * s.ch + share * s.rows, 16), s.rows), :]

    def own_piece(half_of):
        return weight_low.at[
            :,
            pl.ds(pl.multiple_of(share * s.rows, 16), s.rows),
            pl.ds(pl.multiple_of(half_of * s.half, LANES), s.half),
        ]

    sent_rows = 0
    for index, bit in enumerate(s.bits):
        for cc in range(2):
            copy_to(
                own_piece(cc), piece(m), w_send.at[0], w_recv.at[index], d, 2 * flip(z, bit) + cc
            ).start()
            sent_rows += s.rows
    copy_to(
        weight_low.at[:, :, pl.ds(pl.multiple_of(other * s.half, LANES), s.half)],
        weights.at[:, pl.ds(pl.multiple_of(m * s.ch, 16), s.ch), :],
        w_send.at[0],
        w_recv.at[len(s.bits)],
        d,
        mate,
    ).start()
    sent_rows += s.ch
    pack[...] = jnp.zeros_like(pack)
    rgb_low[...] = rgb[...].astype(BF16)
    rgb_eff = rgb_low[...].astype(F32) * rgb_gain
    for zz in range(s.chips):
        pack[zz, : s.group, : s.ch] = styles[zz * s.group : (zz + 1) * s.group, :]
        pack[zz, s.group : s.group + 2, : s.ch] = chan[...]
        pack[zz, 8:11, : s.ch] = rgb_eff
    pack_all[m] = pack[z]
    for i in range(s.ch):
        style_cols[i] = jnp.broadcast_to(styles[:, i : i + 1], (s.images, LANES))

    for dd, mm in line:
        copy_to(pack.at[lax.div(mm, 2)], pack_all.at[m], p_sem.at[0], p_sem.at[1], dd, mm).start()

    get_feat.wait()
    lane = lax.broadcasted_iota(jnp.int32, (1, 1, LANES), 2)
    low_lanes = lane < SIDE
    step = 8

    def modulate(index, carry):
        rows = pl.ds(pl.multiple_of(index * step, step), step)
        factor = style_cols[rows]
        for q in range(s.blocks // 2):
            first = feat[rows, :, q * LANES : (q + 1) * LANES].astype(F32) * factor
            q2 = q + s.blocks // 2
            second = feat[rows, :, q2 * LANES : (q2 + 1) * LANES].astype(F32) * factor
            even = jnp.where(low_lanes, first, swap_halves(second))
            odd = jnp.where(low_lanes, swap_halves(first), second)
            out_rows = pl.ds(pl.multiple_of(index * step * s.images, step * 8), step * s.images)
            turned[2 * q, out_rows, :] = even.reshape(step * s.images, LANES)
            turned[2 * q + 1, out_rows, :] = odd.reshape(step * s.images, LANES)
        return carry

    lax.fori_loop(0, s.ch // step, modulate, 0)

    def pick(n, carry):
        for j in range(s.blocks):
            part = turned[j, pl.ds(n, s.ch, stride=s.images), :]
            outbox[n, :, j * LANES : (j + 1) * LANES] = part.astype(BF16)
        return carry

    lax.fori_loop(0, s.images, pick, 0)

    middle = pl.ds(LANES, s.px)

    def grid_rows(m_of):
        return pl.ds(pl.multiple_of(m_of * s.ch, 16), s.ch)

    def feature_send(q, r):
        zz = z_at(r)
        return copy_to(
            outbox.at[zz * s.group + q],
            grids.at[q, 1, grid_rows(m), middle],
            f_send.at[q],
            f_recv.at[q, 0],
            d,
            2 * zz + c,
        )

    def start_features():
        for q in range(s.group):
            own = outbox.at[z * s.group + q]
            there = grids.at[q, 1, grid_rows(m), middle]
            pltpu.make_async_copy(own, there, f_local.at[0]).start()
            copy_to(own, there, f_send.at[q], f_recv.at[q, 1], d, mate).start()
            if q < 2:
                for r in range(1, s.chips):
                    feature_send(q, r).start()

    held = [z]
    plane_rows = 0
    for index, bit in enumerate(s.bits):
        peer = flip(z, bit)
        for h in held[1:]:
            for cc in range(2):
                at = piece(2 * h + cc)
                copy_to(at, at, w_send.at[0], w_recv.at[index], d, 2 * peer + c).start()
                sent_rows += s.rows
        if index == len(s.bits) - 1:
            start_features()
        fresh = [flip(h, bit) for h in held]
        taken(weights.at[:, pl.ds(0, 2 * len(fresh) * s.rows), :], w_recv.at[index])
        if s.split:
            for h in fresh:
                for cc in range(2):
                    at = piece(2 * h + cc)
                    for r in range(1, s.dp):
                        copy_to(at, at, w_send.at[1], w_recv.at[len(s.bits) + 1], d_at(r), m).start()
                        plane_rows += s.rows
        held = held + fresh

    weights[:, grid_rows(m), :] = weight_low[:, :, pl.ds(pl.multiple_of(c * s.half, LANES), s.half)]
    get_pixels.wait()
    lane2 = lax.broadcasted_iota(jnp.int32, (1, LANES), 1)
    low2 = lane2 < SIDE
    for k in range(4):
        for q in range(s.blocks // 2):
            q2 = q + s.blocks // 2
            cuts = [slice(q * LANES, (q + 1) * LANES), slice(q2 * LANES, (q2 + 1) * LANES)]
            first, second = [pixels[k, :, cut] for cut in cuts]
            pixel_rows[k, :, 2 * q * LANES : (2 * q + 1) * LANES] = jnp.where(low2, first, swap_halves(second))
            pixel_rows[k, :, (2 * q + 1) * LANES : (2 * q + 2) * LANES] = jnp.where(low2, swap_halves(first), second)
    aux_rows[...] = jnp.zeros_like(aux_rows)
    for q in range(s.group):
        for k in range(4):
            row = pixel_rows[k, pl.ds(z * s.group + q, 1), :]
            aux_rows[q, k : k + 1, :] = row
            if k < 3:
                aux_rows[q, 8 + k : 9 + k, :] = row
        aux[q] = aux_rows[q].astype(BF16)

    taken(pack_all.at[pl.ds(0, s.mp - 1)], p_sem.at[1])
    for mm in range(s.mp):
        columns[mm * s.ch : (mm + 1) * s.ch, :] = pack_all[mm].T[: s.ch, :]
    rows_all = columns[...].T
    for h in range(2):
        rgb_rows[h] = rows_all[8:16, h * s.half : (h + 1) * s.half]
    mine = columns[pl.ds(pl.multiple_of(c * s.half, 8), s.half), :]
    for k in range(2):
        chan_cols[k] = jnp.broadcast_to(mine[:, s.group + k : s.group + k + 1], (s.half, LANES))
    total[...] = jnp.zeros_like(total)
    stat_rows[...] = jnp.zeros_like(stat_rows)
    rgb_acc[...] = jnp.zeros_like(rgb_acc)
    loss_acc[...] = jnp.zeros_like(loss_acc)
    chan_acc[...] = jnp.zeros_like(chan_acc)

    column = lax.rem(lane2, SIDE)
    not_first = column >= 1
    not_last = column <= SIDE - 2
    pair = s.width // 2
    up = lax.rem(d + s.dp - 1, s.dp)
    down = lax.rem(d + 1, s.dp)

    def halo_up(q):
        return copy_to(halo_out.at[q, 0], halo_in.at[q, 1], h_send.at[q, 0], h_recv.at[q, 1], up, m)

    def halo_down(q):
        return copy_to(halo_out.at[q, 1], halo_in.at[q, 0], h_send.at[q, 1], h_recv.at[q, 0], down, m)

    def ends(q):
        return grids[q, 1, :, LANES : 2 * LANES], grids[q, 1, :, s.px : s.px + LANES]

    def take_line(q):
        taken(grids.at[q, 1, pl.ds(0, (s.chips - 1) * s.ch), middle], f_recv.at[q, 0])
        for r in range(1, s.chips):
            at = grids.at[q, 1, grid_rows(2 * z_at(r) + c), middle]
            copy_to(at, at, f_send.at[q], f_recv.at[q, 1], d, mate).start()

        @pl.when(q + 2 < s.group)
        def _():
            for r in range(1, s.chips):
                feature_send(q + 2, r).start()

    def take_mate(q):
        taken(grids.at[q, 1, pl.ds(0, s.chips * s.ch), middle], f_recv.at[q, 1])
        top, end = ends(q)
        halo_out[q, 0] = jnp.where(low2, top[:pair], swap_halves(top[pair:]))
        halo_out[q, 1] = jnp.where(low2, swap_halves(end[:pair]), end[pair:])

        @pl.when(d > 0)
        def _():
            halo_up(q).start()

        @pl.when(d < s.dp - 1)
        def _():
            halo_down(q).start()

    def lateral(q, j):
        x = grids[q, 1, :, j * LANES : (j + 1) * LANES]
        none = jnp.zeros_like(x)
        grids[q, 0, :, j * LANES : (j + 1) * LANES] = jnp.where(not_first, pltpu.roll(x, 1, 1), none)
        grids[q, 2, :, j * LANES : (j + 1) * LANES] = jnp.where(not_last, pltpu.roll(x, LANES - 1, 1), none)

    def inner(q):
        for j in range(1, s.blocks + 1):
            lateral(q, j)

    def border(q):
        @pl.when(d > 0)
        def _():
            halo_down(q).wait_recv()

        @pl.when(d < s.dp - 1)
        def _():
            halo_up(q).wait_recv()

        top, end = ends(q)
        above = halo_in[q, 0]
        below = halo_in[q, 1]
        swapped_end = swap_halves(end)
        swapped_top = swap_halves(top)
        grids[q, 1, :pair, :LANES] = jnp.where(low2, above, swapped_end[:pair])
        grids[q, 1, pair:, :LANES] = jnp.where(low2, swap_halves(above), swapped_end[pair:])
        tail = s.px + LANES
        grids[q, 1, :pair, tail : tail + LANES] = jnp.where(low2, swapped_top[:pair], swap_halves(below))
        grids[q, 1, pair:, tail : tail + LANES] = jnp.where(low2, swapped_top[pair:], below)
        lateral(q, 0)
        lateral(q, s.blocks + 1)

    def blocks_of(ref, first, second):
        if second == first + 1:
            return ref[:, first * LANES : (second + 1) * LANES]
        return jnp.concatenate([ref[:, j * LANES : (j + 1) * LANES] for j in (first, second)], axis=1)

    def convolve(q, first, second):
        acc = jnp.zeros((s.half, 2 * LANES), F32)
        for a in range(3):
            for b in range(3):
                k = 3 * a + b
                acc += jnp.dot(
                    weights_t[:, k * s.width : (k + 1) * s.width],
                    blocks_of(grids.at[q, b], first + a, second + a),
                    preferred_element_type=F32,
                )
        acts = []
        for t, j in enumerate((first, second)):
            cut = slice(j * LANES, (j + 1) * LANES)
            conv = acc[:, t * LANES : (t + 1) * LANES] * conv_gain
            noise = aux[q, :, cut].astype(F32)[3:4]
            pre = conv * demod_cols[q] + chan_cols[1] * noise + chan_cols[0]
            sig = jax.nn.sigmoid(pre)
            act = pre * sig
            scaled[lax.rem(q, 2), :, cut] = conv
            slope_of[lax.rem(q, 2), :, cut] = sig * (1.0 + pre * (1.0 - sig))
            acts.append(act.astype(BF16))
        act = jnp.concatenate(acts, axis=1)
        return lax.dot_general(blocks_of(aux.at[q], first, second), act, NT, preferred_element_type=F32)[:8]

    def convolve_inner(q):
        projected = jnp.zeros((8, s.half), F32)
        for j in range(1, s.blocks - 1, 2):
            projected += convolve(q, j, j + 1)
        proj_all[q, place] = projected

    def convolve_border(q):
        proj_all[q, place] += convolve(q, 0, s.blocks - 1)
        for dd, mm in near:
            at = proj_all.at[q, place]
            copy_to(at, at, j_send.at[q], j_recv.at[q], dd, mm).start()

    def signal_back(q):
        taken(proj_all.at[q, pl.ds(0, 2 * s.dp - 1)], j_recv.at[q])
        signal_math(q)

    def signal_math(q):
        halves = []
        for h in range(2):
            acc = proj_all[q, h]
            for dd in range(1, s.dp):
                acc = acc + proj_all[q, 2 * dd + h]
            halves.append(acc)
        slopes = [jnp.sum(rgb_rows[h] * halves[h], axis=0, keepdims=True) for h in range(2)]
        row = lax.broadcasted_iota(jnp.int32, (8, s.half), 0)
        length_sq = jnp.sum(slopes[0] * slopes[0] + slopes[1] * slopes[1], axis=1, keepdims=True)
        length = jnp.sqrt(length_sq + 1e-08)
        excess = length - mean[0]
        loss_acc[...] += jnp.broadcast_to(excess * excess, (1, s.half))
        scale = 2.0 * excess / length
        for h in range(2):
            grad = scale * slopes[h]
            half_pick[h, 0] = grad * rgb_rows[h]
            half_pick[h, 1] = jnp.where(row < 3, grad * halves[h] * rgb_gain, 0.0)
        rgb_acc[...] += half_pick[c, 1]
        coef = half_pick[c, 0]
        high = coef.astype(BF16).astype(F32)
        coef_t = jnp.concatenate([high, coef - high], axis=0).T.astype(BF16)
        wide = 2 * LANES
        bias_part = chan_acc[0]
        strength_part = chan_acc[1]
        stat_part = jnp.zeros((s.half, LANES), F32)
        back = demod_cols[q] * conv_gain
        for p in range(0, s.px, wide):
            act_grad = jnp.dot(coef_t, aux[q, :, p : p + wide], preferred_element_type=F32)
            for t in range(2):
                cut = slice(p + t * LANES, p + (t + 1) * LANES)
                noise = aux[q, :, cut].astype(F32)[3:4]
                grad = act_grad[:, t * LANES : (t + 1) * LANES] * slope_of[lax.rem(q, 2), :, cut]
                bias_part = bias_part + grad
                strength_part = strength_part + grad * noise
                stat_part = stat_part + grad * scaled[lax.rem(q, 2), :, cut]
                grad_conv[lax.rem(q, 2), :, cut] = (grad * back).astype(BF16)
        chan_acc[0] = bias_part
        chan_acc[1] = strength_part
        stat = jnp.sum(stat_part.T, axis=0, keepdims=True)
        dem = demod_rows[pl.ds(q, 1), :]
        stat_rows[pl.ds(q, 1), :] = stat * (dem * dem * dem) * (-0.5 * conv_gain * conv_gain)

    def tap_grad(q, k):
        a, b = k // 3, k % 3
        return lax.dot_general(
            grids[q, b, :, a * LANES : a * LANES + s.px], grad_conv[lax.rem(q, 2)], NT, preferred_element_type=F32
        )

    pltpu.make_async_copy(
        grids.at[0, 1, pl.ds(0, s.group * s.ch), middle],
        grids.at[0, 1, pl.ds(0, s.group * s.ch), middle],
        f_local.at[0],
    ).wait()
    take_line(0)
    take_mate(0)
    inner(0)

    taken(weights.at[:, pl.ds(0, s.ch), :], w_recv.at[len(s.bits)])
    if s.split:
        taken(weights.at[:, pl.ds(0, plane_rows), :], w_recv.at[len(s.bits) + 1])
    square = jnp.zeros((s.width, s.half), F32)
    for k in range(TAPS):
        w = weights[k]
        weights_t[:, k * s.width : (k + 1) * s.width] = w.T
        wf = w.astype(F32)
        square = square + wf * wf
    weight_sq[...] = square
    demod_sq = jnp.dot(rows_all * rows_all, weight_sq[...], precision=HIGHEST, preferred_element_type=F32)
    demod = lax.rsqrt(conv_gain * conv_gain * demod_sq + DEMOD_EPSILON)
    demod_rows[...] = demod
    demod_t = demod.T
    for q in range(s.group):
        demod_cols[q] = jnp.broadcast_to(demod_t[:, q : q + 1], (s.half, LANES))

    def add_taps(q):
        def three(a, carry):
            rows = pl.ds(pl.multiple_of(a * LANES, LANES), s.px)
            for b in range(3):
                total[3 * a + b] += lax.dot_general(
                    grids[q, b, :, rows], grad_conv[lax.rem(q, 2)], NT, preferred_element_type=F32
                )
            return carry

        lax.fori_loop(0, 3, three, 0)

    def stage(q, carry):
        border(q)
        convolve_border(q)

        @pl.when(q == last - 1)
        def _():
            if last > 1:
                add_taps(q - 1)
            signal_back(q)

        take_line(q + 1)

        @pl.when(lax.rem(q, last - 1) > 0)
        def _():
            add_taps(q - 1)

        take_mate(q + 1)
        inner(q + 1)
        convolve_inner(q + 1)

        @pl.when(q < last - 1)
        def _():
            signal_back(q)

        return carry

    convolve_inner(0)
    lax.fori_loop(0, last, stage, 0)

    border(last)
    convolve_border(last)
    add_taps(last - 1)
    signal_back(last)
    cross = 2.0 * jnp.dot(
        columns[...] * columns[...], stat_rows[...], precision=HIGHEST, preferred_element_type=F32
    )
    weight_sq[...] = cross

    def share_rows(share_of):
        return pl.ds(pl.multiple_of(share_of * s.rows, 16), s.rows)

    own_rows = share_rows(share)
    own_cols = pl.ds(pl.multiple_of(c * s.half, LANES), s.half)
    targets = near if s.split else [(d, mate)]

    def last_tap(k):
        grad = total[k] + tap_grad(last, k) + weights[k].astype(F32) * weight_sq[...]
        grad = grad.astype(BF16).reshape(s.mp, s.ch, s.half)
        if k < s.first:
            share_out[k] = grad
            for r in range(1, s.dp):
                part = share_out.at[k, :, share_rows(d_at(r) if s.split else 0), :]
                copy_to(part, share_in.at[d, k], r_send.at[0], r_recv.at[k], d_at(r), m).start()
        else:
            b = k - s.first
            wide_out[b] = grad
            for r in range(1, s.chips):
                part = wide_out.at[b, pl.ds(2 * z_at(r), 2)]
                copy_to(part, wide_in.at[r, b], l_send.at[1], b_recv.at[b], d, 2 * z_at(r) + c).start()

    def by_shares(own, parts):
        acc = None
        for dd in range(s.dp):
            term = jnp.where(d == dd, own, parts[dd].astype(F32))
            acc = term if acc is None else acc + term
        return acc

    def plane_done(k):
        taken(share_in.at[pl.ds(0, s.dp - 1), k], r_recv.at[k])
        acc = by_shares(share_out[k, :, own_rows, :].astype(F32), [share_in[dd, k] for dd in range(s.dp)])
        line_out[:, k] = acc.astype(BF16).reshape(s.chips, 2, s.rows, s.half)
        for r in range(1, s.chips):
            copy_to(
                line_out.at[z_at(r), k], line_in.at[r, k], l_send.at[0], l_recv.at[k], d, 2 * z_at(r) + c
            ).start()

    def line_done(b):
        taken(wide_in.at[pl.ds(1, s.chips - 1), b], b_recv.at[b])
        acc = wide_out[b, pl.ds(2 * z, 2)].astype(F32)
        for r in range(1, s.chips):
            acc = acc + wide_in[r, b].astype(F32)
        wide_sum[b] = acc.astype(BF16)
        for r in range(1, s.dp):
            part = wide_sum.at[b, :, share_rows(d_at(r) if s.split else 0), :]
            copy_to(part, narrow_in.at[d, b], r_send.at[1], n_recv.at[b], d_at(r), m).start()

    def byte_count():
        return weights.at[:, pl.ds(0, len(targets) * s.rows), :]

    def finish(k, squares):
        if k < s.first:
            taken(line_in.at[pl.ds(1, s.chips - 1), k], l_recv.at[k])
            acc = line_out[z, k].astype(F32)
            for r in range(1, s.chips):
                acc = acc + line_in[r, k].astype(F32)
        else:
            b = k - s.first
            taken(narrow_in.at[pl.ds(0, s.dp - 1), b], n_recv.at[b])
            acc = by_shares(wide_sum[b, :, own_rows, :].astype(F32), [narrow_in[dd, b] for dd in range(s.dp)])
        final[:, k] = acc.astype(BF16)
        kept = final[:, k].astype(F32)
        return squares + jnp.sum(kept * kept, axis=0)

    def hand_out(first_tap, count):
        taps = pl.ds(first_tap, count)
        there = grad_out.at[taps, own_rows, own_cols]
        for dd, mm in targets:
            copy_to(final.at[lax.rem(mm, 2), taps], there, g_sem.at[0], g_sem.at[1], dd, mm).start()
        pltpu.make_async_copy(final.at[c, taps], there, g_sem.at[2]).start()

    def send_small():
        small_own[0:1] = jnp.sum(chan_acc[0].T, axis=0, keepdims=True)
        small_own[1:2] = jnp.sum(chan_acc[1].T, axis=0, keepdims=True)
        small_own[2:3] = loss_acc[...]
        small_own[3:8] = jnp.zeros((5, s.half), F32)
        small_own[8:16] = rgb_acc[...]
        small_plane[place] = small_own[...]
        for dd, mm in near:
            copy_to(small_own, small_plane.at[place], sp_sem.at[0], sp_sem.at[1], dd, mm).start()

    for index, k in enumerate((0, 7, 1, 2, 3, 8, 4, 5, 6)):
        last_tap(k)
        if index == 1:
            send_small()

    taken(small_plane.at[pl.ds(0, 2 * s.dp - 1)], sp_sem.at[1])
    for h in range(2):
        acc = small_plane[h, 0:8]
        for dd in range(1, s.dp):
            acc = acc + small_plane[2 * dd + h, 0:8]
        row = lax.broadcasted_iota(jnp.int32, (8, s.half), 0)
        small_mid[h, 0:8] = jnp.where(row < 2, acc, small_plane[h, 0:8])
        small_mid[h, 8:16] = small_plane[h, 8:16]
    small_line[z] = small_mid[...]
    for r in range(1, s.chips):
        copy_to(small_mid, small_line.at[z], sl_sem.at[0], sl_sem.at[1], d, 2 * z_at(r) + c).start()

    squares = jnp.zeros((s.rows, s.half), F32)
    plane_done(0)
    plane_done(1)
    line_done(0)
    plane_done(2)
    plane_done(3)
    line_done(1)
    plane_done(4)
    for k in (0, 1, 2):
        squares = finish(k, squares)
    hand_out(0, 3)
    plane_done(5)
    plane_done(6)
    for k in (7, 8, 3, 4, 5, 6):
        squares = finish(k, squares)
    square_near[place] = jnp.broadcast_to(jnp.sum(squares, keepdims=True), (8, LANES))
    for dd, mm in near:
        at = square_near.at[place]
        copy_to(at, at, q_sem.at[0], q_sem.at[1], dd, mm).start()
    hand_out(3, TAPS - 3)
    taken(small_line.at[pl.ds(0, s.chips - 1)], sl_sem.at[1])
    sums = small_line[0]
    for zz in range(1, s.chips):
        sums = sums + small_line[zz]
    small_sum[...] = sums
    chan_squares = jnp.sum(sums[:, 0:2] * sums[:, 0:2]) + jnp.sum(sums[:, 8:16] * sums[:, 8:16])
    start = m * s.ch
    first = lax.rem(start, s.half)
    block = pl.multiple_of(lax.div(first, LANES) * LANES, LANES)
    mine = small_sum[lax.div(start, s.half), :, pl.ds(block, LANES)]
    small_out[...] = pltpu.roll(mine, lax.rem(2 * LANES - lax.rem(first, LANES), LANES), 1)

    taken(square_near.at[pl.ds(0, 2 * s.dp - 1)], q_sem.at[1])
    acc = square_near[0]
    for at in range(1, 2 * s.shares):
        acc = acc + square_near[at]
    square_line[z] = acc
    for r in range(1, s.chips):
        at = square_line.at[z]
        copy_to(at, at, q_sem.at[2], q_sem.at[3], d, 2 * z_at(r) + c).start()
    taken(square_line.at[pl.ds(0, s.chips - 1)], q_sem.at[3])
    acc = square_line[0]
    for zz in range(1, s.chips):
        acc = acc + square_line[zz]
    norm_out[...] = jnp.sqrt(acc + chan_squares)
    taken(byte_count(), g_sem.at[1])
    pltpu.make_async_copy(final.at[c], grad_out.at[:, own_rows, own_cols], g_sem.at[2]).wait()

    gone(weights.at[:, pl.ds(0, sent_rows), :], w_send.at[0])
    if s.split:
        gone(weights.at[:, pl.ds(0, plane_rows), :], w_send.at[1])
    gone(pack_all.at[pl.ds(0, s.mp - 1)], p_sem.at[0])
    for q in range(s.group):
        gone(grids.at[q, 1, pl.ds(0, (2 * s.chips - 1) * s.ch), middle], f_send.at[q])
        gone(proj_all.at[q, pl.ds(0, 2 * s.dp - 1)], j_send.at[q])
    gone(small_plane.at[pl.ds(0, 2 * s.dp - 1)], sp_sem.at[0])
    gone(share_in.at[pl.ds(0, s.dp - 1)], r_send.at[0])
    gone(small_line.at[pl.ds(0, s.chips - 1)], sl_sem.at[0])
    gone(line_in.at[pl.ds(1, s.chips - 1)], l_send.at[0])
    gone(wide_in.at[pl.ds(1, s.chips - 1)], l_send.at[1])
    gone(narrow_in.at[pl.ds(0, s.dp - 1)], r_send.at[1])
    gone(byte_count(), g_sem.at[0])
    gone(square_near.at[pl.ds(0, 2 * s.dp - 1)], q_sem.at[0])
    gone(square_line.at[pl.ds(0, s.chips - 1)], q_sem.at[2])

    @pl.when(d > 0)
    def _():
        for q in range(s.group):
            halo_up(q).wait_send()

    @pl.when(d < s.dp - 1)
    def _():
        for q in range(s.group):
            halo_down(q).wait_send()


def run_kernel(s, *operands):
    vm, dma = pltpu.VMEM, pltpu.SemaphoreType.DMA
    rest = TAPS - s.first
    scratch = [
        vm((s.ch, s.images, s.px), BF16),
        vm((s.ch, s.images, LANES), F32),
        vm((s.blocks, s.ch * s.images, LANES), F32),
        vm((s.images, s.ch, s.px), BF16),
        vm((s.group, 3, s.width, s.ext), BF16),
        vm((TAPS, s.ch, s.width), F32),
        vm((TAPS, s.ch, s.width), BF16),
        vm((TAPS, s.width, s.half), BF16),
        vm((s.half, TAPS * s.width), BF16),
        vm((s.width, s.half), F32),
        vm((s.chips, 16, LANES), F32),
        vm((s.mp, 16, LANES), F32),
        vm((s.width, 16), F32),
        vm((3, s.ch), BF16),
        vm((2, 8, s.half), F32),
        vm((16, s.half), F32),
        vm((s.group, s.half, LANES), F32),
        vm((2, s.half, LANES), F32),
        vm((4, s.images, s.px), F32),
        vm((4, s.images, s.px), F32),
        vm((s.group, 16, s.px), F32),
        vm((s.group, 16, s.px), BF16),
        vm((s.group, 2, s.width // 2, LANES), BF16),
        vm((s.group, 2, s.width // 2, LANES), BF16),
        vm((2, s.half, s.px), F32),
        vm((2, s.half, s.px), F32),
        vm((s.group, 2 * s.dp, 8, s.half), F32),
        vm((2, 2, 8, s.half), F32),
        vm((16, s.half), F32),
        vm((8, s.half), F32),
        vm((1, s.half), F32),
        vm((2, s.half, LANES), F32),
        vm((2, s.half, s.px), BF16),
        vm((TAPS, s.width, s.half), F32),
        vm((s.first, s.mp, s.ch, s.half), BF16),
        vm((s.dp, s.first, s.mp, s.rows, s.half), BF16),
        vm((s.chips, s.first, 2, s.rows, s.half), BF16),
        vm((s.chips, s.first, 2, s.rows, s.half), BF16),
        vm((rest, s.mp, s.ch, s.half), BF16),
        vm((s.chips, rest, 2, s.ch, s.half), BF16),
        vm((rest, 2, s.ch, s.half), BF16),
        vm((s.dp, rest, 2, s.rows, s.half), BF16),
        vm((2, TAPS, s.rows, s.half), BF16),
        vm((16, s.half), F32),
        vm((2 * s.dp, 16, s.half), F32),
        vm((2, 16, s.half), F32),
        vm((s.chips, 2, 16, s.half), F32),
        vm((2, 16, s.half), F32),
        vm((2 * s.dp, 8, LANES), F32),
        vm((s.chips, 8, LANES), F32),
        dma((3,)),
        dma((2,)),
        dma((len(s.bits) + 2,)),
        dma((2,)),
        dma((s.group,)),
        dma((s.group, 2)),
        dma((1,)),
        dma((s.group, 2)),
        dma((s.group, 2)),
        dma((s.group,)),
        dma((s.group,)),
        dma((2,)),
        dma((s.first,)),
        dma((2,)),
        dma((s.first,)),
        dma((rest,)),
        dma((rest,)),
        dma((3,)),
        dma((2,)),
        dma((2,)),
        dma((4,)),
    ]
    flops = 2 * 2 * s.group * s.px * s.half * s.width * TAPS
    here, there = pl.BlockSpec(memory_space=pltpu.VMEM), pl.BlockSpec(memory_space=pl.ANY)
    return pl.pallas_call(
        functools.partial(kernel, s),
        out_shape=(
            jax.ShapeDtypeStruct((TAPS, s.ch, s.width), BF16),
            jax.ShapeDtypeStruct((16, LANES), F32),
            jax.ShapeDtypeStruct((8, LANES), F32),
        ),
        in_specs=[there, here, there, there, pl.BlockSpec(memory_space=pltpu.SMEM)],
        out_specs=[here] * 3,
        scratch_shapes=scratch,
        compiler_params=pltpu.CompilerParams(
            collective_id=0, has_side_effects=True, vmem_limit_bytes=53 * 2**20
        ),
        cost_estimate=pl.CostEstimate(flops=flops, bytes_accessed=2**23, transcendentals=2**20),
        name="synthesis_step",
    )(*operands)


def adam_update(weight, moment, second, gradient, factor):
    clipped = gradient * factor
    moment_new = BETA_FIRST * moment + (1.0 - BETA_FIRST) * clipped
    second_new = BETA_SECOND * second + (1.0 - BETA_SECOND) * clipped * clipped
    moment_hat = moment_new / (1.0 - BETA_FIRST**STEP)
    second_hat = second_new / (1.0 - BETA_SECOND**STEP)
    weight_new = weight - LEARN_RATE * (
        moment_hat / (jnp.sqrt(second_hat) + ADAM_EPSILON) + DECAY_RATE * weight
    )
    return (moment_new, second_new, weight_new)


def adam_kernel(
    s,
    grad,
    sums,
    norm,
    conv_w,
    conv_m,
    conv_v,
    chan_w,
    chan_m,
    chan_v,
    rgb_w,
    rgb_m,
    rgb_v,
    loss_out,
    norm_out,
    conv_m_out,
    conv_v_out,
    conv_w_out,
    conv_low_out,
    chan_m_out,
    chan_v_out,
    chan_w_out,
    rgb_m_out,
    rgb_v_out,
    rgb_w_out,
    rgb_low_out,
    new_w,
    new_m,
    new_v,
    new_low,
    put_sem,
):
    def cut(part):
        return pl.ds(part * s.part, s.part)

    def put(part):
        pairs = ((new_m, conv_m_out), (new_v, conv_v_out), (new_w, conv_w_out), (new_low, conv_low_out))
        return [
            pltpu.make_async_copy(src.at[cut(part)], dst.at[cut(part)], put_sem.at[part, j])
            for j, (src, dst) in enumerate(pairs)
        ]

    parts = TAPS // s.part
    factor = jnp.minimum(1.0, CLIP_LIMIT / (norm[0:1, 0:1] + 1e-06))
    loss_out[0] = sums[2, 0]
    norm_out[0] = norm[0, 0]
    moment, second, weight = adam_update(chan_w[...], chan_m[...], chan_v[...], sums[0:2, : s.ch], factor)
    chan_m_out[...] = moment
    chan_v_out[...] = second
    chan_w_out[...] = weight
    moment, second, weight = adam_update(rgb_w[...], rgb_m[...], rgb_v[...], sums[8:11, : s.ch], factor)
    rgb_m_out[...] = moment
    rgb_v_out[...] = second
    rgb_w_out[...] = weight
    rgb_low_out[...] = weight.astype(BF16)
    for part in range(parts):
        for k in range(part * s.part, (part + 1) * s.part):
            moment, second, weight = adam_update(conv_w[k], conv_m[k], conv_v[k], grad[k].astype(F32), factor)
            new_m[k] = moment
            new_v[k] = second
            new_w[k] = weight
            new_low[k] = weight.astype(BF16)
        for cp in put(part):
            cp.start()
    for part in range(parts):
        for cp in put(part):
            cp.wait()


def run_adam(s, *operands):
    here, there = pl.BlockSpec(memory_space=pltpu.VMEM), pl.BlockSpec(memory_space=pl.ANY)
    scalar = pl.BlockSpec(memory_space=pltpu.SMEM)
    conv = jax.ShapeDtypeStruct((TAPS, s.ch, s.width), F32)
    chan = jax.ShapeDtypeStruct((2, s.ch), F32)
    rgb = jax.ShapeDtypeStruct((3, s.ch), F32)
    one = jax.ShapeDtypeStruct((1,), F32)
    parts = TAPS // s.part
    return pl.pallas_call(
        functools.partial(adam_kernel, s),
        out_shape=(one, one)
        + (conv,) * 3
        + (jax.ShapeDtypeStruct(conv.shape, BF16),)
        + (chan,) * 3
        + (rgb,) * 3
        + (jax.ShapeDtypeStruct(rgb.shape, BF16),),
        in_specs=[here] * 12,
        out_specs=[scalar, scalar] + [there] * 4 + [here] * 7,
        scratch_shapes=[
            pltpu.VMEM(conv.shape, F32),
            pltpu.VMEM(conv.shape, F32),
            pltpu.VMEM(conv.shape, F32),
            pltpu.VMEM(conv.shape, BF16),
            pltpu.SemaphoreType.DMA((parts, 4)),
        ],
        compiler_params=pltpu.CompilerParams(vmem_limit_bytes=24 * 2**20),
        name="optimizer_step",
    )(*operands)


def local(
    mesh_shape,
    features,
    styles,
    noise_field,
    noise_keep,
    path_noise,
    length_mean,
    conv_weight,
    conv_moment,
    conv_second,
    chan_params,
    chan_moment,
    chan_second,
    rgb_weight,
    rgb_moment,
    rgb_second,
):
    s = Sizes(mesh_shape, features.shape, conv_weight.shape)
    taps_first = functools.partial(jnp.transpose, axes=(1, 0, 2))
    weight = taps_first(conv_weight)
    grad, sums, norm = run_kernel(
        s,
        features,
        jnp.concatenate([styles, chan_params, rgb_weight], axis=0),
        weight,
        jnp.concatenate(
            [path_noise.astype(F32), (noise_field.astype(F32) * noise_keep.astype(F32))[None]], axis=0
        ),
        length_mean,
    )
    outs = run_adam(
        s,
        grad,
        sums,
        norm,
        weight,
        taps_first(conv_moment),
        taps_first(conv_second),
        chan_params,
        chan_moment,
        chan_second,
        rgb_weight,
        rgb_moment,
        rgb_second,
    )
    return outs[:2] + tuple(taps_first(x) for x in outs[2:6]) + outs[6:]


def solution(mesh):
    whole, line = P(), P("mp", None, None)
    row, pixels = P(None, "mp"), P(None, "dp")
    in_specs = (
        P("mp", None, "dp"),
        row,
        pixels,
        pixels,
        P(None, None, "dp"),
        whole,
        line,
        line,
        line,
    ) + (row,) * 6
    out_specs = (whole, whole) + (line,) * 4 + (row,) * 7
    return jax.shard_map(
        functools.partial(local, dict(mesh.shape)),
        mesh=mesh,
        in_specs=in_specs,
        out_specs=out_specs,
        check_vma=False,
    )
```
